32 devices in a mesh: groups: 2 (over y), seq: 4 (over z), head: 2 (over x), sub: 2 (over core).
Axes of the slice: x: 2, y: 2, z: 4, core: 2. Of those that a mesh axis runs over, the one named last changes fastest.
Arguments:
- queries: bfloat16 [128, 128, 16, 128], P(('groups', 'seq'), None, ('head', 'sub')), parts along dimension 0, may hold values from -6 to 6
- keys: bfloat16 [128, 128, 16, 128], P(('groups', 'seq'), None, ('head', 'sub')), parts along dimension 0, may hold values from -6 to 6
- values: bfloat16 [128, 128, 16, 2, 128], P(('groups', 'seq'), None, ('head', 'sub')), parts along dimension 0, may hold values from -6 to 6
- log_decay: bfloat16 [128, 128, 16, 2], P(('groups', 'seq'), None, ('head', 'sub')), parts along dimension 0, may hold values from -0.8 to 0
- write_rate: bfloat16 [128, 128, 16, 2], P(('groups', 'seq'), None, ('head', 'sub')), parts along dimension 0, may hold values from 0.049804688 to 0.94921875
- norm_gain: bfloat16 [128], replicated, may hold values from 0.25 to 1.75
- parent_cache: float32 [32, 16, 2, 128, 128], P(('groups', 'seq'), ('head', 'sub')), parts along dimension 0, may hold values from -3 to 3
- order: int32 [128], P('groups'), parts along dimension 0, may hold values from 0 to 63, as said below
- parent_owner: int32 [128], P('groups'), parts along dimension 0, may hold values from 0 to 3, as said below
- parent_slot: int32 [128], P('groups'), parts along dimension 0, may hold values from 0 to 3
- token_count: int32 [128], P('groups'), parts along dimension 0, may hold values from 64 to 128, as said below
Outputs:
- mixed: bfloat16 [128, 128, 16, 2, 128], P(('groups', 'seq'), None, ('head', 'sub')), parts along dimension 0
- final_state: float32 [128, 16, 2, 128, 128], P(('groups', 'seq'), ('head', 'sub')), parts along dimension 0
The draws below stay inside these ranges and needn't reach their ends.
There are 2 independent parts, one for each index of `groups`. The reference program is written for one: setup_inputs(seed, part) draws one part's arguments, and reference() takes and returns one part's arrays. A program takes and returns all parts, laid end to end along the dimension named above; an argument that names none is the same for every part. Nothing has to cross between parts.
Inputs may be any that keep to these rules, and one draw needn't show every extreme that they name: A permutation; slot j = p * 16 + s * 4 + r with r < 4 is processed by seq device p and holds an expansion that arrives on seq device s, so order[j] // 16 = s. `parent_owner`: among the 16 expansions processed by one seq device at most 8 have their parent on one owner, and on some device exactly 8 do. `token_count`: multiples of 64; some expansion has 128 and some has 64.
All inputs are finite; a program needn't handle non-finite values.
Results may differ from the reference program's by a relative error of at most 0.001.
Values may be sent and summed in bfloat16 or wider, within the bound.
No kernel may reach another device: no remote copies, remote signals or barrier semaphores. Data moves between devices by JAX's collectives and lax.ppermute only.
A program may use at most 192 MiB of HBM per device.

```python
import jax
import jax.numpy as jnp
from jax import lax

KEY_HEAD_COUNT = 16
DK = 128
DV = 128
TOKEN_SLOTS = 128
SPAN = 64
EXP_DEV = 16
PAR_DEV = 4
GROUP_EXPANSIONS = 64
PARENTS = 16
CAP = 8
N_SEQ = 4


def owner_plan(key):
    key_perm, key_base, key_pair, key_force, key_shuffle = jax.random.split(jax.random.fold_in(key, 11), 5)
    per_peer = EXP_DEV // N_SEQ
    arrivals = jax.vmap(lambda single: jax.random.permutation(single, EXP_DEV))(jax.random.split(key_perm, N_SEQ))
    slot_grid = arrivals.reshape(N_SEQ, N_SEQ, per_peer) + (jnp.arange(N_SEQ, dtype=jnp.int32) * EXP_DEV)[:, None, None]
    order_ids = jnp.transpose(slot_grid, (1, 0, 2)).reshape(-1).astype(jnp.int32)
    base_owner = jax.random.randint(key_base, (N_SEQ,), 0, N_SEQ)
    paired = jax.random.randint(key_pair, (N_SEQ,), 0, 2)
    forced = jax.random.randint(key_force, (), 0, N_SEQ)
    paired = jnp.where(jnp.arange(N_SEQ) == forced, 1, paired)
    shuffled = jax.vmap(lambda single: jax.random.permutation(single, EXP_DEV))(jax.random.split(key_shuffle, N_SEQ))
    offsets = jnp.where(paired[:, None] == 1, shuffled // CAP, shuffled)
    owner_by_slot = ((base_owner[:, None] + offsets) % N_SEQ).reshape(-1).astype(jnp.int32)
    owners = jnp.zeros((GROUP_EXPANSIONS,), jnp.int32).at[order_ids].set(owner_by_slot)
    return (order_ids, owners)


def draw_order(key, part):
    return owner_plan(key)[0]


def draw_parent_owner(key, part):
    return owner_plan(key)[1]


def draw_token_count(key, part):
    key_blocks, key_top, key_low = jax.random.split(jax.random.fold_in(key, 23), 3)
    top_blocks = TOKEN_SLOTS // SPAN
    blocks = jax.random.randint(key_blocks, (GROUP_EXPANSIONS,), 1, top_blocks + 1)
    longest = jax.random.randint(key_top, (), 0, GROUP_EXPANSIONS)
    shortest = (longest + 1 + jax.random.randint(key_low, (), 0, GROUP_EXPANSIONS - 1)) % GROUP_EXPANSIONS
    positions = jnp.arange(GROUP_EXPANSIONS)
    blocks = jnp.where(positions == longest, top_blocks, blocks)
    blocks = jnp.where(positions == shortest, 1, blocks)
    return (blocks * SPAN).astype(jnp.int32)


def draw_log_decay(key, part):
    every_key_row = jax.random.split(jax.random.fold_in(key, 37), 7)
    fast_share = 0.5
    fast_heads = jax.random.uniform(every_key_row[0], (KEY_HEAD_COUNT, 2)) < fast_share
    fast_rate = jnp.exp(jax.random.uniform(every_key_row[1], (KEY_HEAD_COUNT, 2), jnp.float32, jnp.log(1.0 / 50.0), jnp.log(1.0 / 30.0)))
    slow_rate = jnp.exp(jax.random.uniform(every_key_row[2], (KEY_HEAD_COUNT, 2), jnp.float32, jnp.log(3e-05), jnp.log(0.0006)))
    per_head_rate = jnp.where(fast_heads, fast_rate, slow_rate)
    growth_multiplier = jnp.exp(jax.random.uniform(every_key_row[3], (GROUP_EXPANSIONS, 1, 1, 1), jnp.float32, jnp.log(0.5), jnp.log(2.0)))
    jaggedness = jax.random.uniform(every_key_row[4], (GROUP_EXPANSIONS, TOKEN_SLOTS, KEY_HEAD_COUNT, 2), jnp.float32, 0.5, 1.5)
    flurries = jax.random.uniform(every_key_row[5], (GROUP_EXPANSIONS, TOKEN_SLOTS, KEY_HEAD_COUNT, 2)) < 2.0 / TOKEN_SLOTS
    flurry_depth = jnp.log(jax.random.uniform(every_key_row[6], (GROUP_EXPANSIONS, TOKEN_SLOTS, KEY_HEAD_COUNT, 2), jnp.float32, 0.5, 0.8))
    return (-(per_head_rate * growth_multiplier * jaggedness) + jnp.where(flurries, flurry_depth, 0.0)).astype(jnp.bfloat16)


def touch_ends(drawn, key, smallest, high):
    shape = drawn.shape
    spot = [jax.random.randint(jax.random.fold_in(key, axis), (), 0, shape[axis]) for axis in range(len(shape))]
    drawn = drawn.at[tuple(spot)].set(smallest)
    longest = shape.index(max(shape))
    spot[longest] = (spot[longest] + 1) % shape[longest]
    return drawn.at[tuple(spot)].set(high)


def levels(rng, extent, cuts, smallest, high):
    gain, own = 1.0, jax.random.fold_in(rng, 6)
    for axis_at, parts in cuts:
        heights = jnp.exp(jax.random.uniform(jax.random.fold_in(own, axis_at), (parts,), jnp.float32, smallest / len(cuts), high / len(cuts)))
        gain = gain * jnp.repeat(heights, extent[axis_at] // parts).reshape([-1 if axis == axis_at else 1 for axis in range(len(extent))])
    return gain


def scatter_about(own_key, shape, width, bound, cuts=(), kind=jnp.bfloat16):
    values = width * jax.random.normal(own_key, shape, jnp.float32)
    if cuts:
        values = values * levels(own_key, shape, cuts, -0.22, 0.18)
    return jnp.clip(values, -bound, bound).astype(kind)


def setup_inputs(seed: int = 0, part: int = 0) -> dict:
    arg_keys = jax.random.split(jax.random.key(seed), 12)
    part_keys = jax.random.split(jax.random.fold_in(arg_keys[11], part), 12)
    queries = scatter_about(part_keys[0], (GROUP_EXPANSIONS, TOKEN_SLOTS, KEY_HEAD_COUNT, DK), 1.0, 6.0, ((0, 4), (2, 4)))
    keys = scatter_about(part_keys[1], (GROUP_EXPANSIONS, TOKEN_SLOTS, KEY_HEAD_COUNT, DK), 1.0, 6.0, ((0, 4), (2, 4)))
    values = scatter_about(part_keys[2], (GROUP_EXPANSIONS, TOKEN_SLOTS, KEY_HEAD_COUNT, 2, DV), 1.0, 6.0, ((0, 4), (2, 4)))
    log_decay = draw_log_decay(jax.random.fold_in(jax.random.fold_in(arg_keys[11], part), 71), part)
    write_rate = jnp.clip(0.049804688 + 0.89941406 * jax.random.uniform(part_keys[4], (GROUP_EXPANSIONS, TOKEN_SLOTS, KEY_HEAD_COUNT, 2), jnp.float32) ** levels(part_keys[4], (GROUP_EXPANSIONS, TOKEN_SLOTS, KEY_HEAD_COUNT, 2), ((0, 4), (2, 4)), -0.2, 0.2), 0.049804688, 0.94921875).astype(jnp.bfloat16)
    norm_gain = jnp.clip(1.0 + 0.15 * jax.random.normal(arg_keys[5], (DV,), jnp.float32), 0.25, 1.75).astype(jnp.bfloat16)
    parent_cache = scatter_about(part_keys[6], (PARENTS, KEY_HEAD_COUNT, 2, DK, DV), 0.5, 3.0, ((0, 4), (1, 4)), jnp.float32)
    order = draw_order(jax.random.fold_in(jax.random.fold_in(arg_keys[11], part), 71), part)
    parent_owner = draw_parent_owner(jax.random.fold_in(jax.random.fold_in(arg_keys[11], part), 71), part)
    parent_slot = touch_ends(jax.random.randint(part_keys[9], (GROUP_EXPANSIONS,), 0, PAR_DEV), jax.random.fold_in(part_keys[9], 1), 0, PAR_DEV - 1).astype(jnp.int32)
    token_count = draw_token_count(jax.random.fold_in(jax.random.fold_in(arg_keys[11], part), 71), part)
    return {"queries": queries, "keys": keys, "values": values, "log_decay": log_decay, "write_rate": write_rate, "norm_gain": norm_gain, "parent_cache": parent_cache, "order": order, "parent_owner": parent_owner, "parent_slot": parent_slot, "token_count": token_count}


exact_mode = lax.Precision.HIGHEST
norm_epsilon = 1e-06

def inverse_unit(lower_part):
    block_len = lower_part.shape[-1]
    identity = jnp.eye(block_len, dtype=jnp.float32)
    result = identity - lower_part
    powered = lower_part
    for repeat_no in range(block_len.bit_length() - 2):
        powered = jnp.einsum('...ij,...jk->...ik', powered, powered, precision=exact_mode)
        result = result + jnp.einsum('...ij,...jk->...ik', result, powered, precision=exact_mode)
    return result

def arrange(queries, keys, values, log_decay, write_rate, token_count, block_len):
    expansions, length, key_heads, key_dim = queries.shape
    value_dim = values.shape[-1]
    block_count = length // block_len
    head_rows = expansions * key_heads * 2
    positions = lax.broadcasted_iota(jnp.int32, (expansions, length), 1)
    live_mask = positions < token_count[:, None]
    keys_unit = keys.astype(jnp.float32)
    keys_unit = keys_unit / jnp.sqrt(lax.optimization_barrier(jnp.sum(keys_unit * keys_unit, axis=-1, keepdims=True)) + norm_epsilon)

    def spread_heads(tensor):
        turned = jnp.transpose(tensor, (0, 2, 1, 3))[:, :, None]
        widened = jnp.broadcast_to(turned, (expansions, key_heads, 2, length, key_dim))
        return widened.reshape(head_rows, block_count, block_len, key_dim)
    query_rows = spread_heads(queries.astype(jnp.float32))
    key_rows = spread_heads(keys_unit)
    value_rows = jnp.transpose(values.astype(jnp.float32), (0, 2, 3, 1, 4)).reshape(head_rows, block_count, block_len, value_dim)
    live_wide = live_mask[:, :, None, None]
    decay_rows = jnp.transpose(jnp.where(live_wide, log_decay.astype(jnp.float32), 0.0), (0, 2, 3, 1)).reshape(head_rows, block_count, block_len)
    rate_rows = jnp.transpose(jnp.where(live_wide, write_rate.astype(jnp.float32), 0.0), (0, 2, 3, 1)).reshape(head_rows, block_count, block_len)
    live_rows = jnp.broadcast_to(live_mask[:, None, None, :], (expansions, key_heads, 2, length)).reshape(head_rows, length)
    return (query_rows, key_rows, value_rows, decay_rows, rate_rows, live_rows)

def within_spans(query_rows, key_rows, value_rows, decay_rows, rate_rows):
    block_len = decay_rows.shape[-1]
    cumulative = jnp.cumsum(decay_rows, axis=-1)
    spread_log = cumulative[..., :, None] - cumulative[..., None, :]
    row_ids = lax.broadcasted_iota(jnp.int32, (block_len, block_len), 0)
    col_ids = lax.broadcasted_iota(jnp.int32, (block_len, block_len), 1)
    inclusive = row_ids >= col_ids
    strict = row_ids > col_ids
    decay_pair = jnp.where(inclusive, jnp.exp(jnp.where(inclusive, spread_log, 0.0)), 0.0)
    key_key = jnp.einsum('bncd,bnjd->bncj', key_rows, key_rows, precision=exact_mode)
    lower_part = jnp.where(strict, rate_rows[..., :, None] * key_key * decay_pair, 0.0)
    inverse = inverse_unit(lower_part)
    scaled_keys = key_rows * (rate_rows * jnp.exp(cumulative))[..., None]
    scaled_values = value_rows * rate_rows[..., None]
    weights_w = jnp.einsum('bncj,bnjd->bncd', inverse, scaled_keys, precision=exact_mode)
    updates_u = jnp.einsum('bncj,bnjd->bncd', inverse, scaled_values, precision=exact_mode)
    query_key = jnp.einsum('bncd,bnjd->bncj', query_rows, key_rows, precision=exact_mode)
    local_mix = query_key * decay_pair
    decayed_queries = query_rows * jnp.exp(cumulative)[..., None]
    decayed_keys = key_rows * jnp.exp(cumulative[..., -1:] - cumulative)[..., None]
    span_decay = jnp.exp(cumulative[..., -1])
    return (weights_w, updates_u, decayed_queries, decayed_keys, local_mix, span_decay)

def span_step(carried, pieces):
    weights_w, updates_u, decayed_queries, decayed_keys, local_mix, span_decay = pieces
    corrected = updates_u - jnp.einsum('bcd,bde->bce', weights_w, carried, precision=exact_mode)
    output = jnp.einsum('bcd,bde->bce', decayed_queries, carried, precision=exact_mode)
    output = output + jnp.einsum('bcj,bje->bce', local_mix, corrected, precision=exact_mode)
    carried = span_decay[:, None, None] * carried + jnp.einsum('bcd,bce->bde', decayed_keys, corrected, precision=exact_mode)
    return (carried, output)

def finish(outputs, norm_gain, live_rows):
    mean_square = lax.optimization_barrier(jnp.mean(outputs * outputs, axis=-1, keepdims=True))
    normed = outputs * lax.rsqrt(mean_square + norm_epsilon) * norm_gain.astype(jnp.float32)
    return jnp.where(live_rows[..., None], normed, 0.0).astype(jnp.bfloat16)

def restore(mixed_rows, expansions, key_heads):
    head_rows, length, value_dim = mixed_rows.shape
    return jnp.transpose(mixed_rows.reshape(expansions, key_heads, 2, length, value_dim), (0, 3, 1, 2, 4))

def reference(queries, keys, values, log_decay, write_rate, norm_gain, parent_cache, order, parent_owner, parent_slot, token_count):
    key_heads = queries.shape[2]
    parents = (parent_owner * PAR_DEV + parent_slot).astype(jnp.int32)

    def one_expansion(number):

        def pick_rows(tensor):
            return lax.dynamic_slice_in_dim(tensor, number, 1, 0)
        arranged = arrange(pick_rows(queries), pick_rows(keys), pick_rows(values), pick_rows(log_decay), pick_rows(write_rate), pick_rows(token_count), SPAN)
        query_rows, key_rows, value_rows, decay_rows, rate_rows, live_rows = arranged
        pieces = within_spans(query_rows, key_rows, value_rows, decay_rows, rate_rows)
        stacked = tuple((jnp.moveaxis(tensor, 1, 0) for tensor in pieces))
        initial = lax.dynamic_index_in_dim(parent_cache, parents[number], 0, keepdims=False)
        initial = initial.reshape(key_heads * 2, initial.shape[-2], initial.shape[-1])
        final_states, outputs = lax.scan(span_step, initial, stacked)
        outputs = jnp.moveaxis(outputs, 0, 1)
        outputs = outputs.reshape(key_heads * 2, -1, outputs.shape[-1])
        mixed_one = restore(finish(outputs, norm_gain, live_rows), 1, key_heads)
        return (mixed_one[0], final_states.reshape(key_heads, 2, final_states.shape[-2], final_states.shape[-1]))
    numbers = jnp.arange(queries.shape[0], dtype=jnp.int32)
    mixed_all, finals = lax.map(one_expansion, numbers)
    return (mixed_all, jnp.take(finals, order, axis=0))
```

```python
import functools

import jax
import jax.numpy as jnp
from jax import lax
from jax.experimental import pallas as pl
from jax.experimental.pallas import tpu as pltpu
from jax.sharding import PartitionSpec as P

F32 = jnp.float32
BF16 = jnp.bfloat16
HALF = 64
LEN = 128
EPS = 1e-06
TOP = 32512.0
CODE = 64.0
VMEM_LIMIT = 40 * 1024 * 1024
PARTS = 2


def dot(a, b):
    return jnp.dot(a, b, preferred_element_type=F32)


def dot_nt(a, b):
    return lax.dot_general(a, b, (((1,), (1,)), ((), ())), preferred_element_type=F32)


def split(x):
    high = x.astype(BF16)
    return high, (x - high.astype(F32)).astype(BF16)


def iota(shape, dim):
    return lax.broadcasted_iota(jnp.int32, shape, dim)


def step_of(code):
    return jnp.exp2(code * (1.0 / CODE)) * (1.0 / TOP)


def encode(x):
    peak = jnp.maximum(jnp.max(jnp.abs(x), axis=0, keepdims=True), 1e-30)
    code = jnp.ceil(jnp.log2(peak) * CODE) + 1.0
    inverse_step = 1.0 / step_of(code)
    whole = jnp.floor(x * inverse_step + 0.5)
    whole = jnp.minimum(jnp.maximum(whole, -32767.0), 32767.0)
    return whole.astype(jnp.int32).astype(jnp.int16), code


def code_tile(codes):
    row = iota((16, LEN), 0)
    tile = jnp.zeros((16, LEN), F32)
    for at, code in enumerate(codes):
        tile = jnp.where(row == at, code, tile)
    return tile.astype(jnp.int32).astype(jnp.int16)


def decode_codes(tile):
    return tile.astype(jnp.int32).astype(F32)


def pack_kernel(state_ref, out_ref):
    heads = state_ref.shape[1]
    codes = []
    for h in range(heads):
        whole, code = encode(state_ref[0, h])
        out_ref[0, h * LEN:(h + 1) * LEN, :] = whole
        codes.append(code)
    out_ref[0, heads * LEN:heads * LEN + 16, :] = code_tile(codes)


def pack_parents(parents, part, heads):
    count = parents.shape[0]
    rows = heads * LEN + 16
    return pl.pallas_call(
        pack_kernel,
        grid=(count,),
        in_specs=[pl.BlockSpec((1, heads, LEN, LEN), lambda i: (i, part, 0, 0))],
        out_specs=pl.BlockSpec((1, rows, LEN), lambda i: (i, 0, 0)),
        out_shape=jax.ShapeDtypeStruct((count, rows, LEN), jnp.int16),
        compiler_params=pltpu.CompilerParams(vmem_limit_bytes=VMEM_LIMIT),
    )(parents)


def block_diag(x, mask):
    return jnp.where(mask, jnp.concatenate([x, x], axis=0), jnp.zeros((), x.dtype))


def core(q_ref, k_ref, v_ref, rate_ref, s_ref, gain_ref, live_count, part, store_mixed, store_state):
    key_heads = q_ref.shape[1]
    heads = 2 * key_heads
    all_heads = rate_ref.shape[1] // 2
    row = iota((LEN, LEN), 0)
    col = iota((LEN, LEN), 1)
    incl = row >= col
    strict = row > col
    diag_mask = row == col
    prow = iota((HALF, LEN), 0)
    plane = iota((HALF, LEN), 1)
    pcol = jnp.bitwise_and(plane, HALF - 1)
    left = plane < HALF
    bd_mask = (row < HALF) == (col < HALF)
    eye = (prow == pcol).astype(F32)

    def same(size):
        return (prow // size) == (pcol // size)

    base_mask = same(8)
    off_masks = [jnp.logical_and(same(2 * s), jnp.logical_not(same(s))) for s in (8, 16, 32)]

    rates = rate_ref[0]
    rates = jnp.where(iota(rates.shape, 1) < live_count, rates, 0.0).astype(BF16)
    lower_ones = incl.astype(F32).astype(BF16)
    unit = diag_mask.astype(F32).astype(BF16)
    cols = dot_nt(jnp.concatenate([lower_ones, unit], axis=0), rates)
    g_cols = cols[:LEN]
    b_cols = cols[LEN:]
    g_rows = dot_nt(rates, lower_ones)
    eg_cols = jnp.exp(g_cols)
    live = iota((LEN, LEN), 0) < live_count
    gain = gain_ref[...].astype(F32)

    codes_in = decode_codes(s_ref[0, heads * LEN:heads * LEN + 16, :])
    heads_range = range(heads)

    q = [q_ref[0, m] for m in range(key_heads)]
    k = [k_ref[0, m] for m in range(key_heads)]

    a_full, am, mh, n_col, gs_col = [], [], [], [], []
    for m in range(key_heads):
        gram = dot_nt(jnp.concatenate([q[m], k[m]], axis=0), k[m])
        qk, kk = gram[:LEN], gram[LEN:]
        diagonal = jnp.where(diag_mask, kk, 0.0)
        norm_row = lax.rsqrt(jnp.sum(diagonal, axis=0, keepdims=True) + EPS)
        norm_col = lax.rsqrt(jnp.sum(diagonal, axis=1, keepdims=True) + EPS)
        qk = qk * norm_row
        kk = kk * norm_row
        n_col.append(norm_col)
        for r in range(2):
            h = 2 * m + r
            at = part * heads + h
            g_c = g_cols[:, at:at + 1]
            g_r = g_rows[at:at + 1, :]
            pair = jnp.exp(jnp.where(incl, g_c - g_r, -1e4))
            mix = qk * pair
            lower = jnp.where(strict, kk * pair, 0.0) * (b_cols[:, all_heads + at:all_heads + at + 1] * norm_col)
            lower_h, lower_l = split(lower)
            mix_h, mix_l = split(mix)
            a_full.append(lower)
            mh.append(mix_h)
            am.append(
                jnp.concatenate(
                    [
                        jnp.concatenate([lower_h, lower_l], axis=1),
                        jnp.concatenate([mix_h, mix_l], axis=1),
                    ],
                    axis=0,
                )
            )

    packed = [jnp.where(left, a_full[h][:HALF], a_full[h][HALF:]) for h in heads_range]
    base = [jnp.where(base_mask, packed[h], 0.0) for h in heads_range]
    base_h = [base[h].astype(BF16) for h in heads_range]
    power = [dot(base_h[h], block_diag(base_h[h], bd_mask)).astype(BF16) for h in heads_range]
    x = [eye - base[h] for h in heads_range]
    both = [
        dot(jnp.concatenate([x[h].astype(BF16), power[h]], axis=0), block_diag(power[h], bd_mask))
        for h in heads_range
    ]
    x = [x[h] + both[h][:HALF] for h in heads_range]
    power = [both[h][HALF:].astype(BF16) for h in heads_range]
    x = [x[h] + dot(x[h].astype(BF16), block_diag(power[h], bd_mask)) for h in heads_range]
    for off in off_masks:
        x_h = [x[h].astype(BF16) for h in heads_range]
        t = [
            dot(jnp.where(off, packed[h], 0.0).astype(BF16), block_diag(x_h[h], bd_mask)).astype(BF16)
            for h in heads_range
        ]
        x = [x[h] - dot(x_h[h], block_diag(t[h], bd_mask)) for h in heads_range]
    x_h = [x[h].astype(BF16) for h in heads_range]
    t = [
        dot(jnp.where(left, a_full[h][HALF:], 0.0).astype(BF16), block_diag(x_h[h], bd_mask)).astype(BF16)
        for h in heads_range
    ]
    zero_h = jnp.zeros((HALF, LEN), BF16)
    corner = [
        dot(jnp.where(left, zero_h, x_h[h]), jnp.concatenate([t[h], t[h]], axis=0)) for h in heads_range
    ]
    inv = [
        jnp.concatenate(
            [jnp.where(left, x[h], 0.0), jnp.where(left, -corner[h], x[h])], axis=0
        ).astype(BF16)
        for h in heads_range
    ]

    state, products = [], []
    for m in range(key_heads):
        highs, lows = [], []
        for r in range(2):
            h = 2 * m + r
            whole = s_ref[0, h * LEN:(h + 1) * LEN, :].astype(jnp.int32).astype(F32)
            high, low = split(whole)
            highs.append(high)
            lows.append(low)
            state.append(whole)
        rhs = jnp.concatenate(
            [jnp.concatenate(highs, axis=1), jnp.concatenate(lows, axis=1)], axis=0
        )
        lhs = jnp.concatenate([q[m], k[m]], axis=0)
        products.append(dot(jnp.concatenate([lhs, lhs], axis=1), rhs))

    first, right = [], []
    for h in heads_range:
        m, r = h // 2, h % 2
        at = part * heads + h
        step = step_of(codes_in[h:h + 1, :])
        ks = products[m][LEN:, r * LEN:(r + 1) * LEN] * step
        eg = eg_cols[:, at:at + 1]
        want = b_cols[:, all_heads + at:all_heads + at + 1] * (
            v_ref[0, m, r].astype(F32) - (eg * n_col[m]) * ks
        )
        right.append(want)
        first.append(dot(inv[h], want.astype(BF16)).astype(BF16))
    am_v = [dot(am[h], jnp.concatenate([first[h], first[h]], axis=0)) for h in heads_range]
    delta = [
        dot(inv[h], (right[h] - first[h].astype(F32) - am_v[h][:LEN]).astype(BF16)) for h in heads_range
    ]
    scaled_h, scaled_l = [], []
    for h in heads_range:
        m, r = h // 2, h % 2
        at = part * heads + h
        step = step_of(codes_in[h:h + 1, :])
        qs = products[m][:LEN, r * LEN:(r + 1) * LEN] * step
        out = eg_cols[:, at:at + 1] * qs + am_v[h][LEN:] + dot(mh[h], delta[h].astype(BF16))
        mean_square = jnp.mean(out * out, axis=1, keepdims=True)
        normed = out * lax.rsqrt(mean_square + EPS) * gain
        store_mixed(m, r, jnp.where(live, normed, 0.0).astype(BF16))
        g_c = g_cols[:, at:at + 1]
        tail = jnp.exp(g_c[LEN - 1:LEN, :] - g_c) * n_col[m]
        high, low = split(tail * (first[h].astype(F32) + delta[h]))
        scaled_h.append(high)
        scaled_l.append(low)
    finals = []
    for m in range(key_heads):
        turned = jnp.transpose(k[m])
        rhs = jnp.concatenate(
            [
                jnp.concatenate(scaled_h[2 * m:2 * m + 2], axis=1),
                jnp.concatenate(scaled_l[2 * m:2 * m + 2], axis=1),
            ],
            axis=0,
        )
        added = dot(jnp.concatenate([turned, turned], axis=1), rhs)
        for r in range(2):
            h = 2 * m + r
            at = part * heads + h
            step = step_of(codes_in[h:h + 1, :])
            keep = eg_cols[LEN - 1:LEN, at:at + 1] * step
            finals.append(keep * state[h] + added[:, r * LEN:(r + 1) * LEN])
    store_state(finals)


def away_kernel(part, aliased, table, q_ref, k_ref, v_ref, rate_ref, s_ref, gain_ref, *refs):
    mixed_ref, packed_ref = refs[-2:]
    i = pl.program_id(0)

    def store_mixed(m, r, rows):
        mixed_ref[0, m, r] = rows

    def store_state(finals):
        codes = []
        for h, final in enumerate(finals):
            whole, code = encode(final)
            packed_ref[0, h * LEN:(h + 1) * LEN, :] = whole
            codes.append(code)
        packed_ref[0, len(finals) * LEN:len(finals) * LEN + 16, :] = code_tile(codes)

    core(q_ref, k_ref, v_ref, rate_ref, s_ref, gain_ref, table[2, i], part, store_mixed, store_state)


def home_kernel(part, aliased, table, q_ref, k_ref, v_ref, rate_ref, s_ref, gain_ref, *refs):
    mixed_ref, final_ref = refs[-2:]
    i = pl.program_id(0)

    def store_mixed(m, r, rows):
        mixed_ref[0, m, r] = rows

    def store_state(finals):
        for h, final in enumerate(finals):
            final_ref[0, h] = final

    core(q_ref, k_ref, v_ref, rate_ref, s_ref, gain_ref, table[2, i], part, store_mixed, store_state)


def recurrence(part, table, q, k, v, rates, parents, gain, mixed, final_shape=None, final=None):
    count = table.shape[1]
    key_heads = q.shape[1] // PARTS
    heads = 2 * key_heads
    rows = heads * LEN + 16
    in_specs = [
        pl.BlockSpec((1, key_heads, LEN, LEN), lambda i, t: (t[0, i], part, 0, 0)),
        pl.BlockSpec((1, key_heads, LEN, LEN), lambda i, t: (t[0, i], part, 0, 0)),
        pl.BlockSpec((1, key_heads, 2, LEN, LEN), lambda i, t: (t[0, i], part, 0, 0, 0)),
        pl.BlockSpec((1,) + rates.shape[1:], lambda i, t: (t[0, i], 0, 0)),
        pl.BlockSpec((1, rows, LEN), lambda i, t: (t[1, i], 0, 0)),
        pl.BlockSpec((1, LEN), lambda i, t: (0, 0)),
    ]
    operands = [q, k, v, rates, parents, gain]
    aliases = {}
    if mixed is not None:
        in_specs.append(pl.BlockSpec(memory_space=pl.ANY))
        aliases[1 + len(operands)] = 0
        operands.append(mixed)
    mixed_spec = pl.BlockSpec((1, key_heads, 2, LEN, LEN), lambda i, t: (t[0, i], part, 0, 0, 0))
    mixed_shape = jax.ShapeDtypeStruct(v.shape, BF16)
    if final_shape is None:
        body = away_kernel
        state_spec = pl.BlockSpec((1, rows, LEN), lambda i, t: (i, 0, 0))
        state_shape = jax.ShapeDtypeStruct((count, rows, LEN), jnp.int16)
    else:
        body = home_kernel
        if final is not None:
            in_specs.append(pl.BlockSpec(memory_space=pl.ANY))
            aliases[1 + len(operands)] = 1
            operands.append(final)
        state_spec = pl.BlockSpec((1, heads, LEN, LEN), lambda i, t: (t[3, i], part, 0, 0))
        state_shape = jax.ShapeDtypeStruct(final_shape, F32)
    return pl.pallas_call(
        functools.partial(body, part, mixed is not None),
        grid_spec=pltpu.PrefetchScalarGridSpec(
            num_scalar_prefetch=1,
            grid=(count,),
            in_specs=in_specs,
            out_specs=[mixed_spec, state_spec],
        ),
        out_shape=[mixed_shape, state_shape],
        input_output_aliases=aliases,
        compiler_params=pltpu.CompilerParams(vmem_limit_bytes=VMEM_LIMIT),
        cost_estimate=pl.CostEstimate(
            flops=count * key_heads * 300_000_000, bytes_accessed=count * key_heads * 400_000, transcendentals=0
        ),
    )(table, *operands)


def unpack_kernel(table, packed_ref, old_ref, out_ref):
    heads = out_ref.shape[1]
    codes = decode_codes(packed_ref[0, heads * LEN:heads * LEN + 16, :])
    for h in range(heads):
        whole = packed_ref[0, h * LEN:(h + 1) * LEN, :].astype(jnp.int32).astype(F32)
        out_ref[0, h] = whole * step_of(codes[h:h + 1, :])


def unpack_states(part, table, packed, final):
    count, rows = packed.shape[:2]
    heads = final.shape[1] // PARTS
    return pl.pallas_call(
        unpack_kernel,
        grid_spec=pltpu.PrefetchScalarGridSpec(
            num_scalar_prefetch=1,
            grid=(count,),
            in_specs=[
                pl.BlockSpec((1, rows, LEN), lambda i, t: (i, 0, 0)),
                pl.BlockSpec(memory_space=pl.ANY),
            ],
            out_specs=pl.BlockSpec((1, heads, LEN, LEN), lambda i, t: (t[i], part, 0, 0)),
        ),
        out_shape=jax.ShapeDtypeStruct(final.shape, F32),
        input_output_aliases={2: 0},
        compiler_params=pltpu.CompilerParams(vmem_limit_bytes=VMEM_LIMIT),
        cost_estimate=pl.CostEstimate(
            flops=0, bytes_accessed=count * heads * LEN * LEN * 6, transcendentals=0
        ),
    )(table, packed, final)


def shards(
    queries,
    keys,
    values,
    log_decay,
    write_rate,
    norm_gain,
    parent_cache,
    order,
    parent_owner,
    parent_slot,
    token_count,
):
    seq_count = lax.axis_size("seq")
    me = lax.axis_index("seq")
    per_device, length, key_heads, key_dim = queries.shape
    per_peer = per_device // seq_count
    cache_rows = parent_cache.shape[0]
    heads = 2 * key_heads
    part_heads = heads // PARTS

    parents = parent_cache.reshape((cache_rows, heads, key_dim, key_dim))
    gathered = [
        lax.all_gather(pack_parents(parents, part, part_heads), "seq", axis=0, tiled=True)
        for part in range(PARTS)
    ]

    q = jnp.transpose(queries, (0, 2, 1, 3))
    k = jnp.transpose(keys, (0, 2, 1, 3))
    v = jnp.transpose(values, (0, 2, 3, 1, 4))

    def rows_of(tensor):
        return jnp.transpose(tensor, (0, 2, 3, 1)).reshape(per_device, heads, length).astype(F32)

    rates = jnp.concatenate([rows_of(log_decay), rows_of(write_rate)], axis=1)
    gain = norm_gain.reshape(1, -1)

    wanted_all = parent_owner * cache_rows + parent_slot
    slot_grid = order.reshape(seq_count, seq_count, per_peer)
    mine = lax.dynamic_index_in_dim(slot_grid, me, 1, keepdims=False)
    local_ids = mine - me * per_device
    here_parent = lax.dynamic_slice_in_dim(wanted_all, me * per_device, per_device)
    here_count = lax.dynamic_slice_in_dim(token_count, me * per_device, per_device)

    def look_up(vector, ids):
        hit = ids[..., None] == jnp.arange(per_device, dtype=jnp.int32)
        return jnp.sum(jnp.where(hit, vector, 0), axis=-1)

    slots = me * per_peer + jnp.broadcast_to(jnp.arange(per_peer, dtype=jnp.int32), local_ids.shape)
    tables = jnp.stack(
        [local_ids, look_up(here_parent, local_ids), look_up(here_count, local_ids), slots], axis=1
    ).astype(jnp.int32)

    final_shape = (per_device, heads, key_dim, key_dim)
    mixed, final = None, None
    arrived = []
    for part in range(PARTS):
        for away in reversed(range(seq_count)):
            peer = jnp.bitwise_xor(me, away)
            table = lax.dynamic_index_in_dim(tables, peer, 0, keepdims=False)
            common = (part, table, q, k, v, rates, gathered[part], gain, mixed)
            if away:
                mixed, packed = recurrence(*common)
                sent = lax.ppermute(packed, "seq", [(i, i ^ away) for i in range(seq_count)])
                arrived.append((part, peer, sent))
            else:
                mixed, final = recurrence(*common, final_shape, final)
    for part, peer, packed in arrived:
        table = peer * per_peer + jnp.arange(per_peer, dtype=jnp.int32)
        final = unpack_states(part, table, packed, final)
    mixed_out = jnp.transpose(mixed, (0, 3, 1, 2, 4))
    final_out = final.reshape((per_device, key_heads, 2, key_dim, key_dim))
    return (mixed_out, final_out)


def solution(mesh):
    placed = (
        P(("groups", "seq"), None, ("head", "sub"), None),
        P(("groups", "seq"), None, ("head", "sub"), None),
        P(("groups", "seq"), None, ("head", "sub"), None, None),
        P(("groups", "seq"), None, ("head", "sub"), None),
        P(("groups", "seq"), None, ("head", "sub"), None),
        P(),
        P(("groups", "seq"), ("head", "sub"), None, None, None),
        P("groups"),
        P("groups"),
        P("groups"),
        P("groups"),
    )
    return jax.shard_map(
        shards,
        mesh=mesh,
        in_specs=placed,
        out_specs=(
            P(("groups", "seq"), None, ("head", "sub"), None, None),
            P(("groups", "seq"), ("head", "sub"), None, None, None),
        ),
        check_vma=False,
    )
```

```python
import functools

import jax
import jax.numpy as jnp
from jax import lax
from jax.experimental import pallas as pl
from jax.experimental.pallas import tpu as pltpu
from jax.sharding import PartitionSpec as P

F32 = jnp.float32
BF16 = jnp.bfloat16
HALF = 64
LEN = 128
EPS = 1e-06
TOP = 32512.0
CODE = 64.0
VMEM_LIMIT = 40 * 1024 * 1024
WIDE_VMEM_LIMIT = 57 * 1024 * 1024
PARTS = 2
CODE_ROWS = 8
TOGETHER = 2


def dot(a, b):
    return jnp.dot(a, b, preferred_element_type=F32)


def dot_nt(a, b):
    return lax.dot_general(a, b, (((1,), (1,)), ((), ())), preferred_element_type=F32)


def split(x):
    high = x.astype(BF16)
    return high, (x - high.astype(F32)).astype(BF16)


def iota(shape, dim):
    return lax.broadcasted_iota(jnp.int32, shape, dim)


def step_of(code):
    return jnp.exp2(code * (1.0 / CODE)) * (1.0 / TOP)


def encode(x):
    peak = jnp.maximum(jnp.max(jnp.abs(x), axis=0, keepdims=True), 1e-30)
    code = jnp.ceil(jnp.log2(peak) * CODE) + 1.0
    inverse_step = 1.0 / step_of(code)
    whole = jnp.floor(x * inverse_step + 0.5)
    whole = jnp.minimum(jnp.maximum(whole, -32767.0), 32767.0).astype(jnp.int32)
    words = jnp.bitwise_or(lax.shift_left(whole[:HALF], 16), jnp.bitwise_and(whole[HALF:], 0xFFFF))
    return words, code


def decode(words):
    top = lax.shift_right_arithmetic(words, 16)
    bottom = lax.shift_right_arithmetic(lax.shift_left(words, 16), 16)
    return jnp.concatenate([top, bottom], axis=0).astype(F32)


def code_tile(codes):
    row = iota((CODE_ROWS, LEN), 0)
    tile = jnp.zeros((CODE_ROWS, LEN), F32)
    for at, code in enumerate(codes):
        tile = jnp.where(row == at, code, tile)
    return tile.astype(jnp.int32)


def store_packed(ref, states):
    codes = []
    for h, state in enumerate(states):
        words, code = encode(state)
        ref[0, h * HALF:(h + 1) * HALF, :] = words
        codes.append(code)
    at = len(states) * HALF
    ref[0, at:at + CODE_ROWS, :] = code_tile(codes)


def load_steps(ref, heads):
    codes = ref[0, heads * HALF:heads * HALF + CODE_ROWS, :].astype(F32)
    return step_of(codes)


def pack_kernel(state_ref, out_ref):
    store_packed(out_ref, [state_ref[0, h] for h in range(state_ref.shape[1])])


def pack_parents(parents, part, heads):
    count = parents.shape[0]
    rows = heads * HALF + CODE_ROWS
    return pl.pallas_call(
        pack_kernel,
        grid=(count,),
        in_specs=[pl.BlockSpec((1, heads, LEN, LEN), lambda i: (i, part, 0, 0))],
        out_specs=pl.BlockSpec((1, rows, LEN), lambda i: (i, 0, 0)),
        out_shape=jax.ShapeDtypeStruct((count, rows, LEN), jnp.int32),
        compiler_params=pltpu.CompilerParams(vmem_limit_bytes=VMEM_LIMIT),
    )(parents)


def block_diag(x, mask):
    return jnp.where(mask, jnp.concatenate([x, x], axis=0), jnp.zeros((), x.dtype))


def pair_kernel(part, q_ref, k_ref, rate_ref, inv_ref, am_ref):
    expansions, key_heads = q_ref.shape[:2]
    heads = 2 * key_heads
    all_heads = rate_ref.shape[1] // 2
    row = iota((LEN, LEN), 0)
    col = iota((LEN, LEN), 1)
    incl = row >= col
    strict = row > col
    diag_mask = row == col
    prow = iota((HALF, LEN), 0)
    plane = iota((HALF, LEN), 1)
    pcol = jnp.bitwise_and(plane, HALF - 1)
    left = plane < HALF
    bd_mask = (row < HALF) == (col < HALF)
    eye = (prow == pcol).astype(F32)

    def same(size):
        return (prow // size) == (pcol // size)

    base_mask = same(8)
    off_masks = [jnp.logical_and(same(2 * s), jnp.logical_not(same(s))) for s in (8, 16, 32)]
    lower_ones = incl.astype(F32).astype(BF16)
    unit = diag_mask.astype(F32).astype(BF16)

    a_full, where_at = [], []
    for e in range(expansions):
        rates = rate_ref[e].astype(BF16)
        cols = dot_nt(jnp.concatenate([lower_ones, unit], axis=0), rates)
        g_cols = cols[:LEN]
        b_cols = cols[LEN:]
        g_rows = dot_nt(rates, lower_ones)
        for m in range(key_heads):
            k = k_ref[e, m]
            gram = dot_nt(jnp.concatenate([q_ref[e, m], k], axis=0), k)
            qk, kk = gram[:LEN], gram[LEN:]
            diagonal = jnp.where(diag_mask, kk, 0.0)
            norm_row = lax.rsqrt(jnp.sum(diagonal, axis=0, keepdims=True) + EPS)
            norm_col = lax.rsqrt(jnp.sum(diagonal, axis=1, keepdims=True) + EPS)
            qk = qk * norm_row
            kk = kk * norm_row
            for r in range(2):
                h = 2 * m + r
                at = part * heads + h
                g_c = g_cols[:, at:at + 1]
                g_r = g_rows[at:at + 1, :]
                pair = jnp.exp(jnp.where(incl, g_c - g_r, -1e4))
                mix = qk * pair
                b_c = b_cols[:, all_heads + at:all_heads + at + 1]
                lower = jnp.where(strict, kk * pair, 0.0) * (b_c * norm_col)
                lower_h, lower_l = split(lower)
                mix_h, mix_l = split(mix)
                am_ref[e, h, :LEN, :LEN] = lower_h
                am_ref[e, h, :LEN, LEN:] = lower_l
                am_ref[e, h, LEN:, :LEN] = mix_h
                am_ref[e, h, LEN:, LEN:] = mix_l
                a_full.append(lower)
                where_at.append((e, h))

    chains = range(len(a_full))
    packed = [jnp.where(left, a_full[c][:HALF], a_full[c][HALF:]) for c in chains]
    base = [jnp.where(base_mask, packed[c], 0.0) for c in chains]
    base_h = [base[c].astype(BF16) for c in chains]
    power = [dot(base_h[c], block_diag(base_h[c], bd_mask)).astype(BF16) for c in chains]
    x = [eye - base[c] for c in chains]
    both = [
        dot(jnp.concatenate([x[c].astype(BF16), power[c]], axis=0), block_diag(power[c], bd_mask))
        for c in chains
    ]
    x = [x[c] + both[c][:HALF] for c in chains]
    power = [both[c][HALF:].astype(BF16) for c in chains]
    x = [x[c] + dot(x[c].astype(BF16), block_diag(power[c], bd_mask)) for c in chains]
    for off in off_masks:
        x_h = [x[c].astype(BF16) for c in chains]
        t = [
            dot(jnp.where(off, packed[c], 0.0).astype(BF16), block_diag(x_h[c], bd_mask)).astype(BF16)
            for c in chains
        ]
        x = [x[c] - dot(x_h[c], block_diag(t[c], bd_mask)) for c in chains]
    x_h = [x[c].astype(BF16) for c in chains]
    t = [
        dot(jnp.where(left, a_full[c][HALF:], 0.0).astype(BF16), block_diag(x_h[c], bd_mask)).astype(BF16)
        for c in chains
    ]
    zero_h = jnp.zeros((HALF, LEN), BF16)
    corner = [dot(jnp.where(left, zero_h, x_h[c]), jnp.concatenate([t[c], t[c]], axis=0)) for c in chains]
    for c in chains:
        e, h = where_at[c]
        inv_ref[e, h, :HALF, :] = jnp.where(left, x[c], 0.0).astype(BF16)
        inv_ref[e, h, HALF:, :] = jnp.where(left, -corner[c], x[c]).astype(BF16)


def pair_parts(part, q, k, rates):
    count, all_key_heads = q.shape[:2]
    key_heads = all_key_heads // PARTS
    heads = 2 * key_heads
    block = TOGETHER
    head_block = pl.BlockSpec((block, key_heads, LEN, LEN), lambda i: (i, part, 0, 0))
    return pl.pallas_call(
        functools.partial(pair_kernel, part),
        grid=(count // block,),
        in_specs=[
            head_block,
            head_block,
            pl.BlockSpec((block,) + rates.shape[1:], lambda i: (i, 0, 0)),
        ],
        out_specs=[
            pl.BlockSpec((block, heads, LEN, LEN), lambda i: (i, 0, 0, 0)),
            pl.BlockSpec((block, heads, 2 * LEN, 2 * LEN), lambda i: (i, 0, 0, 0)),
        ],
        out_shape=[
            jax.ShapeDtypeStruct((count, heads, LEN, LEN), BF16),
            jax.ShapeDtypeStruct((count, heads, 2 * LEN, 2 * LEN), BF16),
        ],
        compiler_params=pltpu.CompilerParams(vmem_limit_bytes=VMEM_LIMIT),
        cost_estimate=pl.CostEstimate(flops=1000, bytes_accessed=1000, transcendentals=0),
    )(q, k, rates)


def state_kernel(
    part, home, table, q_ref, k_ref, v_ref, rate_ref, inv_ref, am_ref, s_ref, gain_ref, *refs
):
    mixed_ref, state_ref = refs[-2:]
    key_heads = q_ref.shape[1]
    heads = 2 * key_heads
    all_heads = rate_ref.shape[1] // 2
    live_count = table[2, pl.program_id(0)]
    row = iota((LEN, LEN), 0)
    col = iota((LEN, LEN), 1)
    lower_ones = (row >= col).astype(F32).astype(BF16)
    unit = (row == col).astype(F32).astype(BF16)
    rates = rate_ref[0].astype(BF16)
    cols = dot_nt(jnp.concatenate([lower_ones, unit], axis=0), rates)
    g_cols = cols[:LEN]
    b_cols = cols[LEN:]
    eg_cols = jnp.exp(g_cols)
    live = row < live_count
    gain = gain_ref[...].astype(F32)
    steps = load_steps(s_ref, heads)

    def decay_at(h):
        return eg_cols[:, part * heads + h:part * heads + h + 1]

    state, products, n_col = [], [], []
    for m in range(key_heads):
        highs, lows = [], []
        for r in range(2):
            h = 2 * m + r
            whole = decode(s_ref[0, h * HALF:(h + 1) * HALF, :])
            high, low = split(whole)
            highs.append(high)
            lows.append(low)
            state.append(whole)
        rhs = jnp.concatenate(
            [jnp.concatenate(highs, axis=1), jnp.concatenate(lows, axis=1)], axis=0
        )
        lhs = jnp.concatenate([q_ref[0, m], k_ref[0, m]], axis=0)
        products.append(dot(jnp.concatenate([lhs, lhs], axis=1), rhs))
        keys = k_ref[0, m].astype(F32)
        n_col.append(lax.rsqrt(jnp.sum(keys * keys, axis=1, keepdims=True) + EPS))

    every = range(heads)
    right, first = [], []
    for h in every:
        m, r = h // 2, h % 2
        at = all_heads + part * heads + h
        ks = products[m][LEN:, r * LEN:(r + 1) * LEN] * steps[h:h + 1, :]
        want = b_cols[:, at:at + 1] * (v_ref[0, m, r].astype(F32) - (decay_at(h) * n_col[m]) * ks)
        right.append(want)
        first.append(dot(inv_ref[0, h], want.astype(BF16)).astype(BF16))
    am_v = [dot(am_ref[0, h], jnp.concatenate([first[h], first[h]], axis=0)) for h in every]
    delta = [
        dot(inv_ref[0, h], (right[h] - first[h].astype(F32) - am_v[h][:LEN]).astype(BF16)) for h in every
    ]
    scaled_h, scaled_l = [], []
    for h in every:
        g_c = g_cols[:, part * heads + h:part * heads + h + 1]
        tail = jnp.exp(g_c[LEN - 1:LEN, :] - g_c) * n_col[h // 2]
        high, low = split(tail * (first[h].astype(F32) + delta[h]))
        scaled_h.append(high)
        scaled_l.append(low)
    finals = []
    for m in range(key_heads):
        turned = jnp.transpose(k_ref[0, m])
        rhs = jnp.concatenate(
            [
                jnp.concatenate(scaled_h[2 * m:2 * m + 2], axis=1),
                jnp.concatenate(scaled_l[2 * m:2 * m + 2], axis=1),
            ],
            axis=0,
        )
        added = dot(jnp.concatenate([turned, turned], axis=1), rhs)
        for r in range(2):
            h = 2 * m + r
            keep = decay_at(h)[LEN - 1:LEN, :] * steps[h:h + 1, :]
            finals.append(keep * state[h] + added[:, r * LEN:(r + 1) * LEN])
    for h in every:
        m, r = h // 2, h % 2
        qs = products[m][:LEN, r * LEN:(r + 1) * LEN] * steps[h:h + 1, :]
        out = decay_at(h) * qs + am_v[h][LEN:] + dot(am_ref[0, h, LEN:, :LEN], delta[h].astype(BF16))
        mean_square = jnp.mean(out * out, axis=1, keepdims=True)
        normed = out * lax.rsqrt(mean_square + EPS) * gain
        mixed_ref[0, m, r] = jnp.where(live, normed, 0.0).astype(BF16)
    if home:
        for h in every:
            state_ref[0, h] = finals[h]
    else:
        store_packed(state_ref, finals)


def recurrence(part, table, q, k, v, rates, pairs, parents, gain, mixed, final_shape=None, final=None):
    count = table.shape[1]
    key_heads = q.shape[1] // PARTS
    heads = 2 * key_heads
    rows = heads * HALF + CODE_ROWS
    in_specs = [
        pl.BlockSpec((1, key_heads, LEN, LEN), lambda i, t: (t[0, i], part, 0, 0)),
        pl.BlockSpec((1, key_heads, LEN, LEN), lambda i, t: (t[0, i], part, 0, 0)),
        pl.BlockSpec((1, key_heads, 2, LEN, LEN), lambda i, t: (t[0, i], part, 0, 0, 0)),
        pl.BlockSpec((1,) + rates.shape[1:], lambda i, t: (t[0, i], 0, 0)),
        pl.BlockSpec((1, heads, LEN, LEN), lambda i, t: (t[0, i], 0, 0, 0)),
        pl.BlockSpec((1, heads, 2 * LEN, 2 * LEN), lambda i, t: (t[0, i], 0, 0, 0)),
        pl.BlockSpec((1, rows, LEN), lambda i, t: (t[1, i], 0, 0)),
        pl.BlockSpec((1, LEN), lambda i, t: (0, 0)),
    ]
    operands = [q, k, v, rates, *pairs, parents, gain]
    aliases = {}
    if mixed is not None:
        in_specs.append(pl.BlockSpec(memory_space=pl.ANY))
        aliases[1 + len(operands)] = 0
        operands.append(mixed)
    mixed_spec = pl.BlockSpec((1, key_heads, 2, LEN, LEN), lambda i, t: (t[0, i], part, 0, 0, 0))
    mixed_shape = jax.ShapeDtypeStruct(v.shape, BF16)
    if final_shape is None:
        state_spec = pl.BlockSpec((1, rows, LEN), lambda i, t: (i, 0, 0))
        state_shape = jax.ShapeDtypeStruct((count, rows, LEN), jnp.int32)
    else:
        if final is not None:
            in_specs.append(pl.BlockSpec(memory_space=pl.ANY))
            aliases[1 + len(operands)] = 1
            operands.append(final)
        state_spec = pl.BlockSpec((1, heads, LEN, LEN), lambda i, t: (t[3, i], part, 0, 0))
        state_shape = jax.ShapeDtypeStruct(final_shape, F32)
    return pl.pallas_call(
        functools.partial(state_kernel, part, final_shape is not None),
        grid_spec=pltpu.PrefetchScalarGridSpec(
            num_scalar_prefetch=1,
            grid=(count,),
            in_specs=in_specs,
            out_specs=[mixed_spec, state_spec],
        ),
        out_shape=[mixed_shape, state_shape],
        input_output_aliases=aliases,
        compiler_params=pltpu.CompilerParams(vmem_limit_bytes=WIDE_VMEM_LIMIT),
        cost_estimate=pl.CostEstimate(flops=1000, bytes_accessed=1000, transcendentals=0),
    )(table, *operands)


def unpack_kernel(table, packed_ref, old_ref, out_ref):
    heads = out_ref.shape[1]
    steps = load_steps(packed_ref, heads)
    for h in range(heads):
        out_ref[0, h] = decode(packed_ref[0, h * HALF:(h + 1) * HALF, :]) * steps[h:h + 1, :]


def unpack_states(part, table, packed, final):
    count, rows = packed.shape[:2]
    heads = final.shape[1] // PARTS
    return pl.pallas_call(
        unpack_kernel,
        grid_spec=pltpu.PrefetchScalarGridSpec(
            num_scalar_prefetch=1,
            grid=(count,),
            in_specs=[
                pl.BlockSpec((1, rows, LEN), lambda i, t: (i, 0, 0)),
                pl.BlockSpec(memory_space=pl.ANY),
            ],
            out_specs=pl.BlockSpec((1, heads, LEN, LEN), lambda i, t: (t[i], part, 0, 0)),
        ),
        out_shape=jax.ShapeDtypeStruct(final.shape, F32),
        input_output_aliases={2: 0},
        compiler_params=pltpu.CompilerParams(vmem_limit_bytes=VMEM_LIMIT),
        cost_estimate=pl.CostEstimate(flops=1000, bytes_accessed=1000, transcendentals=0),
    )(table, packed, final)


def shards(
    queries,
    keys,
    values,
    log_decay,
    write_rate,
    norm_gain,
    parent_cache,
    order,
    parent_owner,
    parent_slot,
    token_count,
):
    seq_count = lax.axis_size("seq")
    me = lax.axis_index("seq")
    per_device, length, key_heads, key_dim = queries.shape
    per_peer = per_device // seq_count
    cache_rows = parent_cache.shape[0]
    heads = 2 * key_heads
    part_heads = heads // PARTS

    parents = parent_cache.reshape((cache_rows, heads, key_dim, key_dim))
    gathered = [
        lax.all_gather(pack_parents(parents, part, part_heads), "seq", axis=0, tiled=True)
        for part in range(PARTS)
    ]

    q = jnp.transpose(queries, (0, 2, 1, 3))
    k = jnp.transpose(keys, (0, 2, 1, 3))
    v = jnp.transpose(values, (0, 2, 3, 1, 4))

    def rows_of(tensor):
        return jnp.transpose(tensor, (0, 2, 3, 1)).reshape(per_device, heads, length).astype(F32)

    here_count = lax.dynamic_slice_in_dim(token_count, me * per_device, per_device)
    alive = jnp.arange(length, dtype=jnp.int32) < here_count[:, None, None]
    rates = jnp.where(alive, jnp.concatenate([rows_of(log_decay), rows_of(write_rate)], axis=1), 0.0)
    gain = norm_gain.reshape(1, -1)
    pairs = [pair_parts(part, q, k, rates) for part in range(PARTS)]
    gathered[0], pairs, v = lax.optimization_barrier((gathered[0], pairs, v))

    wanted_all = parent_owner * cache_rows + parent_slot
    slot_grid = order.reshape(seq_count, seq_count, per_peer)
    mine = lax.dynamic_index_in_dim(slot_grid, me, 1, keepdims=False)
    local_ids = mine - me * per_device
    here_parent = lax.dynamic_slice_in_dim(wanted_all, me * per_device, per_device)

    def look_up(vector, ids):
        hit = ids[..., None] == jnp.arange(per_device, dtype=jnp.int32)
        return jnp.sum(jnp.where(hit, vector, 0), axis=-1)

    slots = me * per_peer + jnp.broadcast_to(jnp.arange(per_peer, dtype=jnp.int32), local_ids.shape)
    tables = jnp.stack(
        [local_ids, look_up(here_parent, local_ids), look_up(here_count, local_ids), slots], axis=1
    ).astype(jnp.int32)

    final_shape = (per_device, heads, key_dim, key_dim)
    mixed, final = None, None
    arrived = []
    turns = [(part, away) for part in range(PARTS) for away in reversed(range(1, seq_count))]
    turns += [(part, 0) for part in range(PARTS)]
    for part, away in turns:
        peer = jnp.bitwise_xor(me, away)
        table = lax.dynamic_index_in_dim(tables, peer, 0, keepdims=False)
        if part and away:
            at = (part - 1) * (seq_count - 1) + seq_count - 1 - away
            before, other_peer, sent = arrived[at]
            mixed, sent = lax.optimization_barrier((mixed, sent))
            arrived[at] = (before, other_peer, sent)
        common = (part, table, q, k, v, rates, pairs[part], gathered[part], gain, mixed)
        if away:
            mixed, packed = recurrence(*common)
            sent = lax.ppermute(packed, "seq", [(i, i ^ away) for i in range(seq_count)])
            arrived.append((part, peer, sent))
        else:
            mixed, final = recurrence(*common, final_shape, final)
    for part, peer, packed in arrived:
        table = peer * per_peer + jnp.arange(per_peer, dtype=jnp.int32)
        final = unpack_states(part, table, packed, final)
    mixed_out = jnp.transpose(mixed, (0, 3, 1, 2, 4))
    final_out = final.reshape((per_device, key_heads, 2, key_dim, key_dim))
    return (mixed_out, final_out)


def solution(mesh):
    placed = (
        P(("groups", "seq"), None, ("head", "sub"), None),
        P(("groups", "seq"), None, ("head", "sub"), None),
        P(("groups", "seq"), None, ("head", "sub"), None, None),
        P(("groups", "seq"), None, ("head", "sub"), None),
        P(("groups", "seq"), None, ("head", "sub"), None),
        P(),
        P(("groups", "seq"), ("head", "sub"), None, None, None),
        P("groups"),
        P("groups"),
        P("groups"),
        P("groups"),
    )
    return jax.shard_map(
        shards,
        mesh=mesh,
        in_specs=placed,
        out_specs=(
            P(("groups", "seq"), None, ("head", "sub"), None, None),
            P(("groups", "seq"), ("head", "sub"), None, None, None),
        ),
        check_vma=False,
    )
```

```python
import functools

import jax
import jax.numpy as jnp
from jax import lax
from jax.experimental import pallas as pl
from jax.experimental.pallas import tpu as pltpu
from jax.sharding import PartitionSpec as P

F32 = jnp.float32
BF16 = jnp.bfloat16
HALF = 64
LEN = 128
EPS = 1e-06
TOP = 32512.0
CODE = 64.0
VMEM_LIMIT = 40 * 1024 * 1024
WIDE_VMEM_LIMIT = 57 * 1024 * 1024
PARTS = 2
CODE_ROWS = 8
TOGETHER = 2


def dot(a, b):
    return jnp.dot(a, b, preferred_element_type=F32)


def dot_nt(a, b):
    return lax.dot_general(a, b, (((1,), (1,)), ((), ())), preferred_element_type=F32)


def split(x):
    high = x.astype(BF16)
    return high, (x - high.astype(F32)).astype(BF16)


def iota(shape, dim):
    return lax.broadcasted_iota(jnp.int32, shape, dim)


def step_of(code):
    return jnp.exp2(code * (1.0 / CODE)) * (1.0 / TOP)


def encode(x):
    peak = jnp.maximum(jnp.max(jnp.abs(x), axis=0, keepdims=True), 1e-30)
    code = jnp.ceil(jnp.log2(peak) * CODE) + 1.0
    inverse_step = 1.0 / step_of(code)
    whole = jnp.floor(x * inverse_step + 0.5)
    whole = jnp.minimum(jnp.maximum(whole, -32767.0), 32767.0).astype(jnp.int32)
    words = jnp.bitwise_or(lax.shift_left(whole[:HALF], 16), jnp.bitwise_and(whole[HALF:], 0xFFFF))
    return words, code


def decode(words):
    top = lax.shift_right_arithmetic(words, 16)
    bottom = lax.shift_right_arithmetic(lax.shift_left(words, 16), 16)
    return jnp.concatenate([top, bottom], axis=0).astype(F32)


def code_tile(codes):
    row = iota((CODE_ROWS, LEN), 0)
    tile = jnp.zeros((CODE_ROWS, LEN), F32)
    for at, code in enumerate(codes):
        tile = jnp.where(row == at, code, tile)
    return tile.astype(jnp.int32)


def store_packed(ref, states):
    codes = []
    for h, state in enumerate(states):
        words, code = encode(state)
        ref[0, h * HALF:(h + 1) * HALF, :] = words
        codes.append(code)
    at = len(states) * HALF
    ref[0, at:at + CODE_ROWS, :] = code_tile(codes)


def load_steps(ref, heads):
    codes = ref[0, heads * HALF:heads * HALF + CODE_ROWS, :].astype(F32)
    return step_of(codes)


def pack_kernel(state_ref, out_ref):
    store_packed(out_ref, [state_ref[0, h] for h in range(state_ref.shape[1])])


def pack_parents(parents, part, heads):
    count = parents.shape[0]
    rows = heads * HALF + CODE_ROWS
    return pl.pallas_call(
        pack_kernel,
        grid=(count,),
        in_specs=[pl.BlockSpec((1, heads, LEN, LEN), lambda i: (i, part, 0, 0))],
        out_specs=pl.BlockSpec((1, rows, LEN), lambda i: (i, 0, 0)),
        out_shape=jax.ShapeDtypeStruct((count, rows, LEN), jnp.int32),
        compiler_params=pltpu.CompilerParams(vmem_limit_bytes=VMEM_LIMIT),
    )(parents)


def block_diag(x, mask):
    return jnp.where(mask, jnp.concatenate([x, x], axis=0), jnp.zeros((), x.dtype))


def pair_kernel(part, q_ref, k_ref, rate_ref, *refs):
    inv_ref, am_ref = refs[-2:]
    expansions, key_heads = q_ref.shape[:2]
    heads = 2 * key_heads
    all_heads = rate_ref.shape[1] // 2
    row = iota((LEN, LEN), 0)
    col = iota((LEN, LEN), 1)
    incl = row >= col
    strict = row > col
    diag_mask = row == col
    prow = iota((HALF, LEN), 0)
    plane = iota((HALF, LEN), 1)
    pcol = jnp.bitwise_and(plane, HALF - 1)
    left = plane < HALF
    bd_mask = (row < HALF) == (col < HALF)
    eye = (prow == pcol).astype(F32)

    def same(size):
        return (prow // size) == (pcol // size)

    base_mask = same(8)
    off_masks = [jnp.logical_and(same(2 * s), jnp.logical_not(same(s))) for s in (8, 16, 32)]
    lower_ones = incl.astype(F32).astype(BF16)
    unit = diag_mask.astype(F32).astype(BF16)

    a_full, where_at = [], []
    for e in range(expansions):
        rates = rate_ref[e].astype(BF16)
        cols = dot_nt(jnp.concatenate([lower_ones, unit], axis=0), rates)
        g_cols = cols[:LEN]
        b_cols = cols[LEN:]
        g_rows = dot_nt(rates, lower_ones)
        for m in range(key_heads):
            k = k_ref[e, m]
            gram = dot_nt(jnp.concatenate([q_ref[e, m], k], axis=0), k)
            qk, kk = gram[:LEN], gram[LEN:]
            diagonal = jnp.where(diag_mask, kk, 0.0)
            norm_row = lax.rsqrt(jnp.sum(diagonal, axis=0, keepdims=True) + EPS)
            norm_col = lax.rsqrt(jnp.sum(diagonal, axis=1, keepdims=True) + EPS)
            qk = qk * norm_row
            kk = kk * norm_row
            for r in range(2):
                h = 2 * m + r
                at = part * heads + h
                g_c = g_cols[:, at:at + 1]
                g_r = g_rows[at:at + 1, :]
                pair = jnp.exp(jnp.where(incl, g_c - g_r, -1e4))
                mix = qk * pair
                b_c = b_cols[:, all_heads + at:all_heads + at + 1]
                lower = jnp.where(strict, kk * pair, 0.0) * (b_c * norm_col)
                lower_h, lower_l = split(lower)
                mix_h, mix_l = split(mix)
                am_ref[e, h, :LEN, :LEN] = lower_h
                am_ref[e, h, :LEN, LEN:] = lower_l
                am_ref[e, h, LEN:, :LEN] = mix_h
                am_ref[e, h, LEN:, LEN:] = mix_l
                a_full.append(lower)
                where_at.append((e, h))

    chains = range(len(a_full))
    packed = [jnp.where(left, a_full[c][:HALF], a_full[c][HALF:]) for c in chains]
    base = [jnp.where(base_mask, packed[c], 0.0) for c in chains]
    base_h = [base[c].astype(BF16) for c in chains]
    power = [dot(base_h[c], block_diag(base_h[c], bd_mask)).astype(BF16) for c in chains]
    x = [eye - base[c] for c in chains]
    both = [
        dot(jnp.concatenate([x[c].astype(BF16), power[c]], axis=0), block_diag(power[c], bd_mask))
        for c in chains
    ]
    x = [x[c] + both[c][:HALF] for c in chains]
    power = [both[c][HALF:].astype(BF16) for c in chains]
    x = [x[c] + dot(x[c].astype(BF16), block_diag(power[c], bd_mask)) for c in chains]
    for off in off_masks:
        x_h = [x[c].astype(BF16) for c in chains]
        t = [
            dot(jnp.where(off, packed[c], 0.0).astype(BF16), block_diag(x_h[c], bd_mask)).astype(BF16)
            for c in chains
        ]
        x = [x[c] - dot(x_h[c], block_diag(t[c], bd_mask)) for c in chains]
    x_h = [x[c].astype(BF16) for c in chains]
    t = [
        dot(jnp.where(left, a_full[c][HALF:], 0.0).astype(BF16), block_diag(x_h[c], bd_mask)).astype(BF16)
        for c in chains
    ]
    zero_h = jnp.zeros((HALF, LEN), BF16)
    corner = [dot(jnp.where(left, zero_h, x_h[c]), jnp.concatenate([t[c], t[c]], axis=0)) for c in chains]
    for c in chains:
        e, h = where_at[c]
        inv_ref[e, h, :HALF, :] = jnp.where(left, x[c], 0.0).astype(BF16)
        inv_ref[e, h, HALF:, :] = jnp.where(left, -corner[c], x[c]).astype(BF16)


def pair_parts(part, half, q, k, rates, earlier=None):
    count, all_key_heads = q.shape[:2]
    key_heads = all_key_heads // PARTS
    heads = 2 * key_heads
    block = TOGETHER
    turns = count // block // 2
    first = half * turns
    head_block = pl.BlockSpec((block, key_heads, LEN, LEN), lambda i: (first + i, part, 0, 0))
    in_specs = [
        head_block,
        head_block,
        pl.BlockSpec((block,) + rates.shape[1:], lambda i: (first + i, 0, 0)),
    ]
    operands = [q, k, rates]
    aliases = {}
    if earlier is not None:
        in_specs += [pl.BlockSpec(memory_space=pl.ANY)] * 2
        aliases = {3: 0, 4: 1}
        operands += list(earlier)
    return pl.pallas_call(
        functools.partial(pair_kernel, part),
        grid=(turns,),
        in_specs=in_specs,
        out_specs=[
            pl.BlockSpec((block, heads, LEN, LEN), lambda i: (first + i, 0, 0, 0)),
            pl.BlockSpec((block, heads, 2 * LEN, 2 * LEN), lambda i: (first + i, 0, 0, 0)),
        ],
        out_shape=[
            jax.ShapeDtypeStruct((count, heads, LEN, LEN), BF16),
            jax.ShapeDtypeStruct((count, heads, 2 * LEN, 2 * LEN), BF16),
        ],
        input_output_aliases=aliases,
        compiler_params=pltpu.CompilerParams(vmem_limit_bytes=VMEM_LIMIT),
        cost_estimate=pl.CostEstimate(flops=1000, bytes_accessed=1000, transcendentals=0),
    )(*operands)


def state_kernel(
    part, home, shards_held, table, q_ref, k_ref, v_ref, rate_ref, inv_ref, am_ref, gain_ref, *refs
):
    parents = refs[:shards_held]
    mixed_ref, state_ref, buffer, arrivals = refs[-4:]
    turn, turns = pl.program_id(0), pl.num_programs(0)

    def fetch(i, slot):
        for off in range(shards_held):
            @pl.when(table[1, i] == off)
            def _():
                pltpu.make_async_copy(
                    parents[off].at[table[4, i]], buffer.at[slot], arrivals.at[slot]
                ).start()

    @pl.when(turn == 0)
    def _():
        fetch(0, 0)

    @pl.when(turn + 1 < turns)
    def _():
        fetch(turn + 1, (turn + 1) % 2)

    slot = turn % 2
    pltpu.make_async_copy(parents[0].at[0], buffer.at[slot], arrivals.at[slot]).wait()
    s_ref = buffer.at[pl.ds(slot, 1)]
    key_heads = q_ref.shape[1]
    heads = 2 * key_heads
    all_heads = rate_ref.shape[1] // 2
    live_count = table[2, pl.program_id(0)]
    row = iota((LEN, LEN), 0)
    col = iota((LEN, LEN), 1)
    lower_ones = (row >= col).astype(F32).astype(BF16)
    unit = (row == col).astype(F32).astype(BF16)
    rates = rate_ref[0].astype(BF16)
    cols = dot_nt(jnp.concatenate([lower_ones, unit], axis=0), rates)
    g_cols = cols[:LEN]
    b_cols = cols[LEN:]
    eg_cols = jnp.exp(g_cols)
    live = row < live_count
    gain = gain_ref[...].astype(F32)
    steps = load_steps(s_ref, heads)

    def decay_at(h):
        return eg_cols[:, part * heads + h:part * heads + h + 1]

    state, products, n_col = [], [], []
    for m in range(key_heads):
        highs, lows = [], []
        for r in range(2):
            h = 2 * m + r
            whole = decode(s_ref[0, h * HALF:(h + 1) * HALF, :])
            high, low = split(whole)
            highs.append(high)
            lows.append(low)
            state.append(whole)
        rhs = jnp.concatenate(
            [jnp.concatenate(highs, axis=1), jnp.concatenate(lows, axis=1)], axis=0
        )
        lhs = jnp.concatenate([q_ref[0, m], k_ref[0, m]], axis=0)
        products.append(dot(jnp.concatenate([lhs, lhs], axis=1), rhs))
        keys = k_ref[0, m].astype(F32)
        n_col.append(lax.rsqrt(jnp.sum(keys * keys, axis=1, keepdims=True) + EPS))

    every = range(heads)
    right, first = [], []
    for h in every:
        m, r = h // 2, h % 2
        at = all_heads + part * heads + h
        ks = products[m][LEN:, r * LEN:(r + 1) * LEN] * steps[h:h + 1, :]
        want = b_cols[:, at:at + 1] * (v_ref[0, m, r].astype(F32) - (decay_at(h) * n_col[m]) * ks)
        right.append(want)
        first.append(dot(inv_ref[0, h], want.astype(BF16)).astype(BF16))
    am_v = [dot(am_ref[0, h], jnp.concatenate([first[h], first[h]], axis=0)) for h in every]
    delta = [
        dot(inv_ref[0, h], (right[h] - first[h].astype(F32) - am_v[h][:LEN]).astype(BF16)) for h in every
    ]
    scaled_h, scaled_l = [], []
    for h in every:
        g_c = g_cols[:, part * heads + h:part * heads + h + 1]
        tail = jnp.exp(g_c[LEN - 1:LEN, :] - g_c) * n_col[h // 2]
        high, low = split(tail * (first[h].astype(F32) + delta[h]))
        scaled_h.append(high)
        scaled_l.append(low)
    finals = []
    for m in range(key_heads):
        turned = jnp.transpose(k_ref[0, m])
        rhs = jnp.concatenate(
            [
                jnp.concatenate(scaled_h[2 * m:2 * m + 2], axis=1),
                jnp.concatenate(scaled_l[2 * m:2 * m + 2], axis=1),
            ],
            axis=0,
        )
        added = dot(jnp.concatenate([turned, turned], axis=1), rhs)
        for r in range(2):
            h = 2 * m + r
            keep = decay_at(h)[LEN - 1:LEN, :] * steps[h:h + 1, :]
            finals.append(keep * state[h] + added[:, r * LEN:(r + 1) * LEN])
    for h in every:
        m, r = h // 2, h % 2
        qs = products[m][:LEN, r * LEN:(r + 1) * LEN] * steps[h:h + 1, :]
        out = decay_at(h) * qs + am_v[h][LEN:] + dot(am_ref[0, h, LEN:, :LEN], delta[h].astype(BF16))
        mean_square = jnp.mean(out * out, axis=1, keepdims=True)
        normed = out * lax.rsqrt(mean_square + EPS) * gain
        mixed_ref[0, m, r] = jnp.where(live, normed, 0.0).astype(BF16)
    if home:
        for h in every:
            state_ref[0, h] = finals[h]
    else:
        store_packed(state_ref, finals)


def recurrence(part, table, q, k, v, rates, pairs, parents, gain, mixed, final_shape=None, final=None):
    count = table.shape[1]
    key_heads = q.shape[1] // PARTS
    heads = 2 * key_heads
    rows = heads * HALF + CODE_ROWS
    in_specs = [
        pl.BlockSpec((1, key_heads, LEN, LEN), lambda i, t: (t[0, i], part, 0, 0)),
        pl.BlockSpec((1, key_heads, LEN, LEN), lambda i, t: (t[0, i], part, 0, 0)),
        pl.BlockSpec((1, key_heads, 2, LEN, LEN), lambda i, t: (t[0, i], part, 0, 0, 0)),
        pl.BlockSpec((1,) + rates.shape[1:], lambda i, t: (t[0, i], 0, 0)),
        pl.BlockSpec((1, heads, LEN, LEN), lambda i, t: (t[0, i], 0, 0, 0)),
        pl.BlockSpec((1, heads, 2 * LEN, 2 * LEN), lambda i, t: (t[0, i], 0, 0, 0)),
        pl.BlockSpec((1, LEN), lambda i, t: (0, 0)),
    ]
    in_specs += [pl.BlockSpec(memory_space=pl.ANY)] * len(parents)
    operands = [q, k, v, rates, *pairs, gain, *parents]
    aliases = {}
    if mixed is not None:
        in_specs.append(pl.BlockSpec(memory_space=pl.ANY))
        aliases[1 + len(operands)] = 0
        operands.append(mixed)
    mixed_spec = pl.BlockSpec((1, key_heads, 2, LEN, LEN), lambda i, t: (t[0, i], part, 0, 0, 0))
    mixed_shape = jax.ShapeDtypeStruct(v.shape, BF16)
    if final_shape is None:
        state_spec = pl.BlockSpec((1, rows, LEN), lambda i, t: (i, 0, 0))
        state_shape = jax.ShapeDtypeStruct((count, rows, LEN), jnp.int32)
    else:
        if final is not None:
            in_specs.append(pl.BlockSpec(memory_space=pl.ANY))
            aliases[1 + len(operands)] = 1
            operands.append(final)
        state_spec = pl.BlockSpec((1, heads, LEN, LEN), lambda i, t: (t[3, i], part, 0, 0))
        state_shape = jax.ShapeDtypeStruct(final_shape, F32)
    return pl.pallas_call(
        functools.partial(state_kernel, part, final_shape is not None, len(parents)),
        grid_spec=pltpu.PrefetchScalarGridSpec(
            num_scalar_prefetch=1,
            grid=(count,),
            in_specs=in_specs,
            out_specs=[mixed_spec, state_spec],
            scratch_shapes=[
                pltpu.VMEM((2, rows, LEN), jnp.int32),
                pltpu.SemaphoreType.DMA((2,)),
            ],
        ),
        out_shape=[mixed_shape, state_shape],
        input_output_aliases=aliases,
        compiler_params=pltpu.CompilerParams(vmem_limit_bytes=WIDE_VMEM_LIMIT),
        cost_estimate=pl.CostEstimate(flops=1000, bytes_accessed=1000, transcendentals=0),
    )(table, *operands)


def unpack_kernel(table, packed_ref, old_ref, out_ref):
    count, heads = out_ref.shape[:2]
    for e in range(count):
        steps = load_steps(packed_ref.at[pl.ds(e, 1)], heads)
        for h in range(heads):
            out_ref[e, h] = decode(packed_ref[e, h * HALF:(h + 1) * HALF, :]) * steps[h:h + 1, :]


def unpack_states(part, table, packed, final):
    count, rows = packed.shape[:2]
    heads = final.shape[1] // PARTS
    block = max(1, count // 2)
    turns = count // block
    return pl.pallas_call(
        unpack_kernel,
        grid_spec=pltpu.PrefetchScalarGridSpec(
            num_scalar_prefetch=1,
            grid=(turns,),
            in_specs=[
                pl.BlockSpec((block, rows, LEN), lambda i, t: (i, 0, 0)),
                pl.BlockSpec(memory_space=pl.ANY),
            ],
            out_specs=pl.BlockSpec((block, heads, LEN, LEN), lambda i, t: (t[0] * turns + i, part, 0, 0)),
        ),
        out_shape=jax.ShapeDtypeStruct(final.shape, F32),
        input_output_aliases={2: 0},
        compiler_params=pltpu.CompilerParams(vmem_limit_bytes=VMEM_LIMIT),
        cost_estimate=pl.CostEstimate(flops=1000, bytes_accessed=1000, transcendentals=0),
    )(table, packed, final)


def shards(
    queries,
    keys,
    values,
    log_decay,
    write_rate,
    norm_gain,
    parent_cache,
    order,
    parent_owner,
    parent_slot,
    token_count,
):
    seq_count = lax.axis_size("seq")
    me = lax.axis_index("seq")
    per_device, length, key_heads, key_dim = queries.shape
    per_peer = per_device // seq_count
    cache_rows = parent_cache.shape[0]
    heads = 2 * key_heads
    part_heads = heads // PARTS

    parents = parent_cache.reshape((cache_rows, heads, key_dim, key_dim))
    own = [pack_parents(parents, part, part_heads) for part in range(PARTS)]

    def swap(tensor, off):
        return lax.ppermute(tensor, "seq", [(i, i ^ off) for i in range(seq_count)])

    def spread(held, off, tie=False):
        while off:
            if tie:
                held = lax.optimization_barrier(held)
            held = {**held, **{at ^ off: swap(held[at], off) for at in held}}
            off //= 2
        return held

    half_way = seq_count // 2
    far = swap(own[0], half_way)
    q = jnp.transpose(queries, (0, 2, 1, 3))
    k = jnp.transpose(keys, (0, 2, 1, 3))
    v = jnp.transpose(values, (0, 2, 3, 1, 4))

    def rows_of(tensor):
        return jnp.transpose(tensor, (0, 2, 3, 1)).reshape(per_device, heads, length).astype(F32)

    here_count = lax.dynamic_slice_in_dim(token_count, me * per_device, per_device)
    alive = jnp.arange(length, dtype=jnp.int32) < here_count[:, None, None]
    rates = jnp.where(alive, jnp.concatenate([rows_of(log_decay), rows_of(write_rate)], axis=1), 0.0)
    gain = norm_gain.reshape(1, -1)
    pairs = [None, None]
    pairs[0] = pair_parts(0, 0, q, k, rates)
    pairs[0], v, far, own[1] = lax.optimization_barrier((pairs[0], v, far, own[1]))
    held_0 = spread({0: own[0], half_way: far}, half_way // 2)
    far_1 = swap(own[1], half_way)
    held_1 = spread({0: own[1], half_way: far_1}, half_way // 2, tie=True)
    gathered = [[held[at] for at in range(seq_count)] for held in (held_0, held_1)]
    pairs[0] = pair_parts(0, 1, q, k, rates, pairs[0])
    rates, pairs[0] = lax.optimization_barrier((rates, pairs[0]))
    pairs[1] = pair_parts(1, 0, q, k, rates)
    pairs[0], pairs[1] = lax.optimization_barrier((pairs[0], pairs[1]))

    slot_grid = order.reshape(seq_count, seq_count, per_peer)
    local_ids = lax.dynamic_index_in_dim(slot_grid, me, 1, keepdims=False) - me * per_device
    here_owner = lax.dynamic_slice_in_dim(parent_owner, me * per_device, per_device)
    here_slot = lax.dynamic_slice_in_dim(parent_slot, me * per_device, per_device)

    def look_up(vector, ids):
        hit = ids[..., None] == jnp.arange(per_device, dtype=jnp.int32)
        return jnp.sum(jnp.where(hit, vector, 0), axis=-1)

    slots = me * per_peer + jnp.broadcast_to(jnp.arange(per_peer, dtype=jnp.int32), local_ids.shape)
    tables = jnp.stack(
        [
            local_ids,
            jnp.bitwise_xor(look_up(here_owner, local_ids), me),
            look_up(here_count, local_ids),
            slots,
            look_up(here_slot, local_ids),
        ],
        axis=1,
    ).astype(jnp.int32)

    final_shape = (per_device, heads, key_dim, key_dim)
    mixed, final = None, None
    arrived = []
    turns = [(part, away) for part in range(PARTS) for away in reversed(range(1, seq_count))]
    turns += [(part, 0) for part in range(PARTS)]
    for part, away in turns:
        peer = jnp.bitwise_xor(me, away)
        table = lax.dynamic_index_in_dim(tables, peer, 0, keepdims=False)
        if part == 1 and away == seq_count - 1:
            rates, mixed, pairs[1] = lax.optimization_barrier((rates, mixed, pairs[1]))
            pairs[1] = pair_parts(1, 1, q, k, rates, pairs[1])
        if part and away:
            at = seq_count - 1 - away
            before, other_peer, sent = arrived[at]
            mixed, sent = lax.optimization_barrier((mixed, sent))
            arrived[at] = (before, other_peer, sent)
        common = (part, table, q, k, v, rates, pairs[part], gathered[part], gain, mixed)
        if away:
            mixed, packed = recurrence(*common)
            sent = swap(packed, away)
            arrived.append((part, peer, sent))
        else:
            mixed, final = recurrence(*common, final_shape, final)
    for part, peer, packed in arrived:
        table = peer.reshape(1)
        final = unpack_states(part, table, packed, final)
    mixed_out = jnp.transpose(mixed, (0, 3, 1, 2, 4))
    final_out = final.reshape((per_device, key_heads, 2, key_dim, key_dim))
    return (mixed_out, final_out)


def solution(mesh):
    placed = (
        P(("groups", "seq"), None, ("head", "sub"), None),
        P(("groups", "seq"), None, ("head", "sub"), None),
        P(("groups", "seq"), None, ("head", "sub"), None, None),
        P(("groups", "seq"), None, ("head", "sub"), None),
        P(("groups", "seq"), None, ("head", "sub"), None),
        P(),
        P(("groups", "seq"), ("head", "sub"), None, None, None),
        P("groups"),
        P("groups"),
        P("groups"),
        P("groups"),
    )
    return jax.shard_map(
        shards,
        mesh=mesh,
        in_specs=placed,
        out_specs=(
            P(("groups", "seq"), None, ("head", "sub"), None, None),
            P(("groups", "seq"), ("head", "sub"), None, None, None),
        ),
        check_vma=False,
    )
```

```python
import functools

import jax
import jax.numpy as jnp
from jax import lax
from jax.experimental import pallas as pl
from jax.experimental.pallas import tpu as pltpu
from jax.sharding import PartitionSpec as P

F32 = jnp.float32
BF16 = jnp.bfloat16
HALF = 64
LEN = 128
EPS = 1e-06
TOP = 32512.0
BIAS = 32768.0
CODE = 64.0
VMEM_LIMIT = 60 * 1024 * 1024
PARTS = 2
CODE_ROWS = 8
TOGETHER = 2


def dot(a, b):
    return jnp.dot(a, b, preferred_element_type=F32)


def dot_nt(a, b):
    return lax.dot_general(a, b, (((1,), (1,)), ((), ())), preferred_element_type=F32)


def split(x):
    high = x.astype(BF16)
    return high, (x - high.astype(F32)).astype(BF16)


def iota(shape, dim):
    return lax.broadcasted_iota(jnp.int32, shape, dim)


def step_of(code):
    return jnp.exp2(code * (1.0 / CODE)) * (1.0 / TOP)


def encode(x):
    peak = jnp.maximum(jnp.max(jnp.abs(x), axis=0, keepdims=True), 1e-30)
    code = jnp.ceil(jnp.log2(peak) * CODE) + 1.0
    inverse_step = 1.0 / step_of(code)
    whole = (x * inverse_step + (BIAS + 0.5)).astype(jnp.int32)
    words = jnp.bitwise_or(lax.shift_left(whole[:HALF], 16), whole[HALF:])
    return words, code


def decode(words):
    top = lax.shift_right_logical(words, 16)
    bottom = jnp.bitwise_and(words, 0xFFFF)
    return jnp.concatenate([top, bottom], axis=0).astype(F32) - BIAS


def code_tile(codes):
    row = iota((CODE_ROWS, LEN), 0)
    tile = jnp.zeros((CODE_ROWS, LEN), F32)
    for at, code in enumerate(codes):
        tile = jnp.where(row == at, code, tile)
    return tile.astype(jnp.int32)


def store_packed(ref, states):
    codes = []
    for h, state in enumerate(states):
        words, code = encode(state)
        ref[0, h * HALF:(h + 1) * HALF, :] = words
        codes.append(code)
    at = len(states) * HALF
    ref[0, at:at + CODE_ROWS, :] = code_tile(codes)


def load_steps(ref, heads):
    codes = ref[0, heads * HALF:heads * HALF + CODE_ROWS, :].astype(F32)
    return step_of(codes)


def pack_kernel(state_ref, out_ref):
    store_packed(out_ref, [state_ref[0, h] for h in range(state_ref.shape[1])])


def pack_parents(parents, part, heads):
    count = parents.shape[0]
    rows = heads * HALF + CODE_ROWS
    return pl.pallas_call(
        pack_kernel,
        grid=(count,),
        in_specs=[pl.BlockSpec((1, heads, LEN, LEN), lambda i: (i, part, 0, 0))],
        out_specs=pl.BlockSpec((1, rows, LEN), lambda i: (i, 0, 0)),
        out_shape=jax.ShapeDtypeStruct((count, rows, LEN), jnp.int32),
        compiler_params=pltpu.CompilerParams(vmem_limit_bytes=VMEM_LIMIT),
    )(parents)


def block_diag(x, mask):
    return jnp.where(mask, jnp.concatenate([x, x], axis=0), jnp.zeros((), x.dtype))


def pair_kernel(part, q_ref, k_ref, rate_ref, *refs):
    inv_ref, am_ref = refs[-2:]
    expansions, key_heads = q_ref.shape[:2]
    heads = 2 * key_heads
    all_heads = rate_ref.shape[1] // 2
    row = iota((LEN, LEN), 0)
    col = iota((LEN, LEN), 1)
    incl = row >= col
    strict = row > col
    diag_mask = row == col
    prow = iota((HALF, LEN), 0)
    plane = iota((HALF, LEN), 1)
    pcol = jnp.bitwise_and(plane, HALF - 1)
    left = plane < HALF
    bd_mask = (row < HALF) == (col < HALF)
    eye = (prow == pcol).astype(F32)

    def same(size):
        return (prow // size) == (pcol // size)

    base_mask = same(8)
    off_masks = [jnp.logical_and(same(2 * s), jnp.logical_not(same(s))) for s in (8, 16, 32)]
    lower_ones = incl.astype(F32).astype(BF16)
    unit = diag_mask.astype(F32).astype(BF16)

    a_full, where_at = [], []
    for e in range(expansions):
        rates = rate_ref[e].astype(BF16)
        cols = dot_nt(jnp.concatenate([lower_ones, unit], axis=0), rates)
        g_cols = cols[:LEN]
        b_cols = cols[LEN:]
        g_rows = dot_nt(rates, lower_ones)
        for m in range(key_heads):
            k = k_ref[e, m]
            gram = dot_nt(jnp.concatenate([q_ref[e, m], k], axis=0), k)
            qk, kk = gram[:LEN], gram[LEN:]
            diagonal = jnp.where(diag_mask, kk, 0.0)
            norm_row = lax.rsqrt(jnp.sum(diagonal, axis=0, keepdims=True) + EPS)
            norm_col = lax.rsqrt(jnp.sum(diagonal, axis=1, keepdims=True) + EPS)
            qk = qk * norm_row
            kk = kk * norm_row
            for r in range(2):
                h = 2 * m + r
                at = part * heads + h
                g_c = g_cols[:, at:at + 1]
                g_r = g_rows[at:at + 1, :]
                pair = jnp.exp(jnp.where(incl, g_c - g_r, -1e4))
                mix = qk * pair
                b_c = b_cols[:, all_heads + at:all_heads + at + 1]
                lower = jnp.where(strict, kk * pair, 0.0) * (b_c * norm_col)
                lower_h, lower_l = split(lower)
                mix_h, mix_l = split(mix)
                am_ref[e, h, :LEN, :LEN] = lower_h
                am_ref[e, h, :LEN, LEN:] = lower_l
                am_ref[e, h, LEN:, :LEN] = mix_h
                am_ref[e, h, LEN:, LEN:] = mix_l
                a_full.append(lower)
                where_at.append((e, h))

    chains = range(len(a_full))
    packed = [jnp.where(left, a_full[c][:HALF], a_full[c][HALF:]) for c in chains]
    base = [jnp.where(base_mask, packed[c], 0.0) for c in chains]
    base_h = [base[c].astype(BF16) for c in chains]
    power = [dot(base_h[c], block_diag(base_h[c], bd_mask)).astype(BF16) for c in chains]
    x = [eye - base[c] for c in chains]
    both = [
        dot(jnp.concatenate([x[c].astype(BF16), power[c]], axis=0), block_diag(power[c], bd_mask))
        for c in chains
    ]
    x = [x[c] + both[c][:HALF] for c in chains]
    power = [both[c][HALF:].astype(BF16) for c in chains]
    x = [x[c] + dot(x[c].astype(BF16), block_diag(power[c], bd_mask)) for c in chains]
    for off in off_masks:
        x_h = [x[c].astype(BF16) for c in chains]
        t = [
            dot(jnp.where(off, packed[c], 0.0).astype(BF16), block_diag(x_h[c], bd_mask)).astype(BF16)
            for c in chains
        ]
        x = [x[c] - dot(x_h[c], block_diag(t[c], bd_mask)) for c in chains]
    x_h = [x[c].astype(BF16) for c in chains]
    t = [
        dot(jnp.where(left, a_full[c][HALF:], 0.0).astype(BF16), block_diag(x_h[c], bd_mask)).astype(BF16)
        for c in chains
    ]
    zero_h = jnp.zeros((HALF, LEN), BF16)
    corner = [dot(jnp.where(left, zero_h, x_h[c]), jnp.concatenate([t[c], t[c]], axis=0)) for c in chains]
    for c in chains:
        e, h = where_at[c]
        inv_ref[e, h, :HALF, :] = jnp.where(left, x[c], 0.0).astype(BF16)
        inv_ref[e, h, HALF:, :] = jnp.where(left, -corner[c], x[c]).astype(BF16)


def pair_parts(part, half, q, k, rates, earlier=None):
    count, all_key_heads = q.shape[:2]
    key_heads = all_key_heads // PARTS
    heads = 2 * key_heads
    block = TOGETHER
    turns = count // block // 2
    first = half * turns
    head_block = pl.BlockSpec((block, key_heads, LEN, LEN), lambda i: (first + i, part, 0, 0))
    in_specs = [
        head_block,
        head_block,
        pl.BlockSpec((block,) + rates.shape[1:], lambda i: (first + i, 0, 0)),
    ]
    operands = [q, k, rates]
    aliases = {}
    if earlier is not None:
        in_specs += [pl.BlockSpec(memory_space=pl.ANY)] * 2
        aliases = {3: 0, 4: 1}
        operands += list(earlier)
    return pl.pallas_call(
        functools.partial(pair_kernel, part),
        grid=(turns,),
        in_specs=in_specs,
        out_specs=[
            pl.BlockSpec((block, heads, LEN, LEN), lambda i: (first + i, 0, 0, 0)),
            pl.BlockSpec((block, heads, 2 * LEN, 2 * LEN), lambda i: (first + i, 0, 0, 0)),
        ],
        out_shape=[
            jax.ShapeDtypeStruct((count, heads, LEN, LEN), BF16),
            jax.ShapeDtypeStruct((count, heads, 2 * LEN, 2 * LEN), BF16),
        ],
        input_output_aliases=aliases,
        compiler_params=pltpu.CompilerParams(vmem_limit_bytes=VMEM_LIMIT),
        cost_estimate=pl.CostEstimate(flops=1000, bytes_accessed=1000, transcendentals=0),
    )(*operands)


def state_kernel(part, home, shards_held, together, table, gain_ref, *refs):
    per = 6
    inputs = [refs[per * e:per * (e + 1)] for e in range(together)]
    parents = refs[per * together:per * together + shards_held]
    mixed_hbm, state_ref, states_in, mixed_out, arrivals, leaving = refs[-6:]
    turn, turns = pl.program_id(0), pl.num_programs(0)
    key_heads = inputs[0][0].shape[1]
    heads = 2 * key_heads
    all_heads = inputs[0][3].shape[1] // 2

    def fetch(i, slot):
        for e in range(together):
            for off in range(shards_held):
                @pl.when(table[1, i * together + e] == off)
                def _():
                    pltpu.make_async_copy(
                        parents[off].at[table[4, i * together + e]],
                        states_in.at[slot, e],
                        arrivals.at[slot, e],
                    ).start()

    def leave(i, slot, e):
        return pltpu.make_async_copy(
            mixed_out.at[slot, e],
            mixed_hbm.at[table[0, i * together + e], pl.ds(part * key_heads, key_heads)],
            leaving.at[slot, e],
        )

    slot = lax.rem(turn, 2)

    @pl.when(turn == 0)
    def _():
        fetch(0, 0)

    @pl.when(turn + 1 < turns)
    def _():
        fetch(turn + 1, lax.rem(turn + 1, 2))

    for e in range(together):
        pltpu.make_async_copy(parents[0].at[0], states_in.at[slot, e], arrivals.at[slot, e]).wait()

    @pl.when(turn >= 2)
    def _():
        for e in range(together):
            leave(turn - 2, slot, e).wait()

    row = iota((LEN, LEN), 0)
    col = iota((LEN, LEN), 1)
    lower_ones = (row >= col).astype(F32).astype(BF16)
    unit = (row == col).astype(F32).astype(BF16)
    gain = gain_ref[...].astype(F32)

    state, products, n_cols, g_cols, b_cols, eg_cols, steps = [], [], [], [], [], [], []
    for e in range(together):
        q_ref, k_ref, v_ref, rate_ref, inv_ref, am_ref = inputs[e]
        cols = dot_nt(jnp.concatenate([lower_ones, unit], axis=0), rate_ref[0].astype(BF16))
        g_cols.append(cols[:LEN])
        b_cols.append(cols[LEN:])
        eg_cols.append(jnp.exp(cols[:LEN]))
        steps.append(load_steps(states_in.at[slot, pl.ds(e, 1)], heads))
        for m in range(key_heads):
            highs, lows = [], []
            for r in range(2):
                h = 2 * m + r
                whole = decode(states_in[slot, e, h * HALF:(h + 1) * HALF, :])
                high, low = split(whole)
                highs.append(high)
                lows.append(low)
                state.append(whole)
            rhs = jnp.concatenate(
                [jnp.concatenate(highs, axis=1), jnp.concatenate(lows, axis=1)], axis=0
            )
            lhs = jnp.concatenate([q_ref[0, m], k_ref[0, m]], axis=0)
            products.append(dot(jnp.concatenate([lhs, lhs], axis=1), rhs))
            keys = k_ref[0, m].astype(F32)
            n_cols.append(lax.rsqrt(jnp.sum(keys * keys, axis=1, keepdims=True) + EPS))

    every = [(e, h) for e in range(together) for h in range(heads)]

    def at_of(h):
        return part * heads + h

    def decay_at(e, h):
        return eg_cols[e][:, at_of(h):at_of(h) + 1]

    def product_at(e, h):
        lane = (h % 2) * LEN
        return products[e * key_heads + h // 2][:, lane:lane + LEN]

    right, first = [], []
    for e, h in every:
        v_ref, inv_ref = inputs[e][2], inputs[e][4]
        ks = product_at(e, h)[LEN:] * steps[e][h:h + 1, :]
        rate = b_cols[e][:, all_heads + at_of(h):all_heads + at_of(h) + 1]
        scale = decay_at(e, h) * n_cols[e * key_heads + h // 2]
        want = rate * (v_ref[0, h // 2, h % 2].astype(F32) - scale * ks)
        right.append(want)
        first.append(dot(inv_ref[0, h], want.astype(BF16)).astype(BF16))
    am_v = [
        dot(inputs[e][5][0, h], jnp.concatenate([first[c], first[c]], axis=0))
        for c, (e, h) in enumerate(every)
    ]
    delta = [
        dot(inputs[e][4][0, h], (right[c] - first[c].astype(F32) - am_v[c][:LEN]).astype(BF16))
        for c, (e, h) in enumerate(every)
    ]
    scaled = []
    for c, (e, h) in enumerate(every):
        g_c = g_cols[e][:, at_of(h):at_of(h) + 1]
        tail = jnp.exp(g_c[LEN - 1:LEN, :] - g_c) * n_cols[e * key_heads + h // 2]
        scaled.append(split(tail * (first[c].astype(F32) + delta[c])))
    finals = []
    for e in range(together):
        for m in range(key_heads):
            turned = jnp.transpose(inputs[e][1][0, m])
            c = e * heads + 2 * m
            rhs = jnp.concatenate(
                [jnp.concatenate([scaled[c][p], scaled[c + 1][p]], axis=1) for p in range(2)], axis=0
            )
            added = dot(jnp.concatenate([turned, turned], axis=1), rhs)
            for r in range(2):
                h = 2 * m + r
                keep = decay_at(e, h)[LEN - 1:LEN, :] * steps[e][h:h + 1, :]
                finals.append(keep * state[c + r] + added[:, r * LEN:(r + 1) * LEN])
    for c, (e, h) in enumerate(every):
        qs = product_at(e, h)[:LEN] * steps[e][h:h + 1, :]
        out = decay_at(e, h) * qs + am_v[c][LEN:]
        out = out + dot(inputs[e][5][0, h, LEN:, :LEN], delta[c].astype(BF16))
        mean_square = jnp.mean(out * out, axis=1, keepdims=True)
        live = iota((LEN, 1), 0) < table[2, turn * together + e]
        scale = jnp.where(live, lax.rsqrt(mean_square + EPS), 0.0)
        mixed_out[slot, e, h // 2, h % 2] = (out * scale * gain).astype(BF16)
    for e in range(together):
        leave(turn, slot, e).start()
    for e in range(together):
        mine = finals[e * heads:(e + 1) * heads]
        if home:
            for h in range(heads):
                state_ref[e, h] = mine[h]
        else:
            store_packed(state_ref.at[pl.ds(e, 1)], mine)

    @pl.when(turn == turns - 1)
    def _():
        for e in range(together):
            leave(turn, slot, e).wait()

    @pl.when(jnp.logical_and(turn == turns - 1, turn >= 1))
    def _():
        for e in range(together):
            leave(turn - 1, 1 - slot, e).wait()


def recurrence(part, table, q, k, v, rates, pairs, parents, gain, mixed, final_shape=None, final=None):
    count = table.shape[1]
    together = min(TOGETHER, count)
    key_heads = q.shape[1] // PARTS
    heads = 2 * key_heads
    rows = heads * HALF + CODE_ROWS
    in_specs = [pl.BlockSpec((1, LEN), lambda i, t: (0, 0))]
    operands = [gain]

    def one(shape, e, at):
        def index(i, t):
            return (t[0, i * together + e], at) + (0,) * (len(shape) - 2)

        return pl.BlockSpec(shape, index)

    for e in range(together):
        in_specs += [
            one((1, key_heads, LEN, LEN), e, part),
            one((1, key_heads, LEN, LEN), e, part),
            one((1, key_heads, 2, LEN, LEN), e, part),
            one((1,) + rates.shape[1:], e, 0),
            one((1, heads, LEN, LEN), e, 0),
            one((1, heads, 2 * LEN, 2 * LEN), e, 0),
        ]
        operands += [q, k, v, rates, *pairs]
    in_specs += [pl.BlockSpec(memory_space=pl.ANY)] * len(parents)
    operands += parents
    aliases = {}
    if mixed is not None:
        in_specs.append(pl.BlockSpec(memory_space=pl.ANY))
        aliases[1 + len(operands)] = 0
        operands.append(mixed)
    mixed_spec = pl.BlockSpec(memory_space=pl.ANY)
    mixed_shape = jax.ShapeDtypeStruct(v.shape, BF16)
    if final_shape is None:
        state_spec = pl.BlockSpec((together, rows, LEN), lambda i, t: (i, 0, 0))
        state_shape = jax.ShapeDtypeStruct((count, rows, LEN), jnp.int32)
    else:
        if final is not None:
            in_specs.append(pl.BlockSpec(memory_space=pl.ANY))
            aliases[1 + len(operands)] = 1
            operands.append(final)
        state_spec = pl.BlockSpec((together, heads, LEN, LEN), lambda i, t: (t[3, i], part, 0, 0))
        state_shape = jax.ShapeDtypeStruct(final_shape, F32)
    return pl.pallas_call(
        functools.partial(state_kernel, part, final_shape is not None, len(parents), together),
        grid_spec=pltpu.PrefetchScalarGridSpec(
            num_scalar_prefetch=1,
            grid=(count // together,),
            in_specs=in_specs,
            out_specs=[mixed_spec, state_spec],
            scratch_shapes=[
                pltpu.VMEM((2, together, rows, LEN), jnp.int32),
                pltpu.VMEM((2, together, key_heads, 2, LEN, LEN), BF16),
                pltpu.SemaphoreType.DMA((2, together)),
                pltpu.SemaphoreType.DMA((2, together)),
            ],
        ),
        out_shape=[mixed_shape, state_shape],
        input_output_aliases=aliases,
        compiler_params=pltpu.CompilerParams(vmem_limit_bytes=VMEM_LIMIT),
        cost_estimate=pl.CostEstimate(flops=1000, bytes_accessed=1000, transcendentals=0),
    )(table, *operands)


def unpack_kernel(table, packed_ref, old_ref, out_ref):
    count, heads = out_ref.shape[:2]
    for e in range(count):
        steps = load_steps(packed_ref.at[pl.ds(e, 1)], heads)
        for h in range(heads):
            out_ref[e, h] = decode(packed_ref[e, h * HALF:(h + 1) * HALF, :]) * steps[h:h + 1, :]


def unpack_states(part, table, packed, final):
    count, rows = packed.shape[:2]
    heads = final.shape[1] // PARTS
    block = max(1, count // 2)
    turns = count // block
    return pl.pallas_call(
        unpack_kernel,
        grid_spec=pltpu.PrefetchScalarGridSpec(
            num_scalar_prefetch=1,
            grid=(turns,),
            in_specs=[
                pl.BlockSpec((block, rows, LEN), lambda i, t: (i, 0, 0)),
                pl.BlockSpec(memory_space=pl.ANY),
            ],
            out_specs=pl.BlockSpec((block, heads, LEN, LEN), lambda i, t: (t[0] * turns + i, part, 0, 0)),
        ),
        out_shape=jax.ShapeDtypeStruct(final.shape, F32),
        input_output_aliases={2: 0},
        compiler_params=pltpu.CompilerParams(vmem_limit_bytes=VMEM_LIMIT),
        cost_estimate=pl.CostEstimate(flops=1000, bytes_accessed=1000, transcendentals=0),
    )(table, packed, final)


def shards(
    queries,
    keys,
    values,
    log_decay,
    write_rate,
    norm_gain,
    parent_cache,
    order,
    parent_owner,
    parent_slot,
    token_count,
):
    seq_count = lax.axis_size("seq")
    me = lax.axis_index("seq")
    per_device, length, key_heads, key_dim = queries.shape
    per_peer = per_device // seq_count
    cache_rows = parent_cache.shape[0]
    heads = 2 * key_heads
    part_heads = heads // PARTS

    parents = parent_cache.reshape((cache_rows, heads, key_dim, key_dim))
    own = [pack_parents(parents, part, part_heads) for part in range(PARTS)]

    def swap(tensor, off):
        return lax.ppermute(tensor, "seq", [(i, i ^ off) for i in range(seq_count)])

    def spread(held, off):
        while off:
            held = {**held, **{at ^ off: swap(held[at], off) for at in held}}
            off //= 2
        return held

    half_way = seq_count // 2
    far = swap(own[0], half_way)
    q = jnp.transpose(queries, (0, 2, 1, 3))
    k = jnp.transpose(keys, (0, 2, 1, 3))
    v = jnp.transpose(values, (0, 2, 3, 1, 4))

    def rows_of(tensor):
        return jnp.transpose(tensor, (0, 2, 3, 1)).reshape(per_device, heads, length).astype(F32)

    here_count = lax.dynamic_slice_in_dim(token_count, me * per_device, per_device)
    alive = jnp.arange(length, dtype=jnp.int32) < here_count[:, None, None]
    rates = jnp.where(alive, jnp.concatenate([rows_of(log_decay), rows_of(write_rate)], axis=1), 0.0)
    gain = norm_gain.reshape(1, -1)
    pairs = [None, None]
    own[0], q = lax.optimization_barrier((own[0], q))
    pairs[0] = pair_parts(0, 0, q, k, rates)
    pairs[0], v, far, own[1] = lax.optimization_barrier((pairs[0], v, far, own[1]))
    held_0 = spread({0: own[0], half_way: far}, half_way // 2)
    far_1 = swap(own[1], half_way)
    pairs[0] = pair_parts(0, 1, q, k, rates, pairs[0])
    rates, pairs[0] = lax.optimization_barrier((rates, pairs[0]))
    pairs[1] = pair_parts(1, 0, q, k, rates)
    pairs, held_0, far_1, own = lax.optimization_barrier((pairs, held_0, far_1, own))
    held_1 = spread({0: own[1], half_way: far_1}, half_way // 2)
    gathered = [[held[at] for at in range(seq_count)] for held in (held_0, held_1)]

    slot_grid = order.reshape(seq_count, seq_count, per_peer)
    local_ids = lax.dynamic_index_in_dim(slot_grid, me, 1, keepdims=False) - me * per_device
    here_owner = lax.dynamic_slice_in_dim(parent_owner, me * per_device, per_device)
    here_slot = lax.dynamic_slice_in_dim(parent_slot, me * per_device, per_device)

    def look_up(vector, ids):
        hit = ids[..., None] == jnp.arange(per_device, dtype=jnp.int32)
        return jnp.sum(jnp.where(hit, vector, 0), axis=-1)

    block = me * (per_peer // min(TOGETHER, per_peer))
    slots = block + jnp.broadcast_to(jnp.arange(per_peer, dtype=jnp.int32), local_ids.shape)
    tables = jnp.stack(
        [
            local_ids,
            jnp.bitwise_xor(look_up(here_owner, local_ids), me),
            look_up(here_count, local_ids),
            slots,
            look_up(here_slot, local_ids),
        ],
        axis=1,
    ).astype(jnp.int32)

    final_shape = (per_device, heads, key_dim, key_dim)
    mixed, final = None, None
    arrived = []
    crossing = list(reversed(range(half_way, seq_count)))
    near = list(reversed(range(1, half_way)))
    turns = [(part, away) for part in range(PARTS) for away in crossing + near]
    turns += [(part, 0) for part in range(PARTS)]
    for part, away in turns:
        peer = jnp.bitwise_xor(me, away)
        table = lax.dynamic_index_in_dim(tables, peer, 0, keepdims=False)
        if part == 0 and away == near[0]:
            rates, mixed, pairs[1] = lax.optimization_barrier((rates, mixed, pairs[1]))
            pairs[1] = pair_parts(1, 1, q, k, rates, pairs[1])
            mixed, pairs[1], gathered[1] = lax.optimization_barrier((mixed, pairs[1], gathered[1]))
        common = (part, table, q, k, v, rates, pairs[part], gathered[part], gain, mixed)
        if away:
            mixed, packed = recurrence(*common)
            sent = swap(packed, away)
            arrived.append((part, peer, sent))
        else:
            mixed, final = recurrence(*common, final_shape, final)
    for part, peer, packed in arrived:
        table = peer.reshape(1)
        final = unpack_states(part, table, packed, final)
    mixed_out = jnp.transpose(mixed, (0, 3, 1, 2, 4))
    final_out = final.reshape((per_device, key_heads, 2, key_dim, key_dim))
    return (mixed_out, final_out)


def solution(mesh):
    placed = (
        P(("groups", "seq"), None, ("head", "sub"), None),
        P(("groups", "seq"), None, ("head", "sub"), None),
        P(("groups", "seq"), None, ("head", "sub"), None, None),
        P(("groups", "seq"), None, ("head", "sub"), None),
        P(("groups", "seq"), None, ("head", "sub"), None),
        P(),
        P(("groups", "seq"), ("head", "sub"), None, None, None),
        P("groups"),
        P("groups"),
        P("groups"),
        P("groups"),
    )
    return jax.shard_map(
        shards,
        mesh=mesh,
        in_specs=placed,
        out_specs=(
            P(("groups", "seq"), None, ("head", "sub"), None, None),
            P(("groups", "seq"), ("head", "sub"), None, None, None),
        ),
        check_vma=False,
    )
```

```python
import functools

import jax
import jax.numpy as jnp
from jax import lax
from jax.experimental import pallas as pl
from jax.experimental.pallas import tpu as pltpu
from jax.sharding import PartitionSpec as P

F32 = jnp.float32
BF16 = jnp.bfloat16
HALF = 64
LEN = 128
EPS = 1e-06
TOP = 32512.0
BIAS = 32768.0
CODE = 64.0
VMEM_LIMIT = 12 * 1024 * 1024
PARTS = 2
CODE_ROWS = 8
TOGETHER = 2


def dot(a, b):
    return jnp.dot(a, b, preferred_element_type=F32)


def dot_nt(a, b):
    return lax.dot_general(a, b, (((1,), (1,)), ((), ())), preferred_element_type=F32)


def split(x):
    high = x.astype(BF16)
    return high, (x - high.astype(F32)).astype(BF16)


def iota(shape, dim):
    return lax.broadcasted_iota(jnp.int32, shape, dim)


def step_of(code):
    return jnp.exp2(code * (1.0 / CODE)) * (1.0 / TOP)


def encode(x):
    peak = jnp.maximum(jnp.max(jnp.abs(x), axis=0, keepdims=True), 1e-30)
    code = jnp.ceil(jnp.log2(peak) * CODE) + 1.0
    inverse_step = 1.0 / step_of(code)
    whole = (x * inverse_step + (BIAS + 0.5)).astype(jnp.int32)
    words = jnp.bitwise_or(lax.shift_left(whole[:HALF], 16), whole[HALF:])
    return words, code


def decode(words):
    top = lax.shift_right_logical(words, 16)
    bottom = jnp.bitwise_and(words, 0xFFFF)
    return jnp.concatenate([top, bottom], axis=0).astype(F32) - BIAS


def code_tile(codes):
    row = iota((CODE_ROWS, LEN), 0)
    tile = jnp.zeros((CODE_ROWS, LEN), F32)
    for at, code in enumerate(codes):
        tile = jnp.where(row == at, code, tile)
    return tile.astype(jnp.int32)


def store_packed(ref, states):
    codes = []
    for h, state in enumerate(states):
        words, code = encode(state)
        ref[0, h * HALF:(h + 1) * HALF, :] = words
        codes.append(code)
    at = len(states) * HALF
    ref[0, at:at + CODE_ROWS, :] = code_tile(codes)


def load_steps(ref, heads):
    codes = ref[0, heads * HALF:heads * HALF + CODE_ROWS, :].astype(F32)
    return step_of(codes)


def pack_kernel(state_ref, *out_refs):
    heads = state_ref.shape[1] // len(out_refs)
    for part, out_ref in enumerate(out_refs):
        store_packed(out_ref, [state_ref[0, part * heads + h] for h in range(heads)])


def pack_parents(parents):
    count, heads = parents.shape[:2]
    rows = heads // PARTS * HALF + CODE_ROWS
    return pl.pallas_call(
        pack_kernel,
        grid=(count,),
        in_specs=[pl.BlockSpec((1, heads, LEN, LEN), lambda i: (i, 0, 0, 0))],
        out_specs=[pl.BlockSpec((1, rows, LEN), lambda i: (i, 0, 0))] * PARTS,
        out_shape=[jax.ShapeDtypeStruct((count, rows, LEN), jnp.int32)] * PARTS,
        compiler_params=pltpu.CompilerParams(vmem_limit_bytes=VMEM_LIMIT),
    )(parents)


def block_diag(x, mask):
    return jnp.where(mask, jnp.concatenate([x, x], axis=0), jnp.zeros((), x.dtype))


def pair_kernel(part, q_ref, k_ref, rate_ref, *refs):
    inv_ref, am_ref = refs[-2:]
    expansions, key_heads = q_ref.shape[:2]
    heads = 2 * key_heads
    all_heads = rate_ref.shape[1] // 2
    row = iota((LEN, LEN), 0)
    col = iota((LEN, LEN), 1)
    incl = row >= col
    strict = row > col
    diag_mask = row == col
    prow = iota((HALF, LEN), 0)
    plane = iota((HALF, LEN), 1)
    pcol = jnp.bitwise_and(plane, HALF - 1)
    left = plane < HALF
    bd_mask = (row < HALF) == (col < HALF)
    eye = (prow == pcol).astype(F32)

    def same(size):
        return (prow // size) == (pcol // size)

    base_mask = same(8)
    off_masks = [jnp.logical_and(same(2 * s), jnp.logical_not(same(s))) for s in (8, 16, 32)]
    lower_ones = incl.astype(F32).astype(BF16)
    unit = diag_mask.astype(F32).astype(BF16)

    a_full, where_at = [], []
    for e in range(expansions):
        rates = rate_ref[e].astype(BF16)
        cols = dot_nt(jnp.concatenate([lower_ones, unit], axis=0), rates)
        g_cols = cols[:LEN]
        b_cols = cols[LEN:]
        g_rows = dot_nt(rates, lower_ones)
        for m in range(key_heads):
            k = k_ref[e, m]
            gram = dot_nt(jnp.concatenate([q_ref[e, m], k], axis=0), k)
            qk, kk = gram[:LEN], gram[LEN:]
            diagonal = jnp.where(diag_mask, kk, 0.0)
            norm_row = lax.rsqrt(jnp.sum(diagonal, axis=0, keepdims=True) + EPS)
            norm_col = lax.rsqrt(jnp.sum(diagonal, axis=1, keepdims=True) + EPS)
            qk = qk * norm_row
            kk = kk * norm_row
            for r in range(2):
                h = 2 * m + r
                at = part * heads + h
                g_c = g_cols[:, at:at + 1]
                g_r = g_rows[at:at + 1, :]
                pair = jnp.exp(jnp.where(incl, g_c - g_r, -1e4))
                mix = qk * pair
                b_c = b_cols[:, all_heads + at:all_heads + at + 1]
                lower = jnp.where(strict, kk * pair, 0.0) * (b_c * norm_col)
                lower_h, lower_l = split(lower)
                mix_h, mix_l = split(mix)
                am_ref[e, h, :LEN, :LEN] = lower_h
                am_ref[e, h, :LEN, LEN:] = lower_l
                am_ref[e, h, LEN:, :LEN] = mix_h
                am_ref[e, h, LEN:, LEN:] = mix_l
                a_full.append(lower)
                where_at.append((e, h))

    chains = range(len(a_full))
    packed = [jnp.where(left, a_full[c][:HALF], a_full[c][HALF:]) for c in chains]
    base = [jnp.where(base_mask, packed[c], 0.0) for c in chains]
    base_h = [base[c].astype(BF16) for c in chains]
    power = [dot(base_h[c], block_diag(base_h[c], bd_mask)).astype(BF16) for c in chains]
    x = [eye - base[c] for c in chains]
    both = [
        dot(jnp.concatenate([x[c].astype(BF16), power[c]], axis=0), block_diag(power[c], bd_mask))
        for c in chains
    ]
    x = [x[c] + both[c][:HALF] for c in chains]
    power = [both[c][HALF:].astype(BF16) for c in chains]
    x = [x[c] + dot(x[c].astype(BF16), block_diag(power[c], bd_mask)) for c in chains]
    for off in off_masks:
        x_h = [x[c].astype(BF16) for c in chains]
        t = [
            dot(jnp.where(off, packed[c], 0.0).astype(BF16), block_diag(x_h[c], bd_mask)).astype(BF16)
            for c in chains
        ]
        x = [x[c] - dot(x_h[c], block_diag(t[c], bd_mask)) for c in chains]
    x_h = [x[c].astype(BF16) for c in chains]
    t = [
        dot(jnp.where(left, a_full[c][HALF:], 0.0).astype(BF16), block_diag(x_h[c], bd_mask)).astype(BF16)
        for c in chains
    ]
    zero_h = jnp.zeros((HALF, LEN), BF16)
    corner = [dot(jnp.where(left, zero_h, x_h[c]), jnp.concatenate([t[c], t[c]], axis=0)) for c in chains]
    for c in chains:
        e, h = where_at[c]
        inv_ref[e, h, :HALF, :] = jnp.where(left, x[c], 0.0).astype(BF16)
        inv_ref[e, h, HALF:, :] = jnp.where(left, -corner[c], x[c]).astype(BF16)


def pair_parts(part, half, q, k, rates, earlier=None):
    count, all_key_heads = q.shape[:2]
    key_heads = all_key_heads // PARTS
    heads = 2 * key_heads
    block = TOGETHER
    turns = count // block // 2
    first = half * turns
    head_block = pl.BlockSpec((block, key_heads, LEN, LEN), lambda i: (first + i, part, 0, 0))
    in_specs = [
        head_block,
        head_block,
        pl.BlockSpec((block,) + rates.shape[1:], lambda i: (first + i, 0, 0)),
    ]
    operands = [q, k, rates]
    aliases = {}
    if earlier is not None:
        in_specs += [pl.BlockSpec(memory_space=pl.ANY)] * 2
        aliases = {3: 0, 4: 1}
        operands += list(earlier)
    return pl.pallas_call(
        functools.partial(pair_kernel, part),
        grid=(turns,),
        in_specs=in_specs,
        out_specs=[
            pl.BlockSpec((block, heads, LEN, LEN), lambda i: (first + i, 0, 0, 0)),
            pl.BlockSpec((block, heads, 2 * LEN, 2 * LEN), lambda i: (first + i, 0, 0, 0)),
        ],
        out_shape=[
            jax.ShapeDtypeStruct((count, heads, LEN, LEN), BF16),
            jax.ShapeDtypeStruct((count, heads, 2 * LEN, 2 * LEN), BF16),
        ],
        input_output_aliases=aliases,
        compiler_params=pltpu.CompilerParams(vmem_limit_bytes=VMEM_LIMIT),
        cost_estimate=pl.CostEstimate(flops=1000, bytes_accessed=1000, transcendentals=0),
    )(*operands)


def state_kernel(part, home, shards_held, together, table, gain_ref, *refs):
    per = 6
    inputs = [refs[per * e:per * (e + 1)] for e in range(together)]
    parents = refs[per * together:per * together + shards_held]
    mixed_hbm, state_ref, states_in, mixed_out, arrivals, leaving = refs[-6:]
    turn, turns = pl.program_id(0), pl.num_programs(0)
    key_heads = inputs[0][0].shape[1]
    heads = 2 * key_heads
    all_heads = inputs[0][3].shape[1] // 2

    def fetch(i, slot):
        for e in range(together):
            for off in range(shards_held):
                @pl.when(table[1, i * together + e] == off)
                def _():
                    pltpu.make_async_copy(
                        parents[off].at[table[4, i * together + e]],
                        states_in.at[slot, e],
                        arrivals.at[slot, e],
                    ).start()

    def leave(i, slot, e):
        return pltpu.make_async_copy(
            mixed_out.at[slot, e],
            mixed_hbm.at[table[0, i * together + e], pl.ds(part * key_heads, key_heads)],
            leaving.at[slot, e],
        )

    slot = lax.rem(turn, 2)

    @pl.when(turn == 0)
    def _():
        fetch(0, 0)

    @pl.when(turn + 1 < turns)
    def _():
        fetch(turn + 1, lax.rem(turn + 1, 2))

    for e in range(together):
        pltpu.make_async_copy(parents[0].at[0], states_in.at[slot, e], arrivals.at[slot, e]).wait()

    @pl.when(turn >= 2)
    def _():
        for e in range(together):
            leave(turn - 2, slot, e).wait()

    row = iota((LEN, LEN), 0)
    col = iota((LEN, LEN), 1)
    lower_ones = (row >= col).astype(F32).astype(BF16)
    unit = (row == col).astype(F32).astype(BF16)
    gain = gain_ref[...].astype(F32)

    state, products, n_cols, g_cols, b_cols, eg_cols, steps = [], [], [], [], [], [], []
    for e in range(together):
        q_ref, k_ref, v_ref, rate_ref, inv_ref, am_ref = inputs[e]
        cols = dot_nt(jnp.concatenate([lower_ones, unit], axis=0), rate_ref[0].astype(BF16))
        g_cols.append(cols[:LEN])
        b_cols.append(cols[LEN:])
        eg_cols.append(jnp.exp(cols[:LEN]))
        steps.append(load_steps(states_in.at[slot, pl.ds(e, 1)], heads))
        for m in range(key_heads):
            highs, lows = [], []
            for r in range(2):
                h = 2 * m + r
                whole = decode(states_in[slot, e, h * HALF:(h + 1) * HALF, :])
                high, low = split(whole)
                highs.append(high)
                lows.append(low)
                state.append(whole)
            rhs = jnp.concatenate(
                [jnp.concatenate(highs, axis=1), jnp.concatenate(lows, axis=1)], axis=0
            )
            lhs = jnp.concatenate([q_ref[0, m], k_ref[0, m]], axis=0)
            products.append(dot(jnp.concatenate([lhs, lhs], axis=1), rhs))
            keys = k_ref[0, m].astype(F32)
            n_cols.append(lax.rsqrt(jnp.sum(keys * keys, axis=1, keepdims=True) + EPS))

    every = [(e, h) for e in range(together) for h in range(heads)]

    def at_of(h):
        return part * heads + h

    def decay_at(e, h):
        return eg_cols[e][:, at_of(h):at_of(h) + 1]

    def product_at(e, h):
        lane = (h % 2) * LEN
        return products[e * key_heads + h // 2][:, lane:lane + LEN]

    right, first = [], []
    for e, h in every:
        v_ref, inv_ref = inputs[e][2], inputs[e][4]
        ks = product_at(e, h)[LEN:] * steps[e][h:h + 1, :]
        rate = b_cols[e][:, all_heads + at_of(h):all_heads + at_of(h) + 1]
        scale = decay_at(e, h) * n_cols[e * key_heads + h // 2]
        want = rate * (v_ref[0, h // 2, h % 2].astype(F32) - scale * ks)
        right.append(want)
        first.append(dot(inv_ref[0, h], want.astype(BF16)).astype(BF16))
    am_v = [
        dot(inputs[e][5][0, h], jnp.concatenate([first[c], first[c]], axis=0))
        for c, (e, h) in enumerate(every)
    ]
    delta = [
        dot(inputs[e][4][0, h], (right[c] - first[c].astype(F32) - am_v[c][:LEN]).astype(BF16))
        for c, (e, h) in enumerate(every)
    ]
    scaled = []
    for c, (e, h) in enumerate(every):
        g_c = g_cols[e][:, at_of(h):at_of(h) + 1]
        tail = jnp.exp(g_c[LEN - 1:LEN, :] - g_c) * n_cols[e * key_heads + h // 2]
        scaled.append(split(tail * (first[c].astype(F32) + delta[c])))
    finals = []
    for e in range(together):
        for m in range(key_heads):
            turned = jnp.transpose(inputs[e][1][0, m])
            c = e * heads + 2 * m
            rhs = jnp.concatenate(
                [jnp.concatenate([scaled[c][p], scaled[c + 1][p]], axis=1) for p in range(2)], axis=0
            )
            added = dot(jnp.concatenate([turned, turned], axis=1), rhs)
            for r in range(2):
                h = 2 * m + r
                keep = decay_at(e, h)[LEN - 1:LEN, :] * steps[e][h:h + 1, :]
                finals.append(keep * state[c + r] + added[:, r * LEN:(r + 1) * LEN])
    for c, (e, h) in enumerate(every):
        qs = product_at(e, h)[:LEN] * steps[e][h:h + 1, :]
        out = decay_at(e, h) * qs + am_v[c][LEN:]
        out = out + dot(inputs[e][5][0, h, LEN:, :LEN], delta[c].astype(BF16))
        mean_square = jnp.mean(out * out, axis=1, keepdims=True)
        live = iota((LEN, 1), 0) < table[2, turn * together + e]
        scale = jnp.where(live, lax.rsqrt(mean_square + EPS), 0.0)
        mixed_out[slot, e, h // 2, h % 2] = (out * scale * gain).astype(BF16)
    for e in range(together):
        leave(turn, slot, e).start()
    for e in range(together):
        mine = finals[e * heads:(e + 1) * heads]
        if home:
            for h in range(heads):
                state_ref[e, h] = mine[h]
        else:
            store_packed(state_ref.at[pl.ds(e, 1)], mine)

    @pl.when(turn == turns - 1)
    def _():
        for e in range(together):
            leave(turn, slot, e).wait()

    @pl.when(jnp.logical_and(turn == turns - 1, turn >= 1))
    def _():
        for e in range(together):
            leave(turn - 1, 1 - slot, e).wait()


def recurrence(part, table, q, k, v, rates, pairs, parents, gain, mixed, final_shape=None, final=None):
    count = table.shape[1]
    together = min(TOGETHER, count)
    key_heads = q.shape[1] // PARTS
    heads = 2 * key_heads
    rows = heads * HALF + CODE_ROWS
    in_specs = [pl.BlockSpec((1, LEN), lambda i, t: (0, 0))]
    operands = [gain]

    def one(shape, e, at):
        def index(i, t):
            return (t[0, i * together + e], at) + (0,) * (len(shape) - 2)

        return pl.BlockSpec(shape, index)

    for e in range(together):
        in_specs += [
            one((1, key_heads, LEN, LEN), e, part),
            one((1, key_heads, LEN, LEN), e, part),
            one((1, key_heads, 2, LEN, LEN), e, part),
            one((1,) + rates.shape[1:], e, 0),
            one((1, heads, LEN, LEN), e, 0),
            one((1, heads, 2 * LEN, 2 * LEN), e, 0),
        ]
        operands += [q, k, v, rates, *pairs]
    in_specs += [pl.BlockSpec(memory_space=pl.ANY)] * len(parents)
    operands += parents
    aliases = {}
    if mixed is not None:
        in_specs.append(pl.BlockSpec(memory_space=pl.ANY))
        aliases[1 + len(operands)] = 0
        operands.append(mixed)
    mixed_spec = pl.BlockSpec(memory_space=pl.ANY)
    mixed_shape = jax.ShapeDtypeStruct(v.shape, BF16)
    if final_shape is None:
        state_spec = pl.BlockSpec((together, rows, LEN), lambda i, t: (i, 0, 0))
        state_shape = jax.ShapeDtypeStruct((count, rows, LEN), jnp.int32)
    else:
        if final is not None:
            in_specs.append(pl.BlockSpec(memory_space=pl.ANY))
            aliases[1 + len(operands)] = 1
            operands.append(final)
        state_spec = pl.BlockSpec((together, heads, LEN, LEN), lambda i, t: (t[3, i], part, 0, 0))
        state_shape = jax.ShapeDtypeStruct(final_shape, F32)
    return pl.pallas_call(
        functools.partial(state_kernel, part, final_shape is not None, len(parents), together),
        grid_spec=pltpu.PrefetchScalarGridSpec(
            num_scalar_prefetch=1,
            grid=(count // together,),
            in_specs=in_specs,
            out_specs=[mixed_spec, state_spec],
            scratch_shapes=[
                pltpu.VMEM((2, together, rows, LEN), jnp.int32),
                pltpu.VMEM((2, together, key_heads, 2, LEN, LEN), BF16),
                pltpu.SemaphoreType.DMA((2, together)),
                pltpu.SemaphoreType.DMA((2, together)),
            ],
        ),
        out_shape=[mixed_shape, state_shape],
        input_output_aliases=aliases,
        compiler_params=pltpu.CompilerParams(vmem_limit_bytes=VMEM_LIMIT),
        cost_estimate=pl.CostEstimate(flops=1000, bytes_accessed=1000, transcendentals=0),
    )(table, *operands)


def unpack_kernel(table, packed_ref, old_ref, out_ref):
    count, heads = out_ref.shape[:2]
    for e in range(count):
        steps = load_steps(packed_ref.at[pl.ds(e, 1)], heads)
        for h in range(heads):
            out_ref[e, h] = decode(packed_ref[e, h * HALF:(h + 1) * HALF, :]) * steps[h:h + 1, :]


def unpack_states(part, table, packed, final):
    count, rows = packed.shape[:2]
    heads = final.shape[1] // PARTS
    block = max(1, count // 2)
    turns = count // block
    return pl.pallas_call(
        unpack_kernel,
        grid_spec=pltpu.PrefetchScalarGridSpec(
            num_scalar_prefetch=1,
            grid=(turns,),
            in_specs=[
                pl.BlockSpec((block, rows, LEN), lambda i, t: (i, 0, 0)),
                pl.BlockSpec(memory_space=pl.ANY),
            ],
            out_specs=pl.BlockSpec((block, heads, LEN, LEN), lambda i, t: (t[0] * turns + i, part, 0, 0)),
        ),
        out_shape=jax.ShapeDtypeStruct(final.shape, F32),
        input_output_aliases={2: 0},
        compiler_params=pltpu.CompilerParams(vmem_limit_bytes=VMEM_LIMIT),
        cost_estimate=pl.CostEstimate(flops=1000, bytes_accessed=1000, transcendentals=0),
    )(table, packed, final)


def shards(
    queries,
    keys,
    values,
    log_decay,
    write_rate,
    norm_gain,
    parent_cache,
    order,
    parent_owner,
    parent_slot,
    token_count,
):
    seq_count = lax.axis_size("seq")
    me = lax.axis_index("seq")
    per_device, length, key_heads, key_dim = queries.shape
    per_peer = per_device // seq_count
    cache_rows = parent_cache.shape[0]
    heads = 2 * key_heads

    parents = parent_cache.reshape((cache_rows, heads, key_dim, key_dim))
    own = list(pack_parents(parents))

    def swap(tensor, off):
        return lax.ppermute(tensor, "seq", [(i, i ^ off) for i in range(seq_count)])

    def spread(held, off):
        while off:
            held = {**held, **{at ^ off: swap(held[at], off) for at in held}}
            off //= 2
        return held

    half_way = seq_count // 2
    far = swap(own[0], half_way)
    q = jnp.transpose(queries, (0, 2, 1, 3))
    k = jnp.transpose(keys, (0, 2, 1, 3))
    v = jnp.transpose(values, (0, 2, 3, 1, 4))

    def rows_of(tensor):
        return jnp.transpose(tensor, (0, 2, 3, 1)).reshape(per_device, heads, length).astype(F32)

    here_count = lax.dynamic_slice_in_dim(token_count, me * per_device, per_device)
    alive = jnp.arange(length, dtype=jnp.int32) < here_count[:, None, None]
    rates = jnp.where(alive, jnp.concatenate([rows_of(log_decay), rows_of(write_rate)], axis=1), 0.0)
    gain = norm_gain.reshape(1, -1)
    pairs = [None, None]
    own[0], q = lax.optimization_barrier((own[0], q))
    pairs[0] = pair_parts(0, 0, q, k, rates)
    pairs[0], v, far, own[1] = lax.optimization_barrier((pairs[0], v, far, own[1]))
    held_0 = spread({0: own[0], half_way: far}, half_way // 2)
    far_1 = swap(own[1], half_way)
    pairs[0] = pair_parts(0, 1, q, k, rates, pairs[0])
    pairs[0], held_0, far_1, own, v = lax.optimization_barrier((pairs[0], held_0, far_1, own, v))
    held_1 = spread({0: own[1], half_way: far_1}, half_way // 2)
    gathered = [[held[at] for at in range(seq_count)] for held in (held_0, held_1)]

    slot_grid = order.reshape(seq_count, seq_count, per_peer)
    local_ids = lax.dynamic_index_in_dim(slot_grid, me, 1, keepdims=False) - me * per_device
    here_owner = lax.dynamic_slice_in_dim(parent_owner, me * per_device, per_device)
    here_slot = lax.dynamic_slice_in_dim(parent_slot, me * per_device, per_device)

    def look_up(vector, ids):
        hit = ids[..., None] == jnp.arange(per_device, dtype=jnp.int32)
        return jnp.sum(jnp.where(hit, vector, 0), axis=-1)

    block = me * (per_peer // min(TOGETHER, per_peer))
    slots = block + jnp.broadcast_to(jnp.arange(per_peer, dtype=jnp.int32), local_ids.shape)
    tables = jnp.stack(
        [
            local_ids,
            jnp.bitwise_xor(look_up(here_owner, local_ids), me),
            look_up(here_count, local_ids),
            slots,
            look_up(here_slot, local_ids),
        ],
        axis=1,
    ).astype(jnp.int32)

    final_shape = (per_device, heads, key_dim, key_dim)
    mixed, final = None, None
    arrived = []
    crossing = list(reversed(range(half_way, seq_count)))
    near = list(reversed(range(1, half_way)))
    turns = [(part, away) for part in range(PARTS) for away in crossing + near]
    turns += [(part, 0) for part in range(PARTS)]
    for part, away in turns:
        peer = jnp.bitwise_xor(me, away)
        table = lax.dynamic_index_in_dim(tables, peer, 0, keepdims=False)
        if part == 0 and away == near[0]:
            rates, mixed = lax.optimization_barrier((rates, mixed))
            pairs[1] = pair_parts(1, 0, q, k, rates)
            pairs[1] = pair_parts(1, 1, q, k, rates, pairs[1])
            mixed, pairs[1], gathered[1] = lax.optimization_barrier((mixed, pairs[1], gathered[1]))
        common = (part, table, q, k, v, rates, pairs[part], gathered[part], gain, mixed)
        if away:
            mixed, packed = recurrence(*common)
            sent = swap(packed, away)
            arrived.append((part, peer, sent))
        else:
            mixed, final = recurrence(*common, final_shape, final)
    for part, peer, packed in arrived:
        table = peer.reshape(1)
        final = unpack_states(part, table, packed, final)
    mixed_out = jnp.transpose(mixed, (0, 3, 1, 2, 4))
    final_out = final.reshape((per_device, key_heads, 2, key_dim, key_dim))
    return (mixed_out, final_out)


def solution(mesh):
    placed = (
        P(("groups", "seq"), None, ("head", "sub"), None),
        P(("groups", "seq"), None, ("head", "sub"), None),
        P(("groups", "seq"), None, ("head", "sub"), None, None),
        P(("groups", "seq"), None, ("head", "sub"), None),
        P(("groups", "seq"), None, ("head", "sub"), None),
        P(),
        P(("groups", "seq"), ("head", "sub"), None, None, None),
        P("groups"),
        P("groups"),
        P("groups"),
        P("groups"),
    )
    return jax.shard_map(
        shards,
        mesh=mesh,
        in_specs=placed,
        out_specs=(
            P(("groups", "seq"), None, ("head", "sub"), None, None),
            P(("groups", "seq"), ("head", "sub"), None, None, None),
        ),
        check_vma=False,
    )
```

```python
import functools
from typing import NamedTuple

import jax
import jax.numpy as jnp
from jax import lax
from jax.experimental import pallas as pl
from jax.experimental.pallas import tpu as pltpu
from jax.sharding import PartitionSpec as P

F32 = jnp.float32
BF16 = jnp.bfloat16
HALF = 64
LEN = 128
EPS = 1e-06
TOP = 32512.0
BIAS = 32768.0
CODE = 64.0
VMEM_LIMIT = 8 * 1024 * 1024
PARTS = 2
CODE_ROWS = 8
TOGETHER = 2


def dot(a, b):
    return jnp.dot(a, b, preferred_element_type=F32)


def dot_nt(a, b):
    return lax.dot_general(a, b, (((1,), (1,)), ((), ())), preferred_element_type=F32)


def split(x):
    high = x.astype(BF16)
    return high, (x - high.astype(F32)).astype(BF16)


def iota(shape, dim):
    return lax.broadcasted_iota(jnp.int32, shape, dim)


def step_of(code):
    return jnp.exp2(code * (1.0 / CODE)) * (1.0 / TOP)


def encode(x):
    peak = jnp.maximum(jnp.max(jnp.abs(x), axis=0, keepdims=True), 1e-30)
    code = jnp.ceil(jnp.log2(peak) * CODE) + 1.0
    inverse_step = 1.0 / step_of(code)
    whole = (x * inverse_step + (BIAS + 0.5)).astype(jnp.int32)
    words = jnp.bitwise_or(lax.shift_left(whole[:HALF], 16), whole[HALF:])
    return words, code


def decode(words):
    top = lax.shift_right_logical(words, 16)
    bottom = jnp.bitwise_and(words, 0xFFFF)
    return jnp.concatenate([top, bottom], axis=0).astype(F32) - BIAS


def code_tile(codes):
    row = iota((CODE_ROWS, LEN), 0)
    tile = jnp.zeros((CODE_ROWS, LEN), F32)
    for at, code in enumerate(codes):
        tile = jnp.where(row == at, code, tile)
    return tile.astype(jnp.int32)


def store_packed(ref, states):
    codes = []
    for h, state in enumerate(states):
        words, code = encode(state)
        ref[0, h * HALF:(h + 1) * HALF, :] = words
        codes.append(code)
    at = len(states) * HALF
    ref[0, at:at + CODE_ROWS, :] = code_tile(codes)


def load_steps(ref, heads):
    codes = ref[0, heads * HALF:heads * HALF + CODE_ROWS, :].astype(F32)
    return step_of(codes)


class Plan(NamedTuple):
    group: int
    per_device: int
    per_peer: int

    @staticmethod
    def build(order, owner, slot, tokens, me):
        return jnp.concatenate([order, owner, slot, tokens, me.reshape(1)]).astype(jnp.int32)

    def me(self, flat):
        return flat[4 * self.group]

    def peer(self, flat, away):
        return jnp.bitwise_xor(self.me(flat), away)

    def number(self, flat, away, i):
        return flat[self.peer(flat, away) * self.per_device + self.me(flat) * self.per_peer + i]

    def local(self, flat, away, i):
        return self.number(flat, away, i) - self.me(flat) * self.per_device

    def shard(self, flat, away, i):
        return jnp.bitwise_xor(flat[self.group + self.number(flat, away, i)], self.me(flat))

    def row(self, flat, away, i):
        return flat[2 * self.group + self.number(flat, away, i)]

    def tokens(self, flat, away, i):
        return flat[3 * self.group + self.number(flat, away, i)]

    def tokens_here(self, flat, e):
        return flat[3 * self.group + self.me(flat) * self.per_device + e]


def pack_kernel(state_ref, *out_refs):
    heads = state_ref.shape[1] // len(out_refs)
    for part, out_ref in enumerate(out_refs):
        store_packed(out_ref, [state_ref[0, part * heads + h] for h in range(heads)])


def pack_parents(parents):
    count, heads = parents.shape[:2]
    rows = heads // PARTS * HALF + CODE_ROWS
    return pl.pallas_call(
        pack_kernel,
        grid=(count,),
        in_specs=[pl.BlockSpec((1, heads, LEN, LEN), lambda i: (i, 0, 0, 0))],
        out_specs=[pl.BlockSpec((1, rows, LEN), lambda i: (i, 0, 0))] * PARTS,
        out_shape=[jax.ShapeDtypeStruct((count, rows, LEN), jnp.int32)] * PARTS,
        compiler_params=pltpu.CompilerParams(vmem_limit_bytes=VMEM_LIMIT),
    )(parents)


def block_diag(x, mask):
    return jnp.where(mask, jnp.concatenate([x, x], axis=0), jnp.zeros((), x.dtype))


def live_rates(rates, tokens):
    return jnp.where(iota(rates.shape, 1) < tokens, rates, 0.0).astype(BF16)


def pair_kernel(part, first, plan, flat, q_ref, k_ref, rate_ref, *refs):
    inv_ref, am_ref = refs[-2:]
    expansions, key_heads = q_ref.shape[:2]
    heads = 2 * key_heads
    all_heads = rate_ref.shape[1] // 2
    row = iota((LEN, LEN), 0)
    col = iota((LEN, LEN), 1)
    incl = row >= col
    strict = row > col
    diag_mask = row == col
    prow = iota((HALF, LEN), 0)
    plane = iota((HALF, LEN), 1)
    pcol = jnp.bitwise_and(plane, HALF - 1)
    left = plane < HALF
    bd_mask = (row < HALF) == (col < HALF)
    eye = (prow == pcol).astype(F32)

    def same(size):
        return (prow // size) == (pcol // size)

    base_mask = same(8)
    off_masks = [jnp.logical_and(same(2 * s), jnp.logical_not(same(s))) for s in (8, 16, 32)]
    lower_ones = incl.astype(F32).astype(BF16)
    unit = diag_mask.astype(F32).astype(BF16)

    a_full, where_at = [], []
    for e in range(expansions):
        number = (first + pl.program_id(0)) * expansions + e
        rates = live_rates(rate_ref[e], plan.tokens_here(flat, number))
        cols = dot_nt(jnp.concatenate([lower_ones, unit], axis=0), rates)
        g_cols = cols[:LEN]
        b_cols = cols[LEN:]
        g_rows = dot_nt(rates, lower_ones)
        for m in range(key_heads):
            k = k_ref[e, m]
            gram = dot_nt(jnp.concatenate([q_ref[e, m], k], axis=0), k)
            qk, kk = gram[:LEN], gram[LEN:]
            diagonal = jnp.where(diag_mask, kk, 0.0)
            norm_row = lax.rsqrt(jnp.sum(diagonal, axis=0, keepdims=True) + EPS)
            norm_col = lax.rsqrt(jnp.sum(diagonal, axis=1, keepdims=True) + EPS)
            qk = qk * norm_row
            kk = kk * norm_row
            for r in range(2):
                h = 2 * m + r
                at = part * heads + h
                g_c = g_cols[:, at:at + 1]
                g_r = g_rows[at:at + 1, :]
                pair = jnp.exp(jnp.where(incl, g_c - g_r, -1e4))
                mix = qk * pair
                b_c = b_cols[:, all_heads + at:all_heads + at + 1]
                lower = jnp.where(strict, kk * pair, 0.0) * (b_c * norm_col)
                lower_h, lower_l = split(lower)
                mix_h, mix_l = split(mix)
                am_ref[e, h, :LEN, :LEN] = lower_h
                am_ref[e, h, :LEN, LEN:] = lower_l
                am_ref[e, h, LEN:, :LEN] = mix_h
                am_ref[e, h, LEN:, LEN:] = mix_l
                a_full.append(lower)
                where_at.append((e, h))

    chains = range(len(a_full))
    packed = [jnp.where(left, a_full[c][:HALF], a_full[c][HALF:]) for c in chains]
    base = [jnp.where(base_mask, packed[c], 0.0) for c in chains]
    base_h = [base[c].astype(BF16) for c in chains]
    power = [dot(base_h[c], block_diag(base_h[c], bd_mask)).astype(BF16) for c in chains]
    x = [eye - base[c] for c in chains]
    both = [
        dot(jnp.concatenate([x[c].astype(BF16), power[c]], axis=0), block_diag(power[c], bd_mask))
        for c in chains
    ]
    x = [x[c] + both[c][:HALF] for c in chains]
    power = [both[c][HALF:].astype(BF16) for c in chains]
    x = [x[c] + dot(x[c].astype(BF16), block_diag(power[c], bd_mask)) for c in chains]
    for off in off_masks:
        x_h = [x[c].astype(BF16) for c in chains]
        t = [
            dot(jnp.where(off, packed[c], 0.0).astype(BF16), block_diag(x_h[c], bd_mask)).astype(BF16)
            for c in chains
        ]
        x = [x[c] - dot(x_h[c], block_diag(t[c], bd_mask)) for c in chains]
    x_h = [x[c].astype(BF16) for c in chains]
    t = [
        dot(jnp.where(left, a_full[c][HALF:], 0.0).astype(BF16), block_diag(x_h[c], bd_mask)).astype(BF16)
        for c in chains
    ]
    zero_h = jnp.zeros((HALF, LEN), BF16)
    corner = [dot(jnp.where(left, zero_h, x_h[c]), jnp.concatenate([t[c], t[c]], axis=0)) for c in chains]
    for c in chains:
        e, h = where_at[c]
        inv_ref[e, h, :HALF, :] = jnp.where(left, x[c], 0.0).astype(BF16)
        inv_ref[e, h, HALF:, :] = jnp.where(left, -corner[c], x[c]).astype(BF16)


def pair_parts(part, half, plan, flat, q, k, rates, earlier=None):
    count, all_key_heads = q.shape[:2]
    key_heads = all_key_heads // PARTS
    heads = 2 * key_heads
    block = TOGETHER
    turns = count // block // 2
    first = half * turns
    head_block = pl.BlockSpec((block, key_heads, LEN, LEN), lambda i, t: (first + i, part, 0, 0))
    in_specs = [
        head_block,
        head_block,
        pl.BlockSpec((block,) + rates.shape[1:], lambda i, t: (first + i, 0, 0)),
    ]
    operands = [q, k, rates]
    aliases = {}
    if earlier is not None:
        in_specs += [pl.BlockSpec(memory_space=pl.ANY)] * 2
        aliases = {4: 0, 5: 1}
        operands += list(earlier)
    return pl.pallas_call(
        functools.partial(pair_kernel, part, first, plan),
        grid_spec=pltpu.PrefetchScalarGridSpec(
            num_scalar_prefetch=1,
            grid=(turns,),
            in_specs=in_specs,
            out_specs=[
                pl.BlockSpec((block, heads, LEN, LEN), lambda i, t: (first + i, 0, 0, 0)),
                pl.BlockSpec((block, heads, 2 * LEN, 2 * LEN), lambda i, t: (first + i, 0, 0, 0)),
            ],
        ),
        out_shape=[
            jax.ShapeDtypeStruct((count, heads, LEN, LEN), BF16),
            jax.ShapeDtypeStruct((count, heads, 2 * LEN, 2 * LEN), BF16),
        ],
        input_output_aliases=aliases,
        compiler_params=pltpu.CompilerParams(vmem_limit_bytes=VMEM_LIMIT),
        cost_estimate=pl.CostEstimate(flops=1000, bytes_accessed=1000, transcendentals=0),
    )(flat, *operands)


def state_kernel(part, away, plan, shards_held, together, flat, gain_ref, *refs):
    per = 6
    inputs = [refs[per * e:per * (e + 1)] for e in range(together)]
    parents = refs[per * together:per * together + shards_held]
    mixed_hbm, state_ref, states_in, mixed_out, arrivals, leaving = refs[-6:]
    turn, turns = pl.program_id(0), pl.num_programs(0)
    key_heads = inputs[0][0].shape[1]
    heads = 2 * key_heads
    all_heads = inputs[0][3].shape[1] // 2

    def fetch(i, slot):
        for e in range(together):
            shard = plan.shard(flat, away, i * together + e)
            for off in range(shards_held):
                @pl.when(shard == off)
                def _():
                    pltpu.make_async_copy(
                        parents[off].at[plan.row(flat, away, i * together + e)],
                        states_in.at[slot, e],
                        arrivals.at[slot, e],
                    ).start()

    def leave(i, slot, e):
        return pltpu.make_async_copy(
            mixed_out.at[slot, e],
            mixed_hbm.at[plan.local(flat, away, i * together + e), pl.ds(part * key_heads, key_heads)],
            leaving.at[slot, e],
        )

    slot = lax.rem(turn, 2)

    @pl.when(turn == 0)
    def _():
        fetch(0, 0)

    @pl.when(turn + 1 < turns)
    def _():
        fetch(turn + 1, lax.rem(turn + 1, 2))

    for e in range(together):
        pltpu.make_async_copy(parents[0].at[0], states_in.at[slot, e], arrivals.at[slot, e]).wait()

    @pl.when(turn >= 2)
    def _():
        for e in range(together):
            leave(turn - 2, slot, e).wait()

    row = iota((LEN, LEN), 0)
    col = iota((LEN, LEN), 1)
    lower_ones = (row >= col).astype(F32).astype(BF16)
    unit = (row == col).astype(F32).astype(BF16)
    gain = gain_ref[...].astype(F32)

    state, products, n_cols, g_cols, b_cols, eg_cols, steps = [], [], [], [], [], [], []
    for e in range(together):
        q_ref, k_ref, v_ref, rate_ref, inv_ref, am_ref = inputs[e]
        rates = live_rates(rate_ref[0], plan.tokens(flat, away, turn * together + e))
        cols = dot_nt(jnp.concatenate([lower_ones, unit], axis=0), rates)
        g_cols.append(cols[:LEN])
        b_cols.append(cols[LEN:])
        eg_cols.append(jnp.exp(cols[:LEN]))
        steps.append(load_steps(states_in.at[slot, pl.ds(e, 1)], heads))
        for m in range(key_heads):
            highs, lows = [], []
            for r in range(2):
                h = 2 * m + r
                whole = decode(states_in[slot, e, h * HALF:(h + 1) * HALF, :])
                high, low = split(whole)
                highs.append(high)
                lows.append(low)
                state.append(whole)
            rhs = jnp.concatenate(
                [jnp.concatenate(highs, axis=1), jnp.concatenate(lows, axis=1)], axis=0
            )
            lhs = jnp.concatenate([q_ref[0, m], k_ref[0, m]], axis=0)
            products.append(dot(jnp.concatenate([lhs, lhs], axis=1), rhs))
            keys = k_ref[0, m].astype(F32)
            n_cols.append(lax.rsqrt(jnp.sum(keys * keys, axis=1, keepdims=True) + EPS))

    every = [(e, h) for e in range(together) for h in range(heads)]

    def at_of(h):
        return part * heads + h

    def decay_at(e, h):
        return eg_cols[e][:, at_of(h):at_of(h) + 1]

    def product_at(e, h):
        lane = (h % 2) * LEN
        return products[e * key_heads + h // 2][:, lane:lane + LEN]

    right, first = [], []
    for e, h in every:
        v_ref, inv_ref = inputs[e][2], inputs[e][4]
        ks = product_at(e, h)[LEN:] * steps[e][h:h + 1, :]
        rate = b_cols[e][:, all_heads + at_of(h):all_heads + at_of(h) + 1]
        scale = decay_at(e, h) * n_cols[e * key_heads + h // 2]
        want = rate * (v_ref[0, h // 2, h % 2].astype(F32) - scale * ks)
        right.append(want)
        first.append(dot(inv_ref[0, h], want.astype(BF16)).astype(BF16))
    am_v = [
        dot(inputs[e][5][0, h], jnp.concatenate([first[c], first[c]], axis=0))
        for c, (e, h) in enumerate(every)
    ]
    delta = [
        dot(inputs[e][4][0, h], (right[c] - first[c].astype(F32) - am_v[c][:LEN]).astype(BF16))
        for c, (e, h) in enumerate(every)
    ]
    scaled = []
    for c, (e, h) in enumerate(every):
        g_c = g_cols[e][:, at_of(h):at_of(h) + 1]
        tail = jnp.exp(g_c[LEN - 1:LEN, :] - g_c) * n_cols[e * key_heads + h // 2]
        scaled.append(split(tail * (first[c].astype(F32) + delta[c])))
    finals = []
    for e in range(together):
        for m in range(key_heads):
            turned = jnp.transpose(inputs[e][1][0, m])
            c = e * heads + 2 * m
            rhs = jnp.concatenate(
                [jnp.concatenate([scaled[c][p], scaled[c + 1][p]], axis=1) for p in range(2)], axis=0
            )
            added = dot(jnp.concatenate([turned, turned], axis=1), rhs)
            for r in range(2):
                h = 2 * m + r
                keep = decay_at(e, h)[LEN - 1:LEN, :] * steps[e][h:h + 1, :]
                finals.append(keep * state[c + r] + added[:, r * LEN:(r + 1) * LEN])
    for c, (e, h) in enumerate(every):
        qs = product_at(e, h)[:LEN] * steps[e][h:h + 1, :]
        out = decay_at(e, h) * qs + am_v[c][LEN:]
        out = out + dot(inputs[e][5][0, h, LEN:, :LEN], delta[c].astype(BF16))
        mean_square = jnp.mean(out * out, axis=1, keepdims=True)
        live = iota((LEN, 1), 0) < plan.tokens(flat, away, turn * together + e)
        scale = jnp.where(live, lax.rsqrt(mean_square + EPS), 0.0)
        mixed_out[slot, e, h // 2, h % 2] = (out * scale * gain).astype(BF16)
    for e in range(together):
        leave(turn, slot, e).start()
    for e in range(together):
        mine = finals[e * heads:(e + 1) * heads]
        if away == 0:
            for h in range(heads):
                state_ref[e, h] = mine[h]
        else:
            store_packed(state_ref.at[pl.ds(e, 1)], mine)

    @pl.when(turn == turns - 1)
    def _():
        for e in range(together):
            leave(turn, slot, e).wait()

    @pl.when(jnp.logical_and(turn == turns - 1, turn >= 1))
    def _():
        for e in range(together):
            leave(turn - 1, 1 - slot, e).wait()


def recurrence(part, away, plan, flat, q, k, v, rates, pairs, parents, gain, mixed, final_shape=None, final=None):
    count = plan.per_peer
    together = min(TOGETHER, count)
    turns = count // together
    key_heads = q.shape[1] // PARTS
    heads = 2 * key_heads
    rows = heads * HALF + CODE_ROWS
    in_specs = [pl.BlockSpec((1, LEN), lambda i, t: (0, 0))]
    operands = [gain]

    def one(shape, e, at):
        def index(i, t):
            return (plan.local(t, away, i * together + e), at) + (0,) * (len(shape) - 2)

        return pl.BlockSpec(shape, index)

    for e in range(together):
        in_specs += [
            one((1, key_heads, LEN, LEN), e, part),
            one((1, key_heads, LEN, LEN), e, part),
            one((1, key_heads, 2, LEN, LEN), e, part),
            one((1,) + rates.shape[1:], e, 0),
            one((1, heads, LEN, LEN), e, 0),
            one((1, heads, 2 * LEN, 2 * LEN), e, 0),
        ]
        operands += [q, k, v, rates, *pairs]
    in_specs += [pl.BlockSpec(memory_space=pl.ANY)] * len(parents)
    operands += parents
    aliases = {}
    if mixed is not None:
        in_specs.append(pl.BlockSpec(memory_space=pl.ANY))
        aliases[1 + len(operands)] = 0
        operands.append(mixed)
    mixed_spec = pl.BlockSpec(memory_space=pl.ANY)
    mixed_shape = jax.ShapeDtypeStruct(v.shape, BF16)
    if final_shape is None:
        state_spec = pl.BlockSpec((together, rows, LEN), lambda i, t: (i, 0, 0))
        state_shape = jax.ShapeDtypeStruct((count, rows, LEN), jnp.int32)
    else:
        if final is not None:
            in_specs.append(pl.BlockSpec(memory_space=pl.ANY))
            aliases[1 + len(operands)] = 1
            operands.append(final)
        state_spec = pl.BlockSpec((together, heads, LEN, LEN), lambda i, t: (plan.me(t) * turns + i, part, 0, 0))
        state_shape = jax.ShapeDtypeStruct(final_shape, F32)
    return pl.pallas_call(
        functools.partial(state_kernel, part, away, plan, len(parents), together),
        grid_spec=pltpu.PrefetchScalarGridSpec(
            num_scalar_prefetch=1,
            grid=(turns,),
            in_specs=in_specs,
            out_specs=[mixed_spec, state_spec],
            scratch_shapes=[
                pltpu.VMEM((2, together, rows, LEN), jnp.int32),
                pltpu.VMEM((2, together, key_heads, 2, LEN, LEN), BF16),
                pltpu.SemaphoreType.DMA((2, together)),
                pltpu.SemaphoreType.DMA((2, together)),
            ],
        ),
        out_shape=[mixed_shape, state_shape],
        input_output_aliases=aliases,
        compiler_params=pltpu.CompilerParams(vmem_limit_bytes=VMEM_LIMIT),
        cost_estimate=pl.CostEstimate(flops=1000, bytes_accessed=1000, transcendentals=0),
    )(flat, *operands)


def unpack_kernel(flat, packed_ref, old_ref, out_ref):
    count, heads = out_ref.shape[:2]
    for e in range(count):
        steps = load_steps(packed_ref.at[pl.ds(e, 1)], heads)
        for h in range(heads):
            out_ref[e, h] = decode(packed_ref[e, h * HALF:(h + 1) * HALF, :]) * steps[h:h + 1, :]


def unpack_states(part, away, plan, flat, packed, final):
    count, rows = packed.shape[:2]
    heads = final.shape[1] // PARTS
    block = max(1, count // 2)
    turns = count // block
    return pl.pallas_call(
        unpack_kernel,
        grid_spec=pltpu.PrefetchScalarGridSpec(
            num_scalar_prefetch=1,
            grid=(turns,),
            in_specs=[
                pl.BlockSpec((block, rows, LEN), lambda i, t: (i, 0, 0)),
                pl.BlockSpec(memory_space=pl.ANY),
            ],
            out_specs=pl.BlockSpec((block, heads, LEN, LEN), lambda i, t: (plan.peer(t, away) * turns + i, part, 0, 0)),
        ),
        out_shape=jax.ShapeDtypeStruct(final.shape, F32),
        input_output_aliases={2: 0},
        compiler_params=pltpu.CompilerParams(vmem_limit_bytes=VMEM_LIMIT),
        cost_estimate=pl.CostEstimate(flops=1000, bytes_accessed=1000, transcendentals=0),
    )(flat, packed, final)


def shards(
    queries,
    keys,
    values,
    log_decay,
    write_rate,
    norm_gain,
    parent_cache,
    order,
    parent_owner,
    parent_slot,
    token_count,
):
    seq_count = lax.axis_size("seq")
    me = lax.axis_index("seq")
    per_device, length, key_heads, key_dim = queries.shape
    per_peer = per_device // seq_count
    cache_rows = parent_cache.shape[0]
    heads = 2 * key_heads

    parents = parent_cache.reshape((cache_rows, heads, key_dim, key_dim))
    own = list(pack_parents(parents))

    def swap(tensor, off):
        return lax.ppermute(tensor, "seq", [(i, i ^ off) for i in range(seq_count)])

    def spread(held, off):
        while off:
            held = {**held, **{at ^ off: swap(held[at], off) for at in held}}
            off //= 2
        return held

    half_way = seq_count // 2
    far = swap(own[0], half_way)
    q = jnp.transpose(queries, (0, 2, 1, 3))
    k = jnp.transpose(keys, (0, 2, 1, 3))
    v = jnp.transpose(values, (0, 2, 3, 1, 4))

    def rows_of(tensor):
        return jnp.transpose(tensor, (0, 2, 3, 1)).reshape(per_device, heads, length).astype(F32)

    rates = jnp.concatenate([rows_of(log_decay), rows_of(write_rate)], axis=1)
    gain = norm_gain.reshape(1, -1)
    plan = Plan(order.shape[0], per_device, per_peer)
    flat = Plan.build(order, parent_owner, parent_slot, token_count, me)

    own[0], q = lax.optimization_barrier((own[0], q))
    q, k, v, rates, gain, flat = lax.optimization_barrier((q, k, v, rates, gain, flat))

    pairs = [pair_parts(0, 0, plan, flat, q, k, rates), None]
    pairs[0], far, own[1] = lax.optimization_barrier((pairs[0], far, own[1]))
    held_0 = spread({0: own[0], half_way: far}, half_way // 2)
    far_1 = swap(own[1], half_way)
    pairs[0] = pair_parts(0, 1, plan, flat, q, k, rates, pairs[0])
    rates, pairs[0] = lax.optimization_barrier((rates, pairs[0]))
    pairs[1] = pair_parts(1, 0, plan, flat, q, k, rates)
    pairs, held_0, far_1, own = lax.optimization_barrier((pairs, held_0, far_1, own))
    held_1 = spread({0: own[1], half_way: far_1}, half_way // 2)
    gathered = [[held[at] for at in range(seq_count)] for held in (held_0, held_1)]

    final_shape = (per_device, heads, key_dim, key_dim)
    crossing = list(reversed(range(half_way, seq_count)))
    near = list(reversed(range(1, half_way)))
    turns = [(part, away) for part in range(PARTS) for away in crossing]
    turns += [(part, away) for part in range(PARTS) for away in near]
    turns += [(part, 0) for part in range(PARTS)]
    mixed, final = None, None
    arrived = {}
    for part, away in turns:
        if part == 1 and away == crossing[0]:
            rates, mixed, pairs[1] = lax.optimization_barrier((rates, mixed, pairs[1]))
            pairs[1] = pair_parts(1, 1, plan, flat, q, k, rates, pairs[1])
        common = (part, away, plan, flat, q, k, v, rates, pairs[part], gathered[part], gain, mixed)
        if away:
            mixed, packed = recurrence(*common)
            arrived[part, away] = swap(packed, away)
        else:
            mixed, final = recurrence(*common, final_shape, final)
    for part, away in [(0, away) for away in crossing + near] + [(1, away) for away in near + crossing]:
        final = unpack_states(part, away, plan, flat, arrived[part, away], final)
    mixed_out = jnp.transpose(mixed, (0, 3, 1, 2, 4))
    final_out = final.reshape((per_device, key_heads, 2, key_dim, key_dim))
    return (mixed_out, final_out)


def solution(mesh):
    placed = (
        P(("groups", "seq"), None, ("head", "sub"), None),
        P(("groups", "seq"), None, ("head", "sub"), None),
        P(("groups", "seq"), None, ("head", "sub"), None, None),
        P(("groups", "seq"), None, ("head", "sub"), None),
        P(("groups", "seq"), None, ("head", "sub"), None),
        P(),
        P(("groups", "seq"), ("head", "sub"), None, None, None),
        P("groups"),
        P("groups"),
        P("groups"),
        P("groups"),
    )
    return jax.shard_map(
        shards,
        mesh=mesh,
        in_specs=placed,
        out_specs=(
            P(("groups", "seq"), None, ("head", "sub"), None, None),
            P(("groups", "seq"), ("head", "sub"), None, None, None),
        ),
        check_vma=False,
    )
```

```python
import functools
from typing import NamedTuple

import jax
import jax.numpy as jnp
from jax import lax
from jax.experimental import pallas as pl
from jax.experimental.pallas import tpu as pltpu
from jax.sharding import PartitionSpec as P

F32 = jnp.float32
BF16 = jnp.bfloat16
HALF = 64
LEN = 128
EPS = 1e-06
TOP = 32512.0
BIAS = 32768.0
CODE = 64.0
VMEM_LIMIT = 8 * 1024 * 1024
PARTS = 2
CODE_ROWS = 8
TOGETHER = 2


def dot(a, b):
    return jnp.dot(a, b, preferred_element_type=F32)


def dot_nt(a, b):
    return lax.dot_general(a, b, (((1,), (1,)), ((), ())), preferred_element_type=F32)


def split(x):
    high = x.astype(BF16)
    return high, (x - high.astype(F32)).astype(BF16)


def iota(shape, dim):
    return lax.broadcasted_iota(jnp.int32, shape, dim)


def step_of(code):
    return jnp.exp2(code * (1.0 / CODE)) * (1.0 / TOP)


def encode(x):
    peak = jnp.maximum(jnp.max(jnp.abs(x), axis=0, keepdims=True), 1e-30)
    code = jnp.ceil(jnp.log2(peak) * CODE) + 1.0
    inverse_step = 1.0 / step_of(code)
    whole = (x * inverse_step + (BIAS + 0.5)).astype(jnp.int32)
    words = jnp.bitwise_or(lax.shift_left(whole[:HALF], 16), whole[HALF:])
    return words, code


def decode(words):
    top = lax.shift_right_logical(words, 16)
    bottom = jnp.bitwise_and(words, 0xFFFF)
    return jnp.concatenate([top, bottom], axis=0).astype(F32) - BIAS


def code_tile(codes):
    row = iota((CODE_ROWS, LEN), 0)
    tile = jnp.zeros((CODE_ROWS, LEN), F32)
    for at, code in enumerate(codes):
        tile = jnp.where(row == at, code, tile)
    return tile.astype(jnp.int32)


def store_packed(ref, states):
    codes = []
    for h, state in enumerate(states):
        words, code = encode(state)
        ref[0, h * HALF:(h + 1) * HALF, :] = words
        codes.append(code)
    at = len(states) * HALF
    ref[0, at:at + CODE_ROWS, :] = code_tile(codes)


def load_steps(ref, heads):
    codes = ref[0, heads * HALF:heads * HALF + CODE_ROWS, :].astype(F32)
    return step_of(codes)


class Plan(NamedTuple):
    group: int
    per_device: int
    per_peer: int

    @staticmethod
    def build(order, owner, slot, tokens, me):
        return jnp.concatenate([order, owner, slot, tokens, me.reshape(1)]).astype(jnp.int32)

    def me(self, flat):
        return flat[4 * self.group]

    def peer(self, flat, away):
        return jnp.bitwise_xor(self.me(flat), away)

    def number(self, flat, away, i):
        return flat[self.peer(flat, away) * self.per_device + self.me(flat) * self.per_peer + i]

    def local(self, flat, away, i):
        return self.number(flat, away, i) - self.me(flat) * self.per_device

    def shard(self, flat, away, i):
        return jnp.bitwise_xor(flat[self.group + self.number(flat, away, i)], self.me(flat))

    def row(self, flat, away, i):
        return flat[2 * self.group + self.number(flat, away, i)]

    def tokens(self, flat, away, i):
        return flat[3 * self.group + self.number(flat, away, i)]

    def tokens_here(self, flat, e):
        return flat[3 * self.group + self.me(flat) * self.per_device + e]


def pack_kernel(state_ref, *out_refs):
    heads = state_ref.shape[1] // len(out_refs)
    for part, out_ref in enumerate(out_refs):
        store_packed(out_ref, [state_ref[0, part * heads + h] for h in range(heads)])


def pack_parents(parents):
    count, heads = parents.shape[:2]
    rows = heads // PARTS * HALF + CODE_ROWS
    return pl.pallas_call(
        pack_kernel,
        grid=(count,),
        in_specs=[pl.BlockSpec((1, heads, LEN, LEN), lambda i: (i, 0, 0, 0))],
        out_specs=[pl.BlockSpec((1, rows, LEN), lambda i: (i, 0, 0))] * PARTS,
        out_shape=[jax.ShapeDtypeStruct((count, rows, LEN), jnp.int32)] * PARTS,
        compiler_params=pltpu.CompilerParams(vmem_limit_bytes=VMEM_LIMIT),
    )(parents)


def block_diag(x, mask):
    return jnp.where(mask, jnp.concatenate([x, x], axis=0), jnp.zeros((), x.dtype))


def live_rates(rates, tokens):
    return jnp.where(iota(rates.shape, 1) < tokens, rates, 0.0).astype(BF16)


def pair_kernel(part, first, plan, flat, q_ref, k_ref, rate_ref, *refs):
    inv_ref, am_ref = refs[-2:]
    expansions, key_heads = q_ref.shape[:2]
    heads = 2 * key_heads
    all_heads = rate_ref.shape[1] // 2
    row = iota((LEN, LEN), 0)
    col = iota((LEN, LEN), 1)
    incl = row >= col
    strict = row > col
    diag_mask = row == col
    prow = iota((HALF, LEN), 0)
    plane = iota((HALF, LEN), 1)
    pcol = jnp.bitwise_and(plane, HALF - 1)
    left = plane < HALF
    bd_mask = (row < HALF) == (col < HALF)
    eye = (prow == pcol).astype(F32)

    def same(size):
        return (prow // size) == (pcol // size)

    base_mask = same(8)
    off_masks = [jnp.logical_and(same(2 * s), jnp.logical_not(same(s))) for s in (8, 16, 32)]
    lower_ones = incl.astype(F32).astype(BF16)
    unit = diag_mask.astype(F32).astype(BF16)

    a_full, where_at = [], []
    for e in range(expansions):
        number = (first + pl.program_id(0)) * expansions + e
        rates = live_rates(rate_ref[e], plan.tokens_here(flat, number))
        cols = dot_nt(jnp.concatenate([lower_ones, unit], axis=0), rates)
        g_cols = cols[:LEN]
        b_cols = cols[LEN:]
        g_rows = dot_nt(rates, lower_ones)
        for m in range(key_heads):
            k = k_ref[e, m]
            gram = dot_nt(jnp.concatenate([q_ref[e, m], k], axis=0), k)
            qk, kk = gram[:LEN], gram[LEN:]
            diagonal = jnp.where(diag_mask, kk, 0.0)
            norm_row = lax.rsqrt(jnp.sum(diagonal, axis=0, keepdims=True) + EPS)
            norm_col = lax.rsqrt(jnp.sum(diagonal, axis=1, keepdims=True) + EPS)
            qk = qk * norm_row
            kk = kk * norm_row
            for r in range(2):
                h = 2 * m + r
                at = part * heads + h
                g_c = g_cols[:, at:at + 1]
                g_r = g_rows[at:at + 1, :]
                pair = jnp.exp(jnp.where(incl, g_c - g_r, -1e4))
                mix = qk * pair
                b_c = b_cols[:, all_heads + at:all_heads + at + 1]
                lower = jnp.where(strict, kk * pair, 0.0) * (b_c * norm_col)
                lower_h, lower_l = split(lower)
                mix_h, mix_l = split(mix)
                am_ref[e, h, :LEN, :LEN] = lower_h
                am_ref[e, h, :LEN, LEN:] = lower_l
                am_ref[e, h, LEN:, :LEN] = mix_h
                am_ref[e, h, LEN:, LEN:] = mix_l
                a_full.append(lower)
                where_at.append((e, h))

    chains = range(len(a_full))
    packed = [jnp.where(left, a_full[c][:HALF], a_full[c][HALF:]) for c in chains]
    base = [jnp.where(base_mask, packed[c], 0.0) for c in chains]
    base_h = [base[c].astype(BF16) for c in chains]
    power = [dot(base_h[c], block_diag(base_h[c], bd_mask)).astype(BF16) for c in chains]
    x = [eye - base[c] for c in chains]
    both = [
        dot(jnp.concatenate([x[c].astype(BF16), power[c]], axis=0), block_diag(power[c], bd_mask))
        for c in chains
    ]
    x = [x[c] + both[c][:HALF] for c in chains]
    power = [both[c][HALF:].astype(BF16) for c in chains]
    x = [x[c] + dot(x[c].astype(BF16), block_diag(power[c], bd_mask)) for c in chains]
    for off in off_masks:
        x_h = [x[c].astype(BF16) for c in chains]
        t = [
            dot(jnp.where(off, packed[c], 0.0).astype(BF16), block_diag(x_h[c], bd_mask)).astype(BF16)
            for c in chains
        ]
        x = [x[c] - dot(x_h[c], block_diag(t[c], bd_mask)) for c in chains]
    x_h = [x[c].astype(BF16) for c in chains]
    t = [
        dot(jnp.where(left, a_full[c][HALF:], 0.0).astype(BF16), block_diag(x_h[c], bd_mask)).astype(BF16)
        for c in chains
    ]
    zero_h = jnp.zeros((HALF, LEN), BF16)
    corner = [dot(jnp.where(left, zero_h, x_h[c]), jnp.concatenate([t[c], t[c]], axis=0)) for c in chains]
    for c in chains:
        e, h = where_at[c]
        inv_ref[e, h, :HALF, :] = jnp.where(left, x[c], 0.0).astype(BF16)
        inv_ref[e, h, HALF:, :] = jnp.where(left, -corner[c], x[c]).astype(BF16)


def pair_parts(part, half, plan, flat, q, k, rates, earlier=None):
    count, all_key_heads = q.shape[:2]
    key_heads = all_key_heads // PARTS
    heads = 2 * key_heads
    block = TOGETHER
    turns = count // block // 2
    first = half * turns
    head_block = pl.BlockSpec((block, key_heads, LEN, LEN), lambda i, t: (first + i, part, 0, 0))
    in_specs = [
        head_block,
        head_block,
        pl.BlockSpec((block,) + rates.shape[1:], lambda i, t: (first + i, 0, 0)),
    ]
    operands = [q, k, rates]
    aliases = {}
    if earlier is not None:
        in_specs += [pl.BlockSpec(memory_space=pl.ANY)] * 2
        aliases = {4: 0, 5: 1}
        operands += list(earlier)
    return pl.pallas_call(
        functools.partial(pair_kernel, part, first, plan),
        grid_spec=pltpu.PrefetchScalarGridSpec(
            num_scalar_prefetch=1,
            grid=(turns,),
            in_specs=in_specs,
            out_specs=[
                pl.BlockSpec((block, heads, LEN, LEN), lambda i, t: (first + i, 0, 0, 0)),
                pl.BlockSpec((block, heads, 2 * LEN, 2 * LEN), lambda i, t: (first + i, 0, 0, 0)),
            ],
        ),
        out_shape=[
            jax.ShapeDtypeStruct((count, heads, LEN, LEN), BF16),
            jax.ShapeDtypeStruct((count, heads, 2 * LEN, 2 * LEN), BF16),
        ],
        input_output_aliases=aliases,
        compiler_params=pltpu.CompilerParams(vmem_limit_bytes=VMEM_LIMIT),
        cost_estimate=pl.CostEstimate(flops=1000, bytes_accessed=1000, transcendentals=0),
    )(flat, *operands)


def turn_of(aways, each, turn):
    if len(aways) == 1:
        return aways[0], turn
    number = turn // each
    away = aways[-1]
    for at in reversed(range(len(aways) - 1)):
        away = jnp.where(number == at, aways[at], away)
    return away, turn - number * each


def state_kernel(part, aways, plan, shards_held, together, flat, gain_ref, *refs):
    per = 6
    inputs = [refs[per * e:per * (e + 1)] for e in range(together)]
    parents = refs[per * together:per * together + shards_held]
    states_in, mixed_out, arrivals, leaving = refs[-4:]
    mixed_hbm, *state_refs = refs[-5 - len(aways):-4]
    turn, turns = pl.program_id(0), pl.num_programs(0)
    each = plan.per_peer // together
    key_heads = inputs[0][0].shape[1]
    heads = 2 * key_heads
    all_heads = inputs[0][3].shape[1] // 2

    def fetch(i, slot):
        for e in range(together):
            away, at = turn_of(aways, each, i)
            shard = plan.shard(flat, away, at * together + e)
            for off in range(shards_held):
                @pl.when(shard == off)
                def _():
                    pltpu.make_async_copy(
                        parents[off].at[plan.row(flat, away, at * together + e)],
                        states_in.at[slot, e],
                        arrivals.at[slot, e],
                    ).start()

    def leave(i, slot, e):
        away, at = turn_of(aways, each, i)
        return pltpu.make_async_copy(
            mixed_out.at[slot, e],
            mixed_hbm.at[plan.local(flat, away, at * together + e), pl.ds(part * key_heads, key_heads)],
            leaving.at[slot, e],
        )

    slot = lax.rem(turn, 2)
    my_away, my_turn = turn_of(aways, each, turn)

    @pl.when(turn == 0)
    def _():
        fetch(0, 0)

    @pl.when(turn + 1 < turns)
    def _():
        fetch(turn + 1, lax.rem(turn + 1, 2))

    for e in range(together):
        pltpu.make_async_copy(parents[0].at[0], states_in.at[slot, e], arrivals.at[slot, e]).wait()

    @pl.when(turn >= 2)
    def _():
        for e in range(together):
            leave(turn - 2, slot, e).wait()

    row = iota((LEN, LEN), 0)
    col = iota((LEN, LEN), 1)
    lower_ones = (row >= col).astype(F32).astype(BF16)
    unit = (row == col).astype(F32).astype(BF16)
    gain = gain_ref[...].astype(F32)

    state, products, n_cols, g_cols, b_cols, eg_cols, steps = [], [], [], [], [], [], []
    for e in range(together):
        q_ref, k_ref, v_ref, rate_ref, inv_ref, am_ref = inputs[e]
        rates = live_rates(rate_ref[0], plan.tokens(flat, my_away, my_turn * together + e))
        cols = dot_nt(jnp.concatenate([lower_ones, unit], axis=0), rates)
        g_cols.append(cols[:LEN])
        b_cols.append(cols[LEN:])
        eg_cols.append(jnp.exp(cols[:LEN]))
        steps.append(load_steps(states_in.at[slot, pl.ds(e, 1)], heads))
        for m in range(key_heads):
            highs, lows = [], []
            for r in range(2):
                h = 2 * m + r
                whole = decode(states_in[slot, e, h * HALF:(h + 1) * HALF, :])
                high, low = split(whole)
                highs.append(high)
                lows.append(low)
                state.append(whole)
            rhs = jnp.concatenate(
                [jnp.concatenate(highs, axis=1), jnp.concatenate(lows, axis=1)], axis=0
            )
            lhs = jnp.concatenate([q_ref[0, m], k_ref[0, m]], axis=0)
            products.append(dot(jnp.concatenate([lhs, lhs], axis=1), rhs))
            keys = k_ref[0, m].astype(F32)
            n_cols.append(lax.rsqrt(jnp.sum(keys * keys, axis=1, keepdims=True) + EPS))

    every = [(e, h) for e in range(together) for h in range(heads)]

    def at_of(h):
        return part * heads + h

    def decay_at(e, h):
        return eg_cols[e][:, at_of(h):at_of(h) + 1]

    def product_at(e, h):
        lane = (h % 2) * LEN
        return products[e * key_heads + h // 2][:, lane:lane + LEN]

    right, first = [], []
    for e, h in every:
        v_ref, inv_ref = inputs[e][2], inputs[e][4]
        ks = product_at(e, h)[LEN:] * steps[e][h:h + 1, :]
        rate = b_cols[e][:, all_heads + at_of(h):all_heads + at_of(h) + 1]
        scale = decay_at(e, h) * n_cols[e * key_heads + h // 2]
        want = rate * (v_ref[0, h // 2, h % 2].astype(F32) - scale * ks)
        right.append(want)
        first.append(dot(inv_ref[0, h], want.astype(BF16)).astype(BF16))
    am_v = [
        dot(inputs[e][5][0, h], jnp.concatenate([first[c], first[c]], axis=0))
        for c, (e, h) in enumerate(every)
    ]
    delta = [
        dot(inputs[e][4][0, h], (right[c] - first[c].astype(F32) - am_v[c][:LEN]).astype(BF16))
        for c, (e, h) in enumerate(every)
    ]
    scaled = []
    for c, (e, h) in enumerate(every):
        g_c = g_cols[e][:, at_of(h):at_of(h) + 1]
        tail = jnp.exp(g_c[LEN - 1:LEN, :] - g_c) * n_cols[e * key_heads + h // 2]
        scaled.append(split(tail * (first[c].astype(F32) + delta[c])))
    finals = []
    for e in range(together):
        for m in range(key_heads):
            turned = jnp.transpose(inputs[e][1][0, m])
            c = e * heads + 2 * m
            rhs = jnp.concatenate(
                [jnp.concatenate([scaled[c][p], scaled[c + 1][p]], axis=1) for p in range(2)], axis=0
            )
            added = dot(jnp.concatenate([turned, turned], axis=1), rhs)
            for r in range(2):
                h = 2 * m + r
                keep = decay_at(e, h)[LEN - 1:LEN, :] * steps[e][h:h + 1, :]
                finals.append(keep * state[c + r] + added[:, r * LEN:(r + 1) * LEN])
    for c, (e, h) in enumerate(every):
        qs = product_at(e, h)[:LEN] * steps[e][h:h + 1, :]
        out = decay_at(e, h) * qs + am_v[c][LEN:]
        out = out + dot(inputs[e][5][0, h, LEN:, :LEN], delta[c].astype(BF16))
        mean_square = jnp.mean(out * out, axis=1, keepdims=True)
        live = iota((LEN, 1), 0) < plan.tokens(flat, my_away, my_turn * together + e)
        scale = jnp.where(live, lax.rsqrt(mean_square + EPS), 0.0)
        mixed_out[slot, e, h // 2, h % 2] = (out * scale * gain).astype(BF16)
    for e in range(together):
        leave(turn, slot, e).start()

    def store(ref, away):
        for e in range(together):
            mine = finals[e * heads:(e + 1) * heads]
            if away:
                store_packed(ref.at[pl.ds(e, 1)], mine)
            else:
                for h in range(heads):
                    ref[e, h] = mine[h]

    for number, away in enumerate(aways):
        if len(aways) == 1:
            store(state_refs[0], away)
        else:
            pl.when(turn // each == number)(functools.partial(store, state_refs[number], away))

    @pl.when(turn == turns - 1)
    def _():
        for e in range(together):
            leave(turn, slot, e).wait()

    @pl.when(jnp.logical_and(turn == turns - 1, turn >= 1))
    def _():
        for e in range(together):
            leave(turn - 1, 1 - slot, e).wait()


def recurrence(part, aways, plan, flat, q, k, v, rates, pairs, parents, gain, mixed, final_shape, final):
    count = plan.per_peer
    together = min(TOGETHER, count)
    turns = count // together
    key_heads = q.shape[1] // PARTS
    heads = 2 * key_heads
    rows = heads * HALF + CODE_ROWS
    in_specs = [pl.BlockSpec((1, LEN), lambda i, t: (0, 0))]
    operands = [gain]

    def one(shape, e, at):
        def index(i, t):
            away, turn = turn_of(aways, turns, i)
            return (plan.local(t, away, turn * together + e), at) + (0,) * (len(shape) - 2)

        return pl.BlockSpec(shape, index)

    for e in range(together):
        in_specs += [
            one((1, key_heads, LEN, LEN), e, part),
            one((1, key_heads, LEN, LEN), e, part),
            one((1, key_heads, 2, LEN, LEN), e, part),
            one((1,) + rates.shape[1:], e, 0),
            one((1, heads, LEN, LEN), e, 0),
            one((1, heads, 2 * LEN, 2 * LEN), e, 0),
        ]
        operands += [q, k, v, rates, *pairs]
    in_specs += [pl.BlockSpec(memory_space=pl.ANY)] * len(parents)
    operands += parents
    aliases = {}
    if mixed is not None:
        in_specs.append(pl.BlockSpec(memory_space=pl.ANY))
        aliases[1 + len(operands)] = 0
        operands.append(mixed)
    mixed_spec = pl.BlockSpec(memory_space=pl.ANY)
    mixed_shape = jax.ShapeDtypeStruct(v.shape, BF16)
    state_specs, state_shapes = [], []

    def turn_in(number, i):
        return i if len(aways) == 1 else jnp.clip(i - number * turns, 0, turns - 1)

    for number, away in enumerate(aways):
        if away:
            state_specs.append(
                pl.BlockSpec((together, rows, LEN), lambda i, t, n=number: (turn_in(n, i), 0, 0))
            )
            state_shapes.append(jax.ShapeDtypeStruct((count, rows, LEN), jnp.int32))
        else:
            if final is not None:
                in_specs.append(pl.BlockSpec(memory_space=pl.ANY))
                aliases[1 + len(operands)] = 1 + number
                operands.append(final)
            state_specs.append(
                pl.BlockSpec(
                    (together, heads, LEN, LEN),
                    lambda i, t, n=number: (plan.me(t) * turns + turn_in(n, i), part, 0, 0),
                )
            )
            state_shapes.append(jax.ShapeDtypeStruct(final_shape, F32))
    return pl.pallas_call(
        functools.partial(state_kernel, part, aways, plan, len(parents), together),
        grid_spec=pltpu.PrefetchScalarGridSpec(
            num_scalar_prefetch=1,
            grid=(turns * len(aways),),
            in_specs=in_specs,
            out_specs=[mixed_spec, *state_specs],
            scratch_shapes=[
                pltpu.VMEM((2, together, rows, LEN), jnp.int32),
                pltpu.VMEM((2, together, key_heads, 2, LEN, LEN), BF16),
                pltpu.SemaphoreType.DMA((2, together)),
                pltpu.SemaphoreType.DMA((2, together)),
            ],
        ),
        out_shape=[mixed_shape, *state_shapes],
        input_output_aliases=aliases,
        compiler_params=pltpu.CompilerParams(vmem_limit_bytes=VMEM_LIMIT),
        cost_estimate=pl.CostEstimate(flops=1000, bytes_accessed=1000, transcendentals=0),
    )(flat, *operands)


def unpack_kernel(turns, flat, *refs):
    *packed_refs, old_ref, out_ref = refs
    count, heads = out_ref.shape[:2]

    def unpack(ref):
        for e in range(count):
            steps = load_steps(ref.at[pl.ds(e, 1)], heads)
            for h in range(heads):
                out_ref[e, h] = decode(ref[e, h * HALF:(h + 1) * HALF, :]) * steps[h:h + 1, :]

    for number, ref in enumerate(packed_refs):
        if len(packed_refs) == 1:
            unpack(ref)
        else:
            pl.when(pl.program_id(0) // turns == number)(functools.partial(unpack, ref))


def unpack_states(part, aways, plan, flat, packed, final):
    count, rows = packed[0].shape[:2]
    heads = final.shape[1] // PARTS
    block = max(1, count // 2)
    turns = count // block

    def place(i, t):
        away, turn = turn_of(aways, turns, i)
        return (plan.peer(t, away) * turns + turn, part, 0, 0)

    def turn_in(number, i):
        return i if len(aways) == 1 else jnp.clip(i - number * turns, 0, turns - 1)

    return pl.pallas_call(
        functools.partial(unpack_kernel, turns),
        grid_spec=pltpu.PrefetchScalarGridSpec(
            num_scalar_prefetch=1,
            grid=(turns * len(aways),),
            in_specs=[
                pl.BlockSpec((block, rows, LEN), lambda i, t, n=number: (turn_in(n, i), 0, 0))
                for number in range(len(aways))
            ]
            + [pl.BlockSpec(memory_space=pl.ANY)],
            out_specs=pl.BlockSpec((block, heads, LEN, LEN), place),
        ),
        out_shape=jax.ShapeDtypeStruct(final.shape, F32),
        input_output_aliases={1 + len(aways): 0},
        compiler_params=pltpu.CompilerParams(vmem_limit_bytes=VMEM_LIMIT),
        cost_estimate=pl.CostEstimate(flops=1000, bytes_accessed=1000, transcendentals=0),
    )(flat, *packed, final)


def turn_kernel(mixed_ref, out_ref):
    key_heads, pair, length, size = mixed_ref.shape[1:]
    out_ref[0] = jnp.swapaxes(mixed_ref[0].reshape(key_heads * pair, length, size), 0, 1)


def turn_mixed(mixed):
    count, key_heads, pair, length, size = mixed.shape
    heads = key_heads * pair
    return pl.pallas_call(
        turn_kernel,
        grid=(count,),
        in_specs=[pl.BlockSpec((1, key_heads, pair, length, size), lambda i: (i, 0, 0, 0, 0))],
        out_specs=pl.BlockSpec((1, length, heads, size), lambda i: (i, 0, 0, 0)),
        out_shape=jax.ShapeDtypeStruct((count, length, heads, size), mixed.dtype),
        compiler_params=pltpu.CompilerParams(vmem_limit_bytes=VMEM_LIMIT),
        cost_estimate=pl.CostEstimate(flops=1000, bytes_accessed=1000, transcendentals=0),
    )(mixed)


def shards(
    queries,
    keys,
    values,
    log_decay,
    write_rate,
    norm_gain,
    parent_cache,
    order,
    parent_owner,
    parent_slot,
    token_count,
):
    seq_count = lax.axis_size("seq")
    me = lax.axis_index("seq")
    per_device, length, key_heads, key_dim = queries.shape
    per_peer = per_device // seq_count
    cache_rows = parent_cache.shape[0]
    heads = 2 * key_heads

    parents = parent_cache.reshape((cache_rows, heads, key_dim, key_dim))
    own = list(pack_parents(parents))

    def swap(tensor, off):
        return lax.ppermute(tensor, "seq", [(i, i ^ off) for i in range(seq_count)])

    def spread(held, off):
        while off:
            held = {**held, **{at ^ off: swap(held[at], off) for at in held}}
            off //= 2
        return held

    half_way = seq_count // 2
    far = swap(own[0], half_way)
    q = jnp.transpose(queries, (0, 2, 1, 3))
    k = jnp.transpose(keys, (0, 2, 1, 3))
    v = jnp.transpose(values, (0, 2, 3, 1, 4))

    def rows_of(tensor):
        return jnp.transpose(tensor, (0, 2, 3, 1)).reshape(per_device, heads, length).astype(F32)

    rates = jnp.concatenate([rows_of(log_decay), rows_of(write_rate)], axis=1)
    gain = norm_gain.reshape(1, -1)
    plan = Plan(order.shape[0], per_device, per_peer)
    flat = Plan.build(order, parent_owner, parent_slot, token_count, me)

    own[0], q = lax.optimization_barrier((own[0], q))
    q, k, v, rates, gain, flat = lax.optimization_barrier((q, k, v, rates, gain, flat))

    pairs = [pair_parts(0, 0, plan, flat, q, k, rates), None]
    pairs[0], far, own[1] = lax.optimization_barrier((pairs[0], far, own[1]))
    held_0 = spread({0: own[0], half_way: far}, half_way // 2)
    far_1 = swap(own[1], half_way)
    pairs[0] = pair_parts(0, 1, plan, flat, q, k, rates, pairs[0])
    rates, pairs[0] = lax.optimization_barrier((rates, pairs[0]))
    pairs[1] = pair_parts(1, 0, plan, flat, q, k, rates)
    pairs, held_0, far_1, own = lax.optimization_barrier((pairs, held_0, far_1, own))
    held_1 = spread({0: own[1], half_way: far_1}, half_way // 2)
    gathered = [[held[at] for at in range(seq_count)] for held in (held_0, held_1)]

    final_shape = (per_device, heads, key_dim, key_dim)
    crossing = list(reversed(range(half_way, seq_count)))
    near = list(reversed(range(1, half_way)))
    mixed, final = None, None
    arrived = {}

    def work(part, aways, mixed, final):
        mixed, *states = recurrence(
            part, aways, plan, flat, q, k, v, rates, pairs[part], gathered[part], gain, mixed, final_shape, final
        )
        for away, state in zip(aways, states):
            if away:
                arrived[part, away] = swap(state, away)
            else:
                final = state
        return mixed, final

    def gone(mixed, aways):
        for away in aways:
            mixed, arrived[0, away] = lax.optimization_barrier((mixed, arrived[0, away]))
        return mixed

    for away in crossing + near:
        mixed, final = work(0, [away], mixed, final)
    rates, mixed, pairs[1] = lax.optimization_barrier((rates, mixed, pairs[1]))
    pairs[1] = pair_parts(1, 1, plan, flat, q, k, rates, pairs[1])
    mixed = gone(mixed, crossing[:1])
    for away in near + crossing:
        mixed, final = work(1, [away], mixed, final)
    mixed = gone(mixed, crossing[1:] + near)
    for part in range(PARTS):
        mixed, final = work(part, [0], mixed, final)
    away_first = crossing + near
    final = unpack_states(0, away_first, plan, flat, [arrived[0, away] for away in away_first], final)
    for away in near + crossing:
        final = unpack_states(1, [away], plan, flat, [arrived[1, away]], final)
    mixed_out = turn_mixed(mixed).reshape(values.shape)
    final_out = final.reshape((per_device, key_heads, 2, key_dim, key_dim))
    return (mixed_out, final_out)


def solution(mesh):
    placed = (
        P(("groups", "seq"), None, ("head", "sub"), None),
        P(("groups", "seq"), None, ("head", "sub"), None),
        P(("groups", "seq"), None, ("head", "sub"), None, None),
        P(("groups", "seq"), None, ("head", "sub"), None),
        P(("groups", "seq"), None, ("head", "sub"), None),
        P(),
        P(("groups", "seq"), ("head", "sub"), None, None, None),
        P("groups"),
        P("groups"),
        P("groups"),
        P("groups"),
    )
    return jax.shard_map(
        shards,
        mesh=mesh,
        in_specs=placed,
        out_specs=(
            P(("groups", "seq"), None, ("head", "sub"), None, None),
            P(("groups", "seq"), ("head", "sub"), None, None, None),
        ),
        check_vma=False,
    )
```

```python
import functools
from typing import NamedTuple

import jax
import jax.numpy as jnp
from jax import lax
from jax.experimental import pallas as pl
from jax.experimental.pallas import tpu as pltpu
from jax.sharding import PartitionSpec as P

F32 = jnp.float32
BF16 = jnp.bfloat16
HALF = 64
LEN = 128
EPS = 1e-06
TOP = 32512.0
BIAS = 32768.0
CODE = 64.0
VMEM_LIMIT = 8 * 1024 * 1024
PARTS = 2
CODE_ROWS = 8
TOGETHER = 2


def dot(a, b):
    return jnp.dot(a, b, preferred_element_type=F32)


def dot_nt(a, b):
    return lax.dot_general(a, b, (((1,), (1,)), ((), ())), preferred_element_type=F32)


def split(x):
    high = x.astype(BF16)
    return high, (x - high.astype(F32)).astype(BF16)


def iota(shape, dim):
    return lax.broadcasted_iota(jnp.int32, shape, dim)


def step_of(code):
    return jnp.exp2(code * (1.0 / CODE)) * (1.0 / TOP)


def encode(x):
    peak = jnp.maximum(jnp.max(jnp.abs(x), axis=0, keepdims=True), 1e-30)
    code = jnp.ceil(jnp.log2(peak) * CODE) + 1.0
    inverse_step = 1.0 / step_of(code)
    whole = (x * inverse_step + (BIAS + 0.5)).astype(jnp.int32)
    words = jnp.bitwise_or(lax.shift_left(whole[:HALF], 16), whole[HALF:])
    return words, code


def decode(words):
    top = lax.shift_right_logical(words, 16)
    bottom = jnp.bitwise_and(words, 0xFFFF)
    return jnp.concatenate([top, bottom], axis=0).astype(F32) - BIAS


def code_tile(codes):
    row = iota((CODE_ROWS, LEN), 0)
    tile = jnp.zeros((CODE_ROWS, LEN), F32)
    for at, code in enumerate(codes):
        tile = jnp.where(row == at, code, tile)
    return tile.astype(jnp.int32)


def store_packed(ref, states):
    codes = []
    for h, state in enumerate(states):
        words, code = encode(state)
        ref[0, h * HALF:(h + 1) * HALF, :] = words
        codes.append(code)
    at = len(states) * HALF
    ref[0, at:at + CODE_ROWS, :] = code_tile(codes)


def load_steps(ref, heads):
    codes = ref[0, heads * HALF:heads * HALF + CODE_ROWS, :].astype(F32)
    return step_of(codes)


class Plan(NamedTuple):
    group: int
    per_device: int
    per_peer: int

    @staticmethod
    def build(order, owner, slot, tokens, me):
        return jnp.concatenate([order, owner, slot, tokens, me.reshape(1)]).astype(jnp.int32)

    def me(self, flat):
        return flat[4 * self.group]

    def peer(self, flat, away):
        return jnp.bitwise_xor(self.me(flat), away)

    def number(self, flat, away, i):
        return flat[self.peer(flat, away) * self.per_device + self.me(flat) * self.per_peer + i]

    def local(self, flat, away, i):
        return self.number(flat, away, i) - self.me(flat) * self.per_device

    def shard(self, flat, away, i):
        return jnp.bitwise_xor(flat[self.group + self.number(flat, away, i)], self.me(flat))

    def row(self, flat, away, i):
        return flat[2 * self.group + self.number(flat, away, i)]

    def tokens(self, flat, away, i):
        return flat[3 * self.group + self.number(flat, away, i)]

    def tokens_here(self, flat, e):
        return flat[3 * self.group + self.me(flat) * self.per_device + e]


def pack_kernel(state_ref, *out_refs):
    heads = state_ref.shape[1] // len(out_refs)
    for part, out_ref in enumerate(out_refs):
        store_packed(out_ref, [state_ref[0, part * heads + h] for h in range(heads)])


def pack_parents(parents):
    count, heads = parents.shape[:2]
    rows = heads // PARTS * HALF + CODE_ROWS
    return pl.pallas_call(
        pack_kernel,
        grid=(count,),
        in_specs=[pl.BlockSpec((1, heads, LEN, LEN), lambda i: (i, 0, 0, 0))],
        out_specs=[pl.BlockSpec((1, rows, LEN), lambda i: (i, 0, 0))] * PARTS,
        out_shape=[jax.ShapeDtypeStruct((count, rows, LEN), jnp.int32)] * PARTS,
        compiler_params=pltpu.CompilerParams(vmem_limit_bytes=VMEM_LIMIT),
    )(parents)


def block_diag(x, mask):
    return jnp.where(mask, jnp.concatenate([x, x], axis=0), jnp.zeros((), x.dtype))


def live_rates(rates, tokens):
    return jnp.where(iota(rates.shape, 1) < tokens, rates, 0.0).astype(BF16)


def pair_kernel(part, first, plan, flat, q_ref, k_ref, rate_ref, *refs):
    inv_ref, am_ref = refs[-2:]
    expansions, key_heads = q_ref.shape[:2]
    heads = 2 * key_heads
    all_heads = rate_ref.shape[1] // 2
    row = iota((LEN, LEN), 0)
    col = iota((LEN, LEN), 1)
    incl = row >= col
    strict = row > col
    diag_mask = row == col
    prow = iota((HALF, LEN), 0)
    plane = iota((HALF, LEN), 1)
    pcol = jnp.bitwise_and(plane, HALF - 1)
    left = plane < HALF
    bd_mask = (row < HALF) == (col < HALF)
    eye = (prow == pcol).astype(F32)

    def same(size):
        return (prow // size) == (pcol // size)

    base_mask = same(8)
    off_masks = [jnp.logical_and(same(2 * s), jnp.logical_not(same(s))) for s in (8, 16, 32)]
    lower_ones = incl.astype(F32).astype(BF16)
    unit = diag_mask.astype(F32).astype(BF16)

    a_full, where_at = [], []
    for e in range(expansions):
        number = (first + pl.program_id(0)) * expansions + e
        rates = live_rates(rate_ref[e], plan.tokens_here(flat, number))
        cols = dot_nt(jnp.concatenate([lower_ones, unit], axis=0), rates)
        g_cols = cols[:LEN]
        b_cols = cols[LEN:]
        g_rows = dot_nt(rates, lower_ones)
        for m in range(key_heads):
            k = k_ref[e, m]
            gram = dot_nt(jnp.concatenate([q_ref[e, m], k], axis=0), k)
            qk, kk = gram[:LEN], gram[LEN:]
            diagonal = jnp.where(diag_mask, kk, 0.0)
            norm_row = lax.rsqrt(jnp.sum(diagonal, axis=0, keepdims=True) + EPS)
            norm_col = lax.rsqrt(jnp.sum(diagonal, axis=1, keepdims=True) + EPS)
            qk = qk * norm_row
            kk = kk * norm_row
            for r in range(2):
                h = 2 * m + r
                at = part * heads + h
                g_c = g_cols[:, at:at + 1]
                g_r = g_rows[at:at + 1, :]
                pair = jnp.exp(jnp.where(incl, g_c - g_r, -1e4))
                mix = qk * pair
                b_c = b_cols[:, all_heads + at:all_heads + at + 1]
                lower = jnp.where(strict, kk * pair, 0.0) * (b_c * norm_col)
                lower_h, lower_l = split(lower)
                mix_h, mix_l = split(mix)
                am_ref[e, h, :LEN, :LEN] = lower_h
                am_ref[e, h, :LEN, LEN:] = lower_l
                am_ref[e, h, LEN:, :LEN] = mix_h
                am_ref[e, h, LEN:, LEN:] = mix_l
                a_full.append(lower)
                where_at.append((e, h))

    chains = range(len(a_full))
    packed = [jnp.where(left, a_full[c][:HALF], a_full[c][HALF:]) for c in chains]
    base = [jnp.where(base_mask, packed[c], 0.0) for c in chains]
    base_h = [base[c].astype(BF16) for c in chains]
    power = [dot(base_h[c], block_diag(base_h[c], bd_mask)).astype(BF16) for c in chains]
    x = [eye - base[c] for c in chains]
    both = [
        dot(jnp.concatenate([x[c].astype(BF16), power[c]], axis=0), block_diag(power[c], bd_mask))
        for c in chains
    ]
    x = [x[c] + both[c][:HALF] for c in chains]
    power = [both[c][HALF:].astype(BF16) for c in chains]
    x = [x[c] + dot(x[c].astype(BF16), block_diag(power[c], bd_mask)) for c in chains]
    for off in off_masks:
        x_h = [x[c].astype(BF16) for c in chains]
        t = [
            dot(jnp.where(off, packed[c], 0.0).astype(BF16), block_diag(x_h[c], bd_mask)).astype(BF16)
            for c in chains
        ]
        x = [x[c] - dot(x_h[c], block_diag(t[c], bd_mask)) for c in chains]
    x_h = [x[c].astype(BF16) for c in chains]
    t = [
        dot(jnp.where(left, a_full[c][HALF:], 0.0).astype(BF16), block_diag(x_h[c], bd_mask)).astype(BF16)
        for c in chains
    ]
    zero_h = jnp.zeros((HALF, LEN), BF16)
    corner = [dot(jnp.where(left, zero_h, x_h[c]), jnp.concatenate([t[c], t[c]], axis=0)) for c in chains]
    for c in chains:
        e, h = where_at[c]
        inv_ref[e, h, :HALF, :] = jnp.where(left, x[c], 0.0).astype(BF16)
        inv_ref[e, h, HALF:, :] = jnp.where(left, -corner[c], x[c]).astype(BF16)


def pair_parts(part, half, plan, flat, q, k, rates, earlier=None):
    count, all_key_heads = q.shape[:2]
    key_heads = all_key_heads // PARTS
    heads = 2 * key_heads
    block = TOGETHER
    turns = count // block // 2
    first = half * turns
    head_block = pl.BlockSpec((block, key_heads, LEN, LEN), lambda i, t: (first + i, part, 0, 0))
    in_specs = [
        head_block,
        head_block,
        pl.BlockSpec((block,) + rates.shape[1:], lambda i, t: (first + i, 0, 0)),
    ]
    operands = [q, k, rates]
    aliases = {}
    if earlier is not None:
        in_specs += [pl.BlockSpec(memory_space=pl.ANY)] * 2
        aliases = {4: 0, 5: 1}
        operands += list(earlier)
    return pl.pallas_call(
        functools.partial(pair_kernel, part, first, plan),
        grid_spec=pltpu.PrefetchScalarGridSpec(
            num_scalar_prefetch=1,
            grid=(turns,),
            in_specs=in_specs,
            out_specs=[
                pl.BlockSpec((block, heads, LEN, LEN), lambda i, t: (first + i, 0, 0, 0)),
                pl.BlockSpec((block, heads, 2 * LEN, 2 * LEN), lambda i, t: (first + i, 0, 0, 0)),
            ],
        ),
        out_shape=[
            jax.ShapeDtypeStruct((count, heads, LEN, LEN), BF16),
            jax.ShapeDtypeStruct((count, heads, 2 * LEN, 2 * LEN), BF16),
        ],
        input_output_aliases=aliases,
        compiler_params=pltpu.CompilerParams(vmem_limit_bytes=VMEM_LIMIT),
        cost_estimate=pl.CostEstimate(flops=1000, bytes_accessed=1000, transcendentals=0),
    )(flat, *operands)


def turn_of(aways, each, turn):
    if len(aways) == 1:
        return aways[0], turn
    number = turn // each
    away = aways[-1]
    for at in reversed(range(len(aways) - 1)):
        away = jnp.where(number == at, aways[at], away)
    return away, turn - number * each


def state_kernel(part, aways, plan, shards_held, together, flat, gain_ref, *refs):
    per = 6
    inputs = [refs[per * e:per * (e + 1)] for e in range(together)]
    parents = refs[per * together:per * together + shards_held]
    states_in, mixed_out, arrivals, leaving = refs[-4:]
    mixed_hbm, *state_refs = refs[-5 - len(aways):-4]
    turn, turns = pl.program_id(0), pl.num_programs(0)
    each = plan.per_peer // together
    key_heads = inputs[0][0].shape[1]
    heads = 2 * key_heads
    all_heads = inputs[0][3].shape[1] // 2

    def fetch(i, slot):
        for e in range(together):
            away, at = turn_of(aways, each, i)
            shard = plan.shard(flat, away, at * together + e)
            for off in range(shards_held):
                @pl.when(shard == off)
                def _():
                    pltpu.make_async_copy(
                        parents[off].at[plan.row(flat, away, at * together + e)],
                        states_in.at[slot, e],
                        arrivals.at[slot, e],
                    ).start()

    def leave(i, slot, e):
        away, at = turn_of(aways, each, i)
        return pltpu.make_async_copy(
            mixed_out.at[slot, e],
            mixed_hbm.at[plan.local(flat, away, at * together + e), pl.ds(part * key_heads, key_heads)],
            leaving.at[slot, e],
        )

    slot = lax.rem(turn, 2)
    my_away, my_turn = turn_of(aways, each, turn)

    @pl.when(turn == 0)
    def _():
        fetch(0, 0)

    @pl.when(turn + 1 < turns)
    def _():
        fetch(turn + 1, lax.rem(turn + 1, 2))

    for e in range(together):
        pltpu.make_async_copy(parents[0].at[0], states_in.at[slot, e], arrivals.at[slot, e]).wait()

    @pl.when(turn >= 2)
    def _():
        for e in range(together):
            leave(turn - 2, slot, e).wait()

    row = iota((LEN, LEN), 0)
    col = iota((LEN, LEN), 1)
    lower_ones = (row >= col).astype(F32).astype(BF16)
    unit = (row == col).astype(F32).astype(BF16)
    gain = gain_ref[...].astype(F32)

    state, products, n_cols, g_cols, b_cols, eg_cols, steps = [], [], [], [], [], [], []
    for e in range(together):
        q_ref, k_ref, v_ref, rate_ref, inv_ref, am_ref = inputs[e]
        rates = live_rates(rate_ref[0], plan.tokens(flat, my_away, my_turn * together + e))
        cols = dot_nt(jnp.concatenate([lower_ones, unit], axis=0), rates)
        g_cols.append(cols[:LEN])
        b_cols.append(cols[LEN:])
        eg_cols.append(jnp.exp(cols[:LEN]))
        steps.append(load_steps(states_in.at[slot, pl.ds(e, 1)], heads))
        for m in range(key_heads):
            highs, lows = [], []
            for r in range(2):
                h = 2 * m + r
                whole = decode(states_in[slot, e, h * HALF:(h + 1) * HALF, :])
                high, low = split(whole)
                highs.append(high)
                lows.append(low)
                state.append(whole)
            rhs = jnp.concatenate(
                [jnp.concatenate(highs, axis=1), jnp.concatenate(lows, axis=1)], axis=0
            )
            lhs = jnp.concatenate([q_ref[0, m], k_ref[0, m]], axis=0)
            products.append(dot(jnp.concatenate([lhs, lhs], axis=1), rhs))
            keys = k_ref[0, m].astype(F32)
            n_cols.append(lax.rsqrt(jnp.sum(keys * keys, axis=1, keepdims=True) + EPS))

    every = [(e, h) for e in range(together) for h in range(heads)]

    def at_of(h):
        return part * heads + h

    def decay_at(e, h):
        return eg_cols[e][:, at_of(h):at_of(h) + 1]

    def product_at(e, h):
        lane = (h % 2) * LEN
        return products[e * key_heads + h // 2][:, lane:lane + LEN]

    right, first = [], []
    for e, h in every:
        v_ref, inv_ref = inputs[e][2], inputs[e][4]
        ks = product_at(e, h)[LEN:] * steps[e][h:h + 1, :]
        rate = b_cols[e][:, all_heads + at_of(h):all_heads + at_of(h) + 1]
        scale = decay_at(e, h) * n_cols[e * key_heads + h // 2]
        want = rate * (v_ref[0, h // 2, h % 2].astype(F32) - scale * ks)
        right.append(want)
        first.append(dot(inv_ref[0, h], want.astype(BF16)).astype(BF16))
    am_v = [
        dot(inputs[e][5][0, h], jnp.concatenate([first[c], first[c]], axis=0))
        for c, (e, h) in enumerate(every)
    ]
    delta = [
        dot(inputs[e][4][0, h], (right[c] - first[c].astype(F32) - am_v[c][:LEN]).astype(BF16))
        for c, (e, h) in enumerate(every)
    ]
    scaled = []
    for c, (e, h) in enumerate(every):
        g_c = g_cols[e][:, at_of(h):at_of(h) + 1]
        tail = jnp.exp(g_c[LEN - 1:LEN, :] - g_c) * n_cols[e * key_heads + h // 2]
        scaled.append(split(tail * (first[c].astype(F32) + delta[c])))
    finals = []
    for e in range(together):
        for m in range(key_heads):
            turned = jnp.transpose(inputs[e][1][0, m])
            c = e * heads + 2 * m
            rhs = jnp.concatenate(
                [jnp.concatenate([scaled[c][p], scaled[c + 1][p]], axis=1) for p in range(2)], axis=0
            )
            added = dot(jnp.concatenate([turned, turned], axis=1), rhs)
            for r in range(2):
                h = 2 * m + r
                keep = decay_at(e, h)[LEN - 1:LEN, :] * steps[e][h:h + 1, :]
                finals.append(keep * state[c + r] + added[:, r * LEN:(r + 1) * LEN])
    for c, (e, h) in enumerate(every):
        qs = product_at(e, h)[:LEN] * steps[e][h:h + 1, :]
        out = decay_at(e, h) * qs + am_v[c][LEN:]
        out = out + dot(inputs[e][5][0, h, LEN:, :LEN], delta[c].astype(BF16))
        mean_square = jnp.mean(out * out, axis=1, keepdims=True)
        live = iota((LEN, 1), 0) < plan.tokens(flat, my_away, my_turn * together + e)
        scale = jnp.where(live, lax.rsqrt(mean_square + EPS), 0.0)
        mixed_out[slot, e, h // 2, h % 2] = (out * scale * gain).astype(BF16)
    for e in range(together):
        leave(turn, slot, e).start()

    def store(ref, away):
        for e in range(together):
            mine = finals[e * heads:(e + 1) * heads]
            if away:
                store_packed(ref.at[pl.ds(e, 1)], mine)
            else:
                for h in range(heads):
                    ref[e, h] = mine[h]

    for number, away in enumerate(aways):
        if len(aways) == 1:
            store(state_refs[0], away)
        else:
            pl.when(turn // each == number)(functools.partial(store, state_refs[number], away))

    @pl.when(turn == turns - 1)
    def _():
        for e in range(together):
            leave(turn, slot, e).wait()

    @pl.when(jnp.logical_and(turn == turns - 1, turn >= 1))
    def _():
        for e in range(together):
            leave(turn - 1, 1 - slot, e).wait()


def recurrence(part, aways, plan, flat, q, k, v, rates, pairs, parents, gain, mixed, final_shape, final):
    count = plan.per_peer
    together = min(TOGETHER, count)
    turns = count // together
    key_heads = q.shape[1] // PARTS
    heads = 2 * key_heads
    rows = heads * HALF + CODE_ROWS
    in_specs = [pl.BlockSpec((1, LEN), lambda i, t: (0, 0))]
    operands = [gain]

    def one(shape, e, at):
        def index(i, t):
            away, turn = turn_of(aways, turns, i)
            return (plan.local(t, away, turn * together + e), at) + (0,) * (len(shape) - 2)

        return pl.BlockSpec(shape, index)

    for e in range(together):
        in_specs += [
            one((1, key_heads, LEN, LEN), e, part),
            one((1, key_heads, LEN, LEN), e, part),
            one((1, key_heads, 2, LEN, LEN), e, part),
            one((1,) + rates.shape[1:], e, 0),
            one((1, heads, LEN, LEN), e, 0),
            one((1, heads, 2 * LEN, 2 * LEN), e, 0),
        ]
        operands += [q, k, v, rates, *pairs]
    in_specs += [pl.BlockSpec(memory_space=pl.ANY)] * len(parents)
    operands += parents
    aliases = {}
    if mixed is not None:
        in_specs.append(pl.BlockSpec(memory_space=pl.ANY))
        aliases[1 + len(operands)] = 0
        operands.append(mixed)
    mixed_spec = pl.BlockSpec(memory_space=pl.ANY)
    mixed_shape = jax.ShapeDtypeStruct(v.shape, BF16)
    state_specs, state_shapes = [], []

    def turn_in(number, i):
        return i if len(aways) == 1 else jnp.clip(i - number * turns, 0, turns - 1)

    for number, away in enumerate(aways):
        if away:
            state_specs.append(
                pl.BlockSpec((together, rows, LEN), lambda i, t, n=number: (turn_in(n, i), 0, 0))
            )
            state_shapes.append(jax.ShapeDtypeStruct((count, rows, LEN), jnp.int32))
        else:
            if final is not None:
                in_specs.append(pl.BlockSpec(memory_space=pl.ANY))
                aliases[1 + len(operands)] = 1 + number
                operands.append(final)
            state_specs.append(
                pl.BlockSpec(
                    (together, heads, LEN, LEN),
                    lambda i, t, n=number: (plan.me(t) * turns + turn_in(n, i), part, 0, 0),
                )
            )
            state_shapes.append(jax.ShapeDtypeStruct(final_shape, F32))
    return pl.pallas_call(
        functools.partial(state_kernel, part, aways, plan, len(parents), together),
        grid_spec=pltpu.PrefetchScalarGridSpec(
            num_scalar_prefetch=1,
            grid=(turns * len(aways),),
            in_specs=in_specs,
            out_specs=[mixed_spec, *state_specs],
            scratch_shapes=[
                pltpu.VMEM((2, together, rows, LEN), jnp.int32),
                pltpu.VMEM((2, together, key_heads, 2, LEN, LEN), BF16),
                pltpu.SemaphoreType.DMA((2, together)),
                pltpu.SemaphoreType.DMA((2, together)),
            ],
        ),
        out_shape=[mixed_shape, *state_shapes],
        input_output_aliases=aliases,
        compiler_params=pltpu.CompilerParams(vmem_limit_bytes=VMEM_LIMIT),
        cost_estimate=pl.CostEstimate(flops=1000, bytes_accessed=1000, transcendentals=0),
    )(flat, *operands)


def unpack_kernel(turns, flat, *refs):
    *packed_refs, old_ref, out_ref = refs
    count, heads = out_ref.shape[:2]

    def unpack(ref):
        for e in range(count):
            steps = load_steps(ref.at[pl.ds(e, 1)], heads)
            for h in range(heads):
                out_ref[e, h] = decode(ref[e, h * HALF:(h + 1) * HALF, :]) * steps[h:h + 1, :]

    for number, ref in enumerate(packed_refs):
        if len(packed_refs) == 1:
            unpack(ref)
        else:
            pl.when(pl.program_id(0) // turns == number)(functools.partial(unpack, ref))


def unpack_states(part, aways, plan, flat, packed, final):
    count, rows = packed[0].shape[:2]
    heads = final.shape[1] // PARTS
    block = max(1, count // 2)
    turns = count // block

    def place(i, t):
        away, turn = turn_of(aways, turns, i)
        return (plan.peer(t, away) * turns + turn, part, 0, 0)

    def turn_in(number, i):
        return i if len(aways) == 1 else jnp.clip(i - number * turns, 0, turns - 1)

    return pl.pallas_call(
        functools.partial(unpack_kernel, turns),
        grid_spec=pltpu.PrefetchScalarGridSpec(
            num_scalar_prefetch=1,
            grid=(turns * len(aways),),
            in_specs=[
                pl.BlockSpec((block, rows, LEN), lambda i, t, n=number: (turn_in(n, i), 0, 0))
                for number in range(len(aways))
            ]
            + [pl.BlockSpec(memory_space=pl.ANY)],
            out_specs=pl.BlockSpec((block, heads, LEN, LEN), place),
        ),
        out_shape=jax.ShapeDtypeStruct(final.shape, F32),
        input_output_aliases={1 + len(aways): 0},
        compiler_params=pltpu.CompilerParams(vmem_limit_bytes=VMEM_LIMIT),
        cost_estimate=pl.CostEstimate(flops=1000, bytes_accessed=1000, transcendentals=0),
    )(flat, *packed, final)


def turn_kernel(mixed_ref, out_ref):
    key_heads, pair, length, size = mixed_ref.shape[1:]
    out_ref[0] = jnp.swapaxes(mixed_ref[0].reshape(key_heads * pair, length, size), 0, 1)


def turn_mixed(mixed):
    count, key_heads, pair, length, size = mixed.shape
    heads = key_heads * pair
    return pl.pallas_call(
        turn_kernel,
        grid=(count,),
        in_specs=[pl.BlockSpec((1, key_heads, pair, length, size), lambda i: (i, 0, 0, 0, 0))],
        out_specs=pl.BlockSpec((1, length, heads, size), lambda i: (i, 0, 0, 0)),
        out_shape=jax.ShapeDtypeStruct((count, length, heads, size), mixed.dtype),
        compiler_params=pltpu.CompilerParams(vmem_limit_bytes=VMEM_LIMIT),
        cost_estimate=pl.CostEstimate(flops=1000, bytes_accessed=1000, transcendentals=0),
    )(mixed)


def shards(
    queries,
    keys,
    values,
    log_decay,
    write_rate,
    norm_gain,
    parent_cache,
    order,
    parent_owner,
    parent_slot,
    token_count,
):
    seq_count = lax.axis_size("seq")
    me = lax.axis_index("seq")
    per_device, length, key_heads, key_dim = queries.shape
    per_peer = per_device // seq_count
    cache_rows = parent_cache.shape[0]
    heads = 2 * key_heads

    parents = parent_cache.reshape((cache_rows, heads, key_dim, key_dim))
    own = list(pack_parents(parents))

    def swap(tensor, off):
        return lax.ppermute(tensor, "seq", [(i, i ^ off) for i in range(seq_count)])

    def spread(held, off):
        while off:
            held = {**held, **{at ^ off: swap(held[at], off) for at in held}}
            off //= 2
        return held

    half_way = seq_count // 2
    far = swap(own[0], half_way)
    q = jnp.transpose(queries, (0, 2, 1, 3))
    k = jnp.transpose(keys, (0, 2, 1, 3))
    v = jnp.transpose(values, (0, 2, 3, 1, 4))

    def rows_of(tensor):
        return jnp.transpose(tensor, (0, 2, 3, 1)).reshape(per_device, heads, length).astype(F32)

    rates = jnp.concatenate([rows_of(log_decay), rows_of(write_rate)], axis=1)
    gain = norm_gain.reshape(1, -1)
    plan = Plan(order.shape[0], per_device, per_peer)
    flat = Plan.build(order, parent_owner, parent_slot, token_count, me)

    own[0], q = lax.optimization_barrier((own[0], q))
    q, k, v, rates, gain, flat = lax.optimization_barrier((q, k, v, rates, gain, flat))

    pairs = [pair_parts(0, 0, plan, flat, q, k, rates), None]
    pairs[0], far, own[1] = lax.optimization_barrier((pairs[0], far, own[1]))
    held_0 = spread({0: own[0], half_way: far}, half_way // 2)
    far_1 = swap(own[1], half_way)
    pairs[0] = pair_parts(0, 1, plan, flat, q, k, rates, pairs[0])
    rates, pairs[0] = lax.optimization_barrier((rates, pairs[0]))
    pairs[1] = pair_parts(1, 0, plan, flat, q, k, rates)
    pairs, held_0, far_1, own = lax.optimization_barrier((pairs, held_0, far_1, own))
    held_1 = spread({0: own[1], half_way: far_1}, half_way // 2)
    gathered = [[held[at] for at in range(seq_count)] for held in (held_0, held_1)]

    final_shape = (per_device, heads, key_dim, key_dim)
    crossing = list(reversed(range(half_way, seq_count)))
    near = list(reversed(range(1, half_way)))
    mixed, final = None, None
    arrived = {}

    def work(part, aways, mixed, final):
        mixed, *states = recurrence(
            part, aways, plan, flat, q, k, v, rates, pairs[part], gathered[part], gain, mixed, final_shape, final
        )
        for away, state in zip(aways, states):
            if away:
                arrived[part, away] = swap(state, away)
            else:
                final = state
        return mixed, final

    def gone(mixed, aways):
        for away in aways:
            mixed, arrived[0, away] = lax.optimization_barrier((mixed, arrived[0, away]))
        return mixed

    for away in crossing:
        mixed, final = work(0, [away], mixed, final)
    rates, mixed, pairs[1] = lax.optimization_barrier((rates, mixed, pairs[1]))
    pairs[1] = pair_parts(1, 1, plan, flat, q, k, rates, pairs[1])
    for away in near:
        mixed, final = work(0, [away], mixed, final)
    mixed, pairs[1], gathered[1] = lax.optimization_barrier((mixed, pairs[1], gathered[1]))
    mixed = gone(mixed, crossing[:1])
    for away in near + crossing:
        mixed, final = work(1, [away], mixed, final)
    mixed = gone(mixed, crossing[1:])
    for part in range(PARTS):
        mixed, final = work(part, [0], mixed, final)
    away_first = crossing + near
    final = unpack_states(0, away_first, plan, flat, [arrived[0, away] for away in away_first], final)
    for away in near + crossing:
        final = unpack_states(1, [away], plan, flat, [arrived[1, away]], final)
    mixed_out = turn_mixed(mixed).reshape(values.shape)
    final_out = final.reshape((per_device, key_heads, 2, key_dim, key_dim))
    return (mixed_out, final_out)


def solution(mesh):
    placed = (
        P(("groups", "seq"), None, ("head", "sub"), None),
        P(("groups", "seq"), None, ("head", "sub"), None),
        P(("groups", "seq"), None, ("head", "sub"), None, None),
        P(("groups", "seq"), None, ("head", "sub"), None),
        P(("groups", "seq"), None, ("head", "sub"), None),
        P(),
        P(("groups", "seq"), ("head", "sub"), None, None, None),
        P("groups"),
        P("groups"),
        P("groups"),
        P("groups"),
    )
    return jax.shard_map(
        shards,
        mesh=mesh,
        in_specs=placed,
        out_specs=(
            P(("groups", "seq"), None, ("head", "sub"), None, None),
            P(("groups", "seq"), ("head", "sub"), None, None, None),
        ),
        check_vma=False,
    )
```

```python
import functools
from typing import NamedTuple

import jax
import jax.numpy as jnp
from jax import lax
from jax.experimental import pallas as pl
from jax.experimental.pallas import tpu as pltpu
from jax.sharding import PartitionSpec as P

F32 = jnp.float32
BF16 = jnp.bfloat16
HALF = 64
LEN = 128
EPS = 1e-06
TOP = 32512.0
BIAS = 32768.0
CODE = 64.0
VMEM_LIMIT = 8 * 1024 * 1024
PARTS = 2
CODE_ROWS = 8
TOGETHER = 2


def dot(a, b):
    return jnp.dot(a, b, preferred_element_type=F32)


def dot_nt(a, b):
    return lax.dot_general(a, b, (((1,), (1,)), ((), ())), preferred_element_type=F32)


def split(x):
    high = x.astype(BF16)
    return high, (x - high.astype(F32)).astype(BF16)


def iota(shape, dim):
    return lax.broadcasted_iota(jnp.int32, shape, dim)


def step_of(code):
    return jnp.exp2(code * (1.0 / CODE)) * (1.0 / TOP)


def encode(x):
    peak = jnp.maximum(jnp.max(jnp.abs(x), axis=0, keepdims=True), 1e-30)
    code = jnp.ceil(jnp.log2(peak) * CODE) + 1.0
    inverse_step = 1.0 / step_of(code)
    whole = (x * inverse_step + (BIAS + 0.5)).astype(jnp.int32)
    words = jnp.bitwise_or(lax.shift_left(whole[:HALF], 16), whole[HALF:])
    return words, code


def decode(words):
    top = lax.shift_right_logical(words, 16)
    bottom = jnp.bitwise_and(words, 0xFFFF)
    return jnp.concatenate([top, bottom], axis=0).astype(F32) - BIAS


def code_tile(codes):
    row = iota((CODE_ROWS, LEN), 0)
    tile = jnp.zeros((CODE_ROWS, LEN), F32)
    for at, code in enumerate(codes):
        tile = jnp.where(row == at, code, tile)
    return tile.astype(jnp.int32)


def store_packed(ref, states):
    codes = []
    for h, state in enumerate(states):
        words, code = encode(state)
        ref[0, h * HALF:(h + 1) * HALF, :] = words
        codes.append(code)
    at = len(states) * HALF
    ref[0, at:at + CODE_ROWS, :] = code_tile(codes)


def load_steps(ref, heads):
    codes = ref[0, heads * HALF:heads * HALF + CODE_ROWS, :].astype(F32)
    return step_of(codes)


class Plan(NamedTuple):
    group: int
    per_device: int
    per_peer: int

    @staticmethod
    def build(order, owner, slot, tokens, me):
        return jnp.concatenate([order, owner, slot, tokens, me.reshape(1)]).astype(jnp.int32)

    def me(self, flat):
        return flat[4 * self.group]

    def peer(self, flat, away):
        return jnp.bitwise_xor(self.me(flat), away)

    def number(self, flat, away, i):
        return flat[self.peer(flat, away) * self.per_device + self.me(flat) * self.per_peer + i]

    def local(self, flat, away, i):
        return self.number(flat, away, i) - self.me(flat) * self.per_device

    def shard(self, flat, away, i):
        return jnp.bitwise_xor(flat[self.group + self.number(flat, away, i)], self.me(flat))

    def row(self, flat, away, i):
        return flat[2 * self.group + self.number(flat, away, i)]

    def tokens(self, flat, away, i):
        return flat[3 * self.group + self.number(flat, away, i)]

    def tokens_here(self, flat, e):
        return flat[3 * self.group + self.me(flat) * self.per_device + e]


def pack_kernel(state_ref, *out_refs):
    heads = state_ref.shape[1] // len(out_refs)
    for part, out_ref in enumerate(out_refs):
        store_packed(out_ref, [state_ref[0, part * heads + h] for h in range(heads)])


def pack_parents(parents):
    count, heads = parents.shape[:2]
    rows = heads // PARTS * HALF + CODE_ROWS
    return pl.pallas_call(
        pack_kernel,
        grid=(count,),
        in_specs=[pl.BlockSpec((1, heads, LEN, LEN), lambda i: (i, 0, 0, 0))],
        out_specs=[pl.BlockSpec((1, rows, LEN), lambda i: (i, 0, 0))] * PARTS,
        out_shape=[jax.ShapeDtypeStruct((count, rows, LEN), jnp.int32)] * PARTS,
        compiler_params=pltpu.CompilerParams(vmem_limit_bytes=VMEM_LIMIT),
    )(parents)


def block_diag(x, mask):
    return jnp.where(mask, jnp.concatenate([x, x], axis=0), jnp.zeros((), x.dtype))


def live_rates(rates, tokens):
    return jnp.where(iota(rates.shape, 1) < tokens, rates, 0.0).astype(BF16)


def pair_kernel(part, first, plan, flat, q_ref, k_ref, rate_ref, *refs):
    inv_ref, am_ref = refs[-2:]
    expansions, key_heads = q_ref.shape[:2]
    heads = 2 * key_heads
    all_heads = rate_ref.shape[1] // 2
    row = iota((LEN, LEN), 0)
    col = iota((LEN, LEN), 1)
    incl = row >= col
    strict = row > col
    diag_mask = row == col
    prow = iota((HALF, LEN), 0)
    plane = iota((HALF, LEN), 1)
    pcol = jnp.bitwise_and(plane, HALF - 1)
    left = plane < HALF
    bd_mask = (row < HALF) == (col < HALF)
    eye = (prow == pcol).astype(F32)

    def same(size):
        return (prow // size) == (pcol // size)

    base_mask = same(8)
    off_masks = [jnp.logical_and(same(2 * s), jnp.logical_not(same(s))) for s in (8, 16, 32)]
    lower_ones = incl.astype(F32).astype(BF16)
    unit = diag_mask.astype(F32).astype(BF16)

    a_full, where_at = [], []
    for e in range(expansions):
        number = (first + pl.program_id(0)) * expansions + e
        rates = live_rates(rate_ref[e], plan.tokens_here(flat, number))
        cols = dot_nt(jnp.concatenate([lower_ones, unit], axis=0), rates)
        g_cols = cols[:LEN]
        b_cols = cols[LEN:]
        g_rows = dot_nt(rates, lower_ones)
        for m in range(key_heads):
            k = k_ref[e, m]
            gram = dot_nt(jnp.concatenate([q_ref[e, m], k], axis=0), k)
            qk, kk = gram[:LEN], gram[LEN:]
            diagonal = jnp.where(diag_mask, kk, 0.0)
            norm_row = lax.rsqrt(jnp.sum(diagonal, axis=0, keepdims=True) + EPS)
            norm_col = lax.rsqrt(jnp.sum(diagonal, axis=1, keepdims=True) + EPS)
            qk = qk * norm_row
            kk = kk * norm_row
            for r in range(2):
                h = 2 * m + r
                at = part * heads + h
                g_c = g_cols[:, at:at + 1]
                g_r = g_rows[at:at + 1, :]
                pair = jnp.exp(jnp.where(incl, g_c - g_r, -1e4))
                mix = qk * pair
                b_c = b_cols[:, all_heads + at:all_heads + at + 1]
                lower = jnp.where(strict, kk * pair, 0.0) * (b_c * norm_col)
                lower_h, lower_l = split(lower)
                mix_h, mix_l = split(mix)
                am_ref[e, h, :LEN, :LEN] = lower_h
                am_ref[e, h, :LEN, LEN:] = lower_l
                am_ref[e, h, LEN:, :LEN] = mix_h
                am_ref[e, h, LEN:, LEN:] = mix_l
                a_full.append(lower)
                where_at.append((e, h))

    chains = range(len(a_full))
    packed = [jnp.where(left, a_full[c][:HALF], a_full[c][HALF:]) for c in chains]
    base = [jnp.where(base_mask, packed[c], 0.0) for c in chains]
    base_h = [base[c].astype(BF16) for c in chains]
    power = [dot(base_h[c], block_diag(base_h[c], bd_mask)).astype(BF16) for c in chains]
    x = [eye - base[c] for c in chains]
    both = [
        dot(jnp.concatenate([x[c].astype(BF16), power[c]], axis=0), block_diag(power[c], bd_mask))
        for c in chains
    ]
    x = [x[c] + both[c][:HALF] for c in chains]
    power = [both[c][HALF:].astype(BF16) for c in chains]
    x = [x[c] + dot(x[c].astype(BF16), block_diag(power[c], bd_mask)) for c in chains]
    for off in off_masks:
        x_h = [x[c].astype(BF16) for c in chains]
        t = [
            dot(jnp.where(off, packed[c], 0.0).astype(BF16), block_diag(x_h[c], bd_mask)).astype(BF16)
            for c in chains
        ]
        x = [x[c] - dot(x_h[c], block_diag(t[c], bd_mask)) for c in chains]
    x_h = [x[c].astype(BF16) for c in chains]
    t = [
        dot(jnp.where(left, a_full[c][HALF:], 0.0).astype(BF16), block_diag(x_h[c], bd_mask)).astype(BF16)
        for c in chains
    ]
    zero_h = jnp.zeros((HALF, LEN), BF16)
    corner = [dot(jnp.where(left, zero_h, x_h[c]), jnp.concatenate([t[c], t[c]], axis=0)) for c in chains]
    for c in chains:
        e, h = where_at[c]
        inv_ref[e, h, :HALF, :] = jnp.where(left, x[c], 0.0).astype(BF16)
        inv_ref[e, h, HALF:, :] = jnp.where(left, -corner[c], x[c]).astype(BF16)


def pair_parts(part, half, plan, flat, q, k, rates, earlier=None):
    count, all_key_heads = q.shape[:2]
    key_heads = all_key_heads // PARTS
    heads = 2 * key_heads
    block = TOGETHER
    turns = count // block // 2
    first = half * turns
    head_block = pl.BlockSpec((block, key_heads, LEN, LEN), lambda i, t: (first + i, part, 0, 0))
    in_specs = [
        head_block,
        head_block,
        pl.BlockSpec((block,) + rates.shape[1:], lambda i, t: (first + i, 0, 0)),
    ]
    operands = [q, k, rates]
    aliases = {}
    if earlier is not None:
        in_specs += [pl.BlockSpec(memory_space=pl.ANY)] * 2
        aliases = {4: 0, 5: 1}
        operands += list(earlier)
    return pl.pallas_call(
        functools.partial(pair_kernel, part, first, plan),
        grid_spec=pltpu.PrefetchScalarGridSpec(
            num_scalar_prefetch=1,
            grid=(turns,),
            in_specs=in_specs,
            out_specs=[
                pl.BlockSpec((block, heads, LEN, LEN), lambda i, t: (first + i, 0, 0, 0)),
                pl.BlockSpec((block, heads, 2 * LEN, 2 * LEN), lambda i, t: (first + i, 0, 0, 0)),
            ],
        ),
        out_shape=[
            jax.ShapeDtypeStruct((count, heads, LEN, LEN), BF16),
            jax.ShapeDtypeStruct((count, heads, 2 * LEN, 2 * LEN), BF16),
        ],
        input_output_aliases=aliases,
        compiler_params=pltpu.CompilerParams(vmem_limit_bytes=VMEM_LIMIT),
        cost_estimate=pl.CostEstimate(flops=1000, bytes_accessed=1000, transcendentals=0),
    )(flat, *operands)


def turn_of(aways, each, turn):
    if len(aways) == 1:
        return aways[0], turn
    number = turn // each
    away = aways[-1]
    for at in reversed(range(len(aways) - 1)):
        away = jnp.where(number == at, aways[at], away)
    return away, turn - number * each


def state_kernel(part, aways, plan, shards_held, together, flat, gain_ref, *refs):
    per = 6
    inputs = [refs[per * e:per * (e + 1)] for e in range(together)]
    parents = refs[per * together:per * together + shards_held]
    states_in, mixed_out, arrivals, leaving = refs[-4:]
    mixed_hbm, *state_refs = refs[-5 - len(aways):-4]
    turn, turns = pl.program_id(0), pl.num_programs(0)
    each = plan.per_peer // together
    key_heads = inputs[0][0].shape[1]
    heads = 2 * key_heads
    all_heads = inputs[0][3].shape[1] // 2

    def fetch(i, slot):
        for e in range(together):
            away, at = turn_of(aways, each, i)
            shard = plan.shard(flat, away, at * together + e)
            for off in range(shards_held):
                @pl.when(shard == off)
                def _():
                    pltpu.make_async_copy(
                        parents[off].at[plan.row(flat, away, at * together + e)],
                        states_in.at[slot, e],
                        arrivals.at[slot, e],
                    ).start()

    def leave(i, slot, e):
        away, at = turn_of(aways, each, i)
        return pltpu.make_async_copy(
            mixed_out.at[slot, e],
            mixed_hbm.at[plan.local(flat, away, at * together + e), pl.ds(part * key_heads, key_heads)],
            leaving.at[slot, e],
        )

    slot = lax.rem(turn, 2)
    my_away, my_turn = turn_of(aways, each, turn)

    @pl.when(turn == 0)
    def _():
        fetch(0, 0)

    @pl.when(turn + 1 < turns)
    def _():
        fetch(turn + 1, lax.rem(turn + 1, 2))

    for e in range(together):
        pltpu.make_async_copy(parents[0].at[0], states_in.at[slot, e], arrivals.at[slot, e]).wait()

    @pl.when(turn >= 2)
    def _():
        for e in range(together):
            leave(turn - 2, slot, e).wait()

    row = iota((LEN, LEN), 0)
    col = iota((LEN, LEN), 1)
    lower_ones = (row >= col).astype(F32).astype(BF16)
    unit = (row == col).astype(F32).astype(BF16)
    gain = gain_ref[...].astype(F32)

    state, products, n_cols, g_cols, b_cols, eg_cols, steps = [], [], [], [], [], [], []
    for e in range(together):
        q_ref, k_ref, v_ref, rate_ref, inv_ref, am_ref = inputs[e]
        rates = live_rates(rate_ref[0], plan.tokens(flat, my_away, my_turn * together + e))
        cols = dot_nt(jnp.concatenate([lower_ones, unit], axis=0), rates)
        g_cols.append(cols[:LEN])
        b_cols.append(cols[LEN:])
        eg_cols.append(jnp.exp(cols[:LEN]))
        steps.append(load_steps(states_in.at[slot, pl.ds(e, 1)], heads))
        for m in range(key_heads):
            highs, lows = [], []
            for r in range(2):
                h = 2 * m + r
                whole = decode(states_in[slot, e, h * HALF:(h + 1) * HALF, :])
                high, low = split(whole)
                highs.append(high)
                lows.append(low)
                state.append(whole)
            rhs = jnp.concatenate(
                [jnp.concatenate(highs, axis=1), jnp.concatenate(lows, axis=1)], axis=0
            )
            lhs = jnp.concatenate([q_ref[0, m], k_ref[0, m]], axis=0)
            products.append(dot(jnp.concatenate([lhs, lhs], axis=1), rhs))
            keys = k_ref[0, m].astype(F32)
            n_cols.append(lax.rsqrt(jnp.sum(keys * keys, axis=1, keepdims=True) + EPS))

    every = [(e, h) for e in range(together) for h in range(heads)]

    def at_of(h):
        return part * heads + h

    def decay_at(e, h):
        return eg_cols[e][:, at_of(h):at_of(h) + 1]

    def product_at(e, h):
        lane = (h % 2) * LEN
        return products[e * key_heads + h // 2][:, lane:lane + LEN]

    right, first = [], []
    for e, h in every:
        v_ref, inv_ref = inputs[e][2], inputs[e][4]
        ks = product_at(e, h)[LEN:] * steps[e][h:h + 1, :]
        rate = b_cols[e][:, all_heads + at_of(h):all_heads + at_of(h) + 1]
        scale = decay_at(e, h) * n_cols[e * key_heads + h // 2]
        want = rate * (v_ref[0, h // 2, h % 2].astype(F32) - scale * ks)
        right.append(want)
        first.append(dot(inv_ref[0, h], want.astype(BF16)).astype(BF16))
    am_v = [
        dot(inputs[e][5][0, h], jnp.concatenate([first[c], first[c]], axis=0))
        for c, (e, h) in enumerate(every)
    ]
    delta = [
        dot(inputs[e][4][0, h], (right[c] - first[c].astype(F32) - am_v[c][:LEN]).astype(BF16))
        for c, (e, h) in enumerate(every)
    ]
    scaled = []
    for c, (e, h) in enumerate(every):
        g_c = g_cols[e][:, at_of(h):at_of(h) + 1]
        tail = jnp.exp(g_c[LEN - 1:LEN, :] - g_c) * n_cols[e * key_heads + h // 2]
        scaled.append(split(tail * (first[c].astype(F32) + delta[c])))
    finals = []
    for e in range(together):
        for m in range(key_heads):
            turned = jnp.transpose(inputs[e][1][0, m])
            c = e * heads + 2 * m
            rhs = jnp.concatenate(
                [jnp.concatenate([scaled[c][p], scaled[c + 1][p]], axis=1) for p in range(2)], axis=0
            )
            added = dot(jnp.concatenate([turned, turned], axis=1), rhs)
            for r in range(2):
                h = 2 * m + r
                keep = decay_at(e, h)[LEN - 1:LEN, :] * steps[e][h:h + 1, :]
                finals.append(keep * state[c + r] + added[:, r * LEN:(r + 1) * LEN])
    for c, (e, h) in enumerate(every):
        qs = product_at(e, h)[:LEN] * steps[e][h:h + 1, :]
        out = decay_at(e, h) * qs + am_v[c][LEN:]
        out = out + dot(inputs[e][5][0, h, LEN:, :LEN], delta[c].astype(BF16))
        mean_square = jnp.mean(out * out, axis=1, keepdims=True)
        live = iota((LEN, 1), 0) < plan.tokens(flat, my_away, my_turn * together + e)
        scale = jnp.where(live, lax.rsqrt(mean_square + EPS), 0.0)
        mixed_out[slot, e, h // 2, h % 2] = (out * scale * gain).astype(BF16)
    for e in range(together):
        leave(turn, slot, e).start()

    def store(ref, away):
        for e in range(together):
            mine = finals[e * heads:(e + 1) * heads]
            if away:
                store_packed(ref.at[pl.ds(e, 1)], mine)
            else:
                for h in range(heads):
                    ref[e, h] = mine[h]

    for number, away in enumerate(aways):
        if len(aways) == 1:
            store(state_refs[0], away)
        else:
            pl.when(turn // each == number)(functools.partial(store, state_refs[number], away))

    @pl.when(turn == turns - 1)
    def _():
        for e in range(together):
            leave(turn, slot, e).wait()

    @pl.when(jnp.logical_and(turn == turns - 1, turn >= 1))
    def _():
        for e in range(together):
            leave(turn - 1, 1 - slot, e).wait()


def recurrence(part, aways, plan, flat, q, k, v, rates, pairs, parents, gain, mixed, final_shape, final):
    count = plan.per_peer
    together = min(TOGETHER, count)
    turns = count // together
    key_heads = q.shape[1] // PARTS
    heads = 2 * key_heads
    rows = heads * HALF + CODE_ROWS
    in_specs = [pl.BlockSpec((1, LEN), lambda i, t: (0, 0))]
    operands = [gain]

    def one(shape, e, at):
        def index(i, t):
            away, turn = turn_of(aways, turns, i)
            return (plan.local(t, away, turn * together + e), at) + (0,) * (len(shape) - 2)

        return pl.BlockSpec(shape, index)

    for e in range(together):
        in_specs += [
            one((1, key_heads, LEN, LEN), e, part),
            one((1, key_heads, LEN, LEN), e, part),
            one((1, key_heads, 2, LEN, LEN), e, part),
            one((1,) + rates.shape[1:], e, 0),
            one((1, heads, LEN, LEN), e, 0),
            one((1, heads, 2 * LEN, 2 * LEN), e, 0),
        ]
        operands += [q, k, v, rates, *pairs]
    in_specs += [pl.BlockSpec(memory_space=pl.ANY)] * len(parents)
    operands += parents
    aliases = {}
    if mixed is not None:
        in_specs.append(pl.BlockSpec(memory_space=pl.ANY))
        aliases[1 + len(operands)] = 0
        operands.append(mixed)
    mixed_spec = pl.BlockSpec(memory_space=pl.ANY)
    mixed_shape = jax.ShapeDtypeStruct(v.shape, BF16)
    state_specs, state_shapes = [], []

    def turn_in(number, i):
        return i if len(aways) == 1 else jnp.clip(i - number * turns, 0, turns - 1)

    for number, away in enumerate(aways):
        if away:
            state_specs.append(
                pl.BlockSpec((together, rows, LEN), lambda i, t, n=number: (turn_in(n, i), 0, 0))
            )
            state_shapes.append(jax.ShapeDtypeStruct((count, rows, LEN), jnp.int32))
        else:
            if final is not None:
                in_specs.append(pl.BlockSpec(memory_space=pl.ANY))
                aliases[1 + len(operands)] = 1 + number
                operands.append(final)
            state_specs.append(
                pl.BlockSpec(
                    (together, heads, LEN, LEN),
                    lambda i, t, n=number: (plan.me(t) * turns + turn_in(n, i), part, 0, 0),
                )
            )
            state_shapes.append(jax.ShapeDtypeStruct(final_shape, F32))
    return pl.pallas_call(
        functools.partial(state_kernel, part, aways, plan, len(parents), together),
        grid_spec=pltpu.PrefetchScalarGridSpec(
            num_scalar_prefetch=1,
            grid=(turns * len(aways),),
            in_specs=in_specs,
            out_specs=[mixed_spec, *state_specs],
            scratch_shapes=[
                pltpu.VMEM((2, together, rows, LEN), jnp.int32),
                pltpu.VMEM((2, together, key_heads, 2, LEN, LEN), BF16),
                pltpu.SemaphoreType.DMA((2, together)),
                pltpu.SemaphoreType.DMA((2, together)),
            ],
        ),
        out_shape=[mixed_shape, *state_shapes],
        input_output_aliases=aliases,
        compiler_params=pltpu.CompilerParams(vmem_limit_bytes=VMEM_LIMIT),
        cost_estimate=pl.CostEstimate(flops=1000, bytes_accessed=1000, transcendentals=0),
    )(flat, *operands)


def unpack_kernel(turns, flat, *refs):
    *packed_refs, old_ref, out_ref = refs
    count, heads = out_ref.shape[:2]

    def unpack(ref):
        for e in range(count):
            steps = load_steps(ref.at[pl.ds(e, 1)], heads)
            for h in range(heads):
                out_ref[e, h] = decode(ref[e, h * HALF:(h + 1) * HALF, :]) * steps[h:h + 1, :]

    for number, ref in enumerate(packed_refs):
        if len(packed_refs) == 1:
            unpack(ref)
        else:
            pl.when(pl.program_id(0) // turns == number)(functools.partial(unpack, ref))


def unpack_states(part, aways, plan, flat, packed, final):
    count, rows = packed[0].shape[:2]
    heads = final.shape[1] // PARTS
    block = max(1, count // 2)
    turns = count // block

    def place(i, t):
        away, turn = turn_of(aways, turns, i)
        return (plan.peer(t, away) * turns + turn, part, 0, 0)

    def turn_in(number, i):
        return i if len(aways) == 1 else jnp.clip(i - number * turns, 0, turns - 1)

    return pl.pallas_call(
        functools.partial(unpack_kernel, turns),
        grid_spec=pltpu.PrefetchScalarGridSpec(
            num_scalar_prefetch=1,
            grid=(turns * len(aways),),
            in_specs=[
                pl.BlockSpec((block, rows, LEN), lambda i, t, n=number: (turn_in(n, i), 0, 0))
                for number in range(len(aways))
            ]
            + [pl.BlockSpec(memory_space=pl.ANY)],
            out_specs=pl.BlockSpec((block, heads, LEN, LEN), place),
        ),
        out_shape=jax.ShapeDtypeStruct(final.shape, F32),
        input_output_aliases={1 + len(aways): 0},
        compiler_params=pltpu.CompilerParams(vmem_limit_bytes=VMEM_LIMIT),
        cost_estimate=pl.CostEstimate(flops=1000, bytes_accessed=1000, transcendentals=0),
    )(flat, *packed, final)


def turn_kernel(mixed_ref, out_ref):
    key_heads, pair, length, size = mixed_ref.shape[1:]
    out_ref[0] = jnp.swapaxes(mixed_ref[0].reshape(key_heads * pair, length, size), 0, 1)


def turn_mixed(mixed):
    count, key_heads, pair, length, size = mixed.shape
    heads = key_heads * pair
    return pl.pallas_call(
        turn_kernel,
        grid=(count,),
        in_specs=[pl.BlockSpec((1, key_heads, pair, length, size), lambda i: (i, 0, 0, 0, 0))],
        out_specs=pl.BlockSpec((1, length, heads, size), lambda i: (i, 0, 0, 0)),
        out_shape=jax.ShapeDtypeStruct((count, length, heads, size), mixed.dtype),
        compiler_params=pltpu.CompilerParams(vmem_limit_bytes=VMEM_LIMIT),
        cost_estimate=pl.CostEstimate(flops=1000, bytes_accessed=1000, transcendentals=0),
    )(mixed)


def shards(
    queries,
    keys,
    values,
    log_decay,
    write_rate,
    norm_gain,
    parent_cache,
    order,
    parent_owner,
    parent_slot,
    token_count,
):
    seq_count = lax.axis_size("seq")
    me = lax.axis_index("seq")
    per_device, length, key_heads, key_dim = queries.shape
    per_peer = per_device // seq_count
    cache_rows = parent_cache.shape[0]
    heads = 2 * key_heads

    parents = parent_cache.reshape((cache_rows, heads, key_dim, key_dim))
    own = list(pack_parents(parents))

    def swap(tensor, off):
        return lax.ppermute(tensor, "seq", [(i, i ^ off) for i in range(seq_count)])

    def spread(held, off):
        while off:
            held = {**held, **{at ^ off: swap(held[at], off) for at in held}}
            off //= 2
        return held

    half_way = seq_count // 2
    far = swap(own[0], half_way)
    q = jnp.transpose(queries, (0, 2, 1, 3))
    k = jnp.transpose(keys, (0, 2, 1, 3))
    v = jnp.transpose(values, (0, 2, 3, 1, 4))

    def rows_of(tensor):
        return jnp.transpose(tensor, (0, 2, 3, 1)).reshape(per_device, heads, length).astype(F32)

    rates = jnp.concatenate([rows_of(log_decay), rows_of(write_rate)], axis=1)
    gain = norm_gain.reshape(1, -1)
    plan = Plan(order.shape[0], per_device, per_peer)
    flat = Plan.build(order, parent_owner, parent_slot, token_count, me)

    own[0], q = lax.optimization_barrier((own[0], q))
    q, k, v, rates, gain, flat = lax.optimization_barrier((q, k, v, rates, gain, flat))

    pairs = [pair_parts(0, 0, plan, flat, q, k, rates), None]
    pairs[0], far, own[1] = lax.optimization_barrier((pairs[0], far, own[1]))
    held_0 = spread({0: own[0], half_way: far}, half_way // 2)
    far_1 = swap(own[1], half_way)
    pairs[0] = pair_parts(0, 1, plan, flat, q, k, rates, pairs[0])
    rates, pairs[0] = lax.optimization_barrier((rates, pairs[0]))
    pairs[1] = pair_parts(1, 0, plan, flat, q, k, rates)
    pairs, held_0, far_1, own = lax.optimization_barrier((pairs, held_0, far_1, own))
    held_1 = spread({0: own[1], half_way: far_1}, half_way // 2)
    gathered = [[held[at] for at in range(seq_count)] for held in (held_0, held_1)]

    final_shape = (per_device, heads, key_dim, key_dim)
    crossing = list(reversed(range(half_way, seq_count)))
    near = list(reversed(range(1, half_way)))
    mixed, final = None, None
    arrived = {}

    def work(part, aways, mixed, final):
        mixed, *states = recurrence(
            part, aways, plan, flat, q, k, v, rates, pairs[part], gathered[part], gain, mixed, final_shape, final
        )
        for away, state in zip(aways, states):
            if away:
                arrived[part, away] = swap(state, away)
            else:
                final = state
        return mixed, final

    def gone(mixed, aways):
        for away in aways:
            mixed, arrived[0, away] = lax.optimization_barrier((mixed, arrived[0, away]))
        return mixed

    for away in crossing:
        mixed, final = work(0, [away], mixed, final)
    rates, mixed, pairs[1] = lax.optimization_barrier((rates, mixed, pairs[1]))
    pairs[1] = pair_parts(1, 1, plan, flat, q, k, rates, pairs[1])
    held_back = []
    for away in near:
        mixed, state = recurrence(
            0, [away], plan, flat, q, k, v, rates, pairs[0], gathered[0], gain, mixed, final_shape, final
        )
        held_back.append(state)
    mixed, pairs[1], gathered[1], held_back = lax.optimization_barrier((mixed, pairs[1], gathered[1], held_back))
    for away, state in zip(near, held_back):
        arrived[0, away] = swap(state, away)
    mixed = gone(mixed, crossing[:1])
    for away in near + crossing:
        mixed, final = work(1, [away], mixed, final)
    mixed = gone(mixed, crossing[1:])
    for part in range(PARTS):
        mixed, final = work(part, [0], mixed, final)
    away_first = crossing + near
    final = unpack_states(0, away_first, plan, flat, [arrived[0, away] for away in away_first], final)
    for away in near + crossing:
        final = unpack_states(1, [away], plan, flat, [arrived[1, away]], final)
    mixed_out = turn_mixed(mixed).reshape(values.shape)
    final_out = final.reshape((per_device, key_heads, 2, key_dim, key_dim))
    return (mixed_out, final_out)


def solution(mesh):
    placed = (
        P(("groups", "seq"), None, ("head", "sub"), None),
        P(("groups", "seq"), None, ("head", "sub"), None),
        P(("groups", "seq"), None, ("head", "sub"), None, None),
        P(("groups", "seq"), None, ("head", "sub"), None),
        P(("groups", "seq"), None, ("head", "sub"), None),
        P(),
        P(("groups", "seq"), ("head", "sub"), None, None, None),
        P("groups"),
        P("groups"),
        P("groups"),
        P("groups"),
    )
    return jax.shard_map(
        shards,
        mesh=mesh,
        in_specs=placed,
        out_specs=(
            P(("groups", "seq"), None, ("head", "sub"), None, None),
            P(("groups", "seq"), ("head", "sub"), None, None, None),
        ),
        check_vma=False,
    )
```

```python
import functools
from typing import NamedTuple

import jax
import jax.numpy as jnp
from jax import lax
from jax.experimental import pallas as pl
from jax.experimental.pallas import tpu as pltpu
from jax.sharding import PartitionSpec as P

F32 = jnp.float32
BF16 = jnp.bfloat16
HALF = 64
LEN = 128
EPS = 1e-06
TOP = 32512.0
BIAS = 32768.0
CODE = 64.0
VMEM_LIMIT = 8 * 1024 * 1024
PARTS = 2
CODE_ROWS = 8
TOGETHER = 2


def dot(a, b):
    return jnp.dot(a, b, preferred_element_type=F32)


def dot_nt(a, b):
    return lax.dot_general(a, b, (((1,), (1,)), ((), ())), preferred_element_type=F32)


def split(x):
    high = x.astype(BF16)
    return high, (x - high.astype(F32)).astype(BF16)


def iota(shape, dim):
    return lax.broadcasted_iota(jnp.int32, shape, dim)


def step_of(code):
    return jnp.exp2(code * (1.0 / CODE)) * (1.0 / TOP)


def encode(x):
    peak = jnp.maximum(jnp.max(jnp.abs(x), axis=0, keepdims=True), 1e-30)
    code = jnp.ceil(jnp.log2(peak) * CODE) + 1.0
    inverse_step = 1.0 / step_of(code)
    whole = (x * inverse_step + (BIAS + 0.5)).astype(jnp.int32)
    words = jnp.bitwise_or(lax.shift_left(whole[:HALF], 16), whole[HALF:])
    return words, code


def decode(words):
    top = lax.shift_right_logical(words, 16)
    bottom = jnp.bitwise_and(words, 0xFFFF)
    return jnp.concatenate([top, bottom], axis=0).astype(F32) - BIAS


def code_tile(codes):
    row = iota((CODE_ROWS, LEN), 0)
    tile = jnp.zeros((CODE_ROWS, LEN), F32)
    for at, code in enumerate(codes):
        tile = jnp.where(row == at, code, tile)
    return tile.astype(jnp.int32)


def store_packed(ref, states):
    codes = []
    for h, state in enumerate(states):
        words, code = encode(state)
        ref[0, h * HALF:(h + 1) * HALF, :] = words
        codes.append(code)
    at = len(states) * HALF
    ref[0, at:at + CODE_ROWS, :] = code_tile(codes)


def load_steps(ref, heads):
    codes = ref[0, heads * HALF:heads * HALF + CODE_ROWS, :].astype(F32)
    return step_of(codes)


class Plan(NamedTuple):
    group: int
    per_device: int
    per_peer: int

    @staticmethod
    def build(order, owner, slot, tokens, me):
        return jnp.concatenate([order, owner, slot, tokens, me.reshape(1)]).astype(jnp.int32)

    def me(self, flat):
        return flat[4 * self.group]

    def peer(self, flat, away):
        return jnp.bitwise_xor(self.me(flat), away)

    def number(self, flat, away, i):
        return flat[self.peer(flat, away) * self.per_device + self.me(flat) * self.per_peer + i]

    def local(self, flat, away, i):
        return self.number(flat, away, i) - self.me(flat) * self.per_device

    def shard(self, flat, away, i):
        return jnp.bitwise_xor(flat[self.group + self.number(flat, away, i)], self.me(flat))

    def row(self, flat, away, i):
        return flat[2 * self.group + self.number(flat, away, i)]

    def tokens(self, flat, away, i):
        return flat[3 * self.group + self.number(flat, away, i)]

    def tokens_here(self, flat, e):
        return flat[3 * self.group + self.me(flat) * self.per_device + e]


def pack_kernel(state_ref, *out_refs):
    heads = state_ref.shape[1] // len(out_refs)
    for part, out_ref in enumerate(out_refs):
        store_packed(out_ref, [state_ref[0, part * heads + h] for h in range(heads)])


def pack_parents(parents):
    count, heads = parents.shape[:2]
    rows = heads // PARTS * HALF + CODE_ROWS
    return pl.pallas_call(
        pack_kernel,
        grid=(count,),
        in_specs=[pl.BlockSpec((1, heads, LEN, LEN), lambda i: (i, 0, 0, 0))],
        out_specs=[pl.BlockSpec((1, rows, LEN), lambda i: (i, 0, 0))] * PARTS,
        out_shape=[jax.ShapeDtypeStruct((count, rows, LEN), jnp.int32)] * PARTS,
        compiler_params=pltpu.CompilerParams(vmem_limit_bytes=VMEM_LIMIT),
    )(parents)


def block_diag(x, mask):
    return jnp.where(mask, jnp.concatenate([x, x], axis=0), jnp.zeros((), x.dtype))


def live_rates(rates, tokens):
    return jnp.where(iota(rates.shape, 1) < tokens, rates, 0.0).astype(BF16)


def pair_kernel(part, first, plan, flat, q_ref, k_ref, rate_ref, *refs):
    inv_ref, am_ref = refs[-2:]
    expansions, key_heads = q_ref.shape[:2]
    heads = 2 * key_heads
    all_heads = rate_ref.shape[1] // 2
    row = iota((LEN, LEN), 0)
    col = iota((LEN, LEN), 1)
    incl = row >= col
    strict = row > col
    diag_mask = row == col
    prow = iota((HALF, LEN), 0)
    plane = iota((HALF, LEN), 1)
    pcol = jnp.bitwise_and(plane, HALF - 1)
    left = plane < HALF
    bd_mask = (row < HALF) == (col < HALF)
    eye = (prow == pcol).astype(F32)

    def same(size):
        return (prow // size) == (pcol // size)

    base_mask = same(8)
    off_masks = [jnp.logical_and(same(2 * s), jnp.logical_not(same(s))) for s in (8, 16, 32)]
    lower_ones = incl.astype(F32).astype(BF16)
    unit = diag_mask.astype(F32).astype(BF16)

    a_full, where_at = [], []
    for e in range(expansions):
        number = (first + pl.program_id(0)) * expansions + e
        rates = live_rates(rate_ref[e], plan.tokens_here(flat, number))
        cols = dot_nt(jnp.concatenate([lower_ones, unit], axis=0), rates)
        g_cols = cols[:LEN]
        b_cols = cols[LEN:]
        g_rows = dot_nt(rates, lower_ones)
        for m in range(key_heads):
            k = k_ref[e, m]
            gram = dot_nt(jnp.concatenate([q_ref[e, m], k], axis=0), k)
            qk, kk = gram[:LEN], gram[LEN:]
            diagonal = jnp.where(diag_mask, kk, 0.0)
            norm_row = lax.rsqrt(jnp.sum(diagonal, axis=0, keepdims=True) + EPS)
            norm_col = lax.rsqrt(jnp.sum(diagonal, axis=1, keepdims=True) + EPS)
            qk = qk * norm_row
            kk = kk * norm_row
            for r in range(2):
                h = 2 * m + r
                at = part * heads + h
                g_c = g_cols[:, at:at + 1]
                g_r = g_rows[at:at + 1, :]
                pair = jnp.exp(jnp.where(incl, g_c - g_r, -1e4))
                mix = qk * pair
                b_c = b_cols[:, all_heads + at:all_heads + at + 1]
                lower = jnp.where(strict, kk * pair, 0.0) * (b_c * norm_col)
                lower_h, lower_l = split(lower)
                mix_h, mix_l = split(mix)
                am_ref[e, h, :LEN, :LEN] = lower_h
                am_ref[e, h, :LEN, LEN:] = lower_l
                am_ref[e, h, LEN:, :LEN] = mix_h
                am_ref[e, h, LEN:, LEN:] = mix_l
                a_full.append(lower)
                where_at.append((e, h))

    chains = range(len(a_full))
    packed = [jnp.where(left, a_full[c][:HALF], a_full[c][HALF:]) for c in chains]
    base = [jnp.where(base_mask, packed[c], 0.0) for c in chains]
    base_h = [base[c].astype(BF16) for c in chains]
    power = [dot(base_h[c], block_diag(base_h[c], bd_mask)).astype(BF16) for c in chains]
    x = [eye - base[c] for c in chains]
    both = [
        dot(jnp.concatenate([x[c].astype(BF16), power[c]], axis=0), block_diag(power[c], bd_mask))
        for c in chains
    ]
    x = [x[c] + both[c][:HALF] for c in chains]
    power = [both[c][HALF:].astype(BF16) for c in chains]
    x = [x[c] + dot(x[c].astype(BF16), block_diag(power[c], bd_mask)) for c in chains]
    for off in off_masks:
        x_h = [x[c].astype(BF16) for c in chains]
        t = [
            dot(jnp.where(off, packed[c], 0.0).astype(BF16), block_diag(x_h[c], bd_mask)).astype(BF16)
            for c in chains
        ]
        x = [x[c] - dot(x_h[c], block_diag(t[c], bd_mask)) for c in chains]
    x_h = [x[c].astype(BF16) for c in chains]
    t = [
        dot(jnp.where(left, a_full[c][HALF:], 0.0).astype(BF16), block_diag(x_h[c], bd_mask)).astype(BF16)
        for c in chains
    ]
    zero_h = jnp.zeros((HALF, LEN), BF16)
    corner = [dot(jnp.where(left, zero_h, x_h[c]), jnp.concatenate([t[c], t[c]], axis=0)) for c in chains]
    for c in chains:
        e, h = where_at[c]
        inv_ref[e, h, :HALF, :] = jnp.where(left, x[c], 0.0).astype(BF16)
        inv_ref[e, h, HALF:, :] = jnp.where(left, -corner[c], x[c]).astype(BF16)


def pair_parts(part, half, plan, flat, q, k, rates, earlier=None):
    count, all_key_heads = q.shape[:2]
    key_heads = all_key_heads // PARTS
    heads = 2 * key_heads
    block = TOGETHER
    turns = count // block // 2
    first = half * turns
    head_block = pl.BlockSpec((block, key_heads, LEN, LEN), lambda i, t: (first + i, part, 0, 0))
    in_specs = [
        head_block,
        head_block,
        pl.BlockSpec((block,) + rates.shape[1:], lambda i, t: (first + i, 0, 0)),
    ]
    operands = [q, k, rates]
    aliases = {}
    if earlier is not None:
        in_specs += [pl.BlockSpec(memory_space=pl.ANY)] * 2
        aliases = {4: 0, 5: 1}
        operands += list(earlier)
    return pl.pallas_call(
        functools.partial(pair_kernel, part, first, plan),
        grid_spec=pltpu.PrefetchScalarGridSpec(
            num_scalar_prefetch=1,
            grid=(turns,),
            in_specs=in_specs,
            out_specs=[
                pl.BlockSpec((block, heads, LEN, LEN), lambda i, t: (first + i, 0, 0, 0)),
                pl.BlockSpec((block, heads, 2 * LEN, 2 * LEN), lambda i, t: (first + i, 0, 0, 0)),
            ],
        ),
        out_shape=[
            jax.ShapeDtypeStruct((count, heads, LEN, LEN), BF16),
            jax.ShapeDtypeStruct((count, heads, 2 * LEN, 2 * LEN), BF16),
        ],
        input_output_aliases=aliases,
        compiler_params=pltpu.CompilerParams(vmem_limit_bytes=VMEM_LIMIT),
        cost_estimate=pl.CostEstimate(flops=1000, bytes_accessed=1000, transcendentals=0),
    )(flat, *operands)


def turn_of(aways, each, turn):
    if len(aways) == 1:
        return aways[0], turn
    number = turn // each
    away = aways[-1]
    for at in reversed(range(len(aways) - 1)):
        away = jnp.where(number == at, aways[at], away)
    return away, turn - number * each


def state_kernel(part, aways, plan, shards_held, together, flat, gain_ref, *refs):
    per = 6
    inputs = [refs[per * e:per * (e + 1)] for e in range(together)]
    parents = refs[per * together:per * together + shards_held]
    states_in, mixed_out, arrivals, leaving = refs[-4:]
    mixed_hbm, *state_refs = refs[-5 - len(aways):-4]
    turn, turns = pl.program_id(0), pl.num_programs(0)
    each = plan.per_peer // together
    key_heads = inputs[0][0].shape[1]
    heads = 2 * key_heads
    all_heads = inputs[0][3].shape[1] // 2

    def fetch(i, slot):
        for e in range(together):
            away, at = turn_of(aways, each, i)
            shard = plan.shard(flat, away, at * together + e)
            for off in range(shards_held):
                @pl.when(shard == off)
                def _():
                    pltpu.make_async_copy(
                        parents[off].at[plan.row(flat, away, at * together + e)],
                        states_in.at[slot, e],
                        arrivals.at[slot, e],
                    ).start()

    def leave(i, slot, e):
        away, at = turn_of(aways, each, i)
        return pltpu.make_async_copy(
            mixed_out.at[slot, e],
            mixed_hbm.at[plan.local(flat, away, at * together + e), pl.ds(part * key_heads, key_heads)],
            leaving.at[slot, e],
        )

    slot = lax.rem(turn, 2)
    my_away, my_turn = turn_of(aways, each, turn)

    @pl.when(turn == 0)
    def _():
        fetch(0, 0)

    @pl.when(turn + 1 < turns)
    def _():
        fetch(turn + 1, lax.rem(turn + 1, 2))

    for e in range(together):
        pltpu.make_async_copy(parents[0].at[0], states_in.at[slot, e], arrivals.at[slot, e]).wait()

    @pl.when(turn >= 2)
    def _():
        for e in range(together):
            leave(turn - 2, slot, e).wait()

    row = iota((LEN, LEN), 0)
    col = iota((LEN, LEN), 1)
    lower_ones = (row >= col).astype(F32).astype(BF16)
    unit = (row == col).astype(F32).astype(BF16)
    gain = gain_ref[...].astype(F32)

    state, products, n_cols, g_cols, b_cols, eg_cols, steps = [], [], [], [], [], [], []
    for e in range(together):
        q_ref, k_ref, v_ref, rate_ref, inv_ref, am_ref = inputs[e]
        rates = live_rates(rate_ref[0], plan.tokens(flat, my_away, my_turn * together + e))
        cols = dot_nt(jnp.concatenate([lower_ones, unit], axis=0), rates)
        g_cols.append(cols[:LEN])
        b_cols.append(cols[LEN:])
        eg_cols.append(jnp.exp(cols[:LEN]))
        steps.append(load_steps(states_in.at[slot, pl.ds(e, 1)], heads))
        for m in range(key_heads):
            highs, lows = [], []
            for r in range(2):
                h = 2 * m + r
                whole = decode(states_in[slot, e, h * HALF:(h + 1) * HALF, :])
                high, low = split(whole)
                highs.append(high)
                lows.append(low)
                state.append(whole)
            rhs = jnp.concatenate(
                [jnp.concatenate(highs, axis=1), jnp.concatenate(lows, axis=1)], axis=0
            )
            lhs = jnp.concatenate([q_ref[0, m], k_ref[0, m]], axis=0)
            products.append(dot(jnp.concatenate([lhs, lhs], axis=1), rhs))
            keys = k_ref[0, m].astype(F32)
            n_cols.append(lax.rsqrt(jnp.sum(keys * keys, axis=1, keepdims=True) + EPS))

    every = [(e, h) for e in range(together) for h in range(heads)]

    def at_of(h):
        return part * heads + h

    def decay_at(e, h):
        return eg_cols[e][:, at_of(h):at_of(h) + 1]

    def product_at(e, h):
        lane = (h % 2) * LEN
        return products[e * key_heads + h // 2][:, lane:lane + LEN]

    right, first = [], []
    for e, h in every:
        v_ref, inv_ref = inputs[e][2], inputs[e][4]
        ks = product_at(e, h)[LEN:] * steps[e][h:h + 1, :]
        rate = b_cols[e][:, all_heads + at_of(h):all_heads + at_of(h) + 1]
        scale = decay_at(e, h) * n_cols[e * key_heads + h // 2]
        want = rate * (v_ref[0, h // 2, h % 2].astype(F32) - scale * ks)
        right.append(want)
        first.append(dot(inv_ref[0, h], want.astype(BF16)).astype(BF16))
    am_v = [
        dot(inputs[e][5][0, h], jnp.concatenate([first[c], first[c]], axis=0))
        for c, (e, h) in enumerate(every)
    ]
    delta = [
        dot(inputs[e][4][0, h], (right[c] - first[c].astype(F32) - am_v[c][:LEN]).astype(BF16))
        for c, (e, h) in enumerate(every)
    ]
    scaled = []
    for c, (e, h) in enumerate(every):
        g_c = g_cols[e][:, at_of(h):at_of(h) + 1]
        tail = jnp.exp(g_c[LEN - 1:LEN, :] - g_c) * n_cols[e * key_heads + h // 2]
        scaled.append(split(tail * (first[c].astype(F32) + delta[c])))
    finals = []
    for e in range(together):
        for m in range(key_heads):
            turned = jnp.transpose(inputs[e][1][0, m])
            c = e * heads + 2 * m
            rhs = jnp.concatenate(
                [jnp.concatenate([scaled[c][p], scaled[c + 1][p]], axis=1) for p in range(2)], axis=0
            )
            added = dot(jnp.concatenate([turned, turned], axis=1), rhs)
            for r in range(2):
                h = 2 * m + r
                keep = decay_at(e, h)[LEN - 1:LEN, :] * steps[e][h:h + 1, :]
                finals.append(keep * state[c + r] + added[:, r * LEN:(r + 1) * LEN])
    for c, (e, h) in enumerate(every):
        qs = product_at(e, h)[:LEN] * steps[e][h:h + 1, :]
        out = decay_at(e, h) * qs + am_v[c][LEN:]
        out = out + dot(inputs[e][5][0, h, LEN:, :LEN], delta[c].astype(BF16))
        mean_square = jnp.mean(out * out, axis=1, keepdims=True)
        live = iota((LEN, 1), 0) < plan.tokens(flat, my_away, my_turn * together + e)
        scale = jnp.where(live, lax.rsqrt(mean_square + EPS), 0.0)
        mixed_out[slot, e, h // 2, h % 2] = (out * scale * gain).astype(BF16)
    for e in range(together):
        leave(turn, slot, e).start()

    def store(ref, away):
        for e in range(together):
            mine = finals[e * heads:(e + 1) * heads]
            if away:
                store_packed(ref.at[pl.ds(e, 1)], mine)
            else:
                for h in range(heads):
                    ref[e, h] = mine[h]

    for number, away in enumerate(aways):
        if len(aways) == 1:
            store(state_refs[0], away)
        else:
            pl.when(turn // each == number)(functools.partial(store, state_refs[number], away))

    @pl.when(turn == turns - 1)
    def _():
        for e in range(together):
            leave(turn, slot, e).wait()

    @pl.when(jnp.logical_and(turn == turns - 1, turn >= 1))
    def _():
        for e in range(together):
            leave(turn - 1, 1 - slot, e).wait()


def recurrence(part, aways, plan, flat, q, k, v, rates, pairs, parents, gain, mixed, final_shape, final):
    count = plan.per_peer
    together = min(TOGETHER, count)
    turns = count // together
    key_heads = q.shape[1] // PARTS
    heads = 2 * key_heads
    rows = heads * HALF + CODE_ROWS
    in_specs = [pl.BlockSpec((1, LEN), lambda i, t: (0, 0))]
    operands = [gain]

    def one(shape, e, at):
        def index(i, t):
            away, turn = turn_of(aways, turns, i)
            return (plan.local(t, away, turn * together + e), at) + (0,) * (len(shape) - 2)

        return pl.BlockSpec(shape, index)

    for e in range(together):
        in_specs += [
            one((1, key_heads, LEN, LEN), e, part),
            one((1, key_heads, LEN, LEN), e, part),
            one((1, key_heads, 2, LEN, LEN), e, part),
            one((1,) + rates.shape[1:], e, 0),
            one((1, heads, LEN, LEN), e, 0),
            one((1, heads, 2 * LEN, 2 * LEN), e, 0),
        ]
        operands += [q, k, v, rates, *pairs]
    in_specs += [pl.BlockSpec(memory_space=pl.ANY)] * len(parents)
    operands += parents
    aliases = {}
    if mixed is not None:
        in_specs.append(pl.BlockSpec(memory_space=pl.ANY))
        aliases[1 + len(operands)] = 0
        operands.append(mixed)
    mixed_spec = pl.BlockSpec(memory_space=pl.ANY)
    mixed_shape = jax.ShapeDtypeStruct(v.shape, BF16)
    state_specs, state_shapes = [], []

    def turn_in(number, i):
        return i if len(aways) == 1 else jnp.clip(i - number * turns, 0, turns - 1)

    for number, away in enumerate(aways):
        if away:
            state_specs.append(
                pl.BlockSpec((together, rows, LEN), lambda i, t, n=number: (turn_in(n, i), 0, 0))
            )
            state_shapes.append(jax.ShapeDtypeStruct((count, rows, LEN), jnp.int32))
        else:
            if final is not None:
                in_specs.append(pl.BlockSpec(memory_space=pl.ANY))
                aliases[1 + len(operands)] = 1 + number
                operands.append(final)
            state_specs.append(
                pl.BlockSpec(
                    (together, heads, LEN, LEN),
                    lambda i, t, n=number: (plan.me(t) * turns + turn_in(n, i), part, 0, 0),
                )
            )
            state_shapes.append(jax.ShapeDtypeStruct(final_shape, F32))
    return pl.pallas_call(
        functools.partial(state_kernel, part, aways, plan, len(parents), together),
        grid_spec=pltpu.PrefetchScalarGridSpec(
            num_scalar_prefetch=1,
            grid=(turns * len(aways),),
            in_specs=in_specs,
            out_specs=[mixed_spec, *state_specs],
            scratch_shapes=[
                pltpu.VMEM((2, together, rows, LEN), jnp.int32),
                pltpu.VMEM((2, together, key_heads, 2, LEN, LEN), BF16),
                pltpu.SemaphoreType.DMA((2, together)),
                pltpu.SemaphoreType.DMA((2, together)),
            ],
        ),
        out_shape=[mixed_shape, *state_shapes],
        input_output_aliases=aliases,
        compiler_params=pltpu.CompilerParams(vmem_limit_bytes=VMEM_LIMIT),
        cost_estimate=pl.CostEstimate(flops=1000, bytes_accessed=1000, transcendentals=0),
    )(flat, *operands)


def unpack_kernel(turns, flat, *refs):
    *packed_refs, old_ref, out_ref = refs
    count, heads = out_ref.shape[:2]

    def unpack(ref):
        for e in range(count):
            steps = load_steps(ref.at[pl.ds(e, 1)], heads)
            for h in range(heads):
                out_ref[e, h] = decode(ref[e, h * HALF:(h + 1) * HALF, :]) * steps[h:h + 1, :]

    for number, ref in enumerate(packed_refs):
        if len(packed_refs) == 1:
            unpack(ref)
        else:
            pl.when(pl.program_id(0) // turns == number)(functools.partial(unpack, ref))


def unpack_states(part, aways, plan, flat, packed, final):
    count, rows = packed[0].shape[:2]
    heads = final.shape[1] // PARTS
    block = max(1, count // 2)
    turns = count // block

    def place(i, t):
        away, turn = turn_of(aways, turns, i)
        return (plan.peer(t, away) * turns + turn, part, 0, 0)

    def turn_in(number, i):
        return i if len(aways) == 1 else jnp.clip(i - number * turns, 0, turns - 1)

    return pl.pallas_call(
        functools.partial(unpack_kernel, turns),
        grid_spec=pltpu.PrefetchScalarGridSpec(
            num_scalar_prefetch=1,
            grid=(turns * len(aways),),
            in_specs=[
                pl.BlockSpec((block, rows, LEN), lambda i, t, n=number: (turn_in(n, i), 0, 0))
                for number in range(len(aways))
            ]
            + [pl.BlockSpec(memory_space=pl.ANY)],
            out_specs=pl.BlockSpec((block, heads, LEN, LEN), place),
        ),
        out_shape=jax.ShapeDtypeStruct(final.shape, F32),
        input_output_aliases={1 + len(aways): 0},
        compiler_params=pltpu.CompilerParams(vmem_limit_bytes=VMEM_LIMIT),
        cost_estimate=pl.CostEstimate(flops=1000, bytes_accessed=1000, transcendentals=0),
    )(flat, *packed, final)


def turn_kernel(mixed_ref, out_ref):
    key_heads, pair, length, size = mixed_ref.shape[1:]
    out_ref[0] = jnp.swapaxes(mixed_ref[0].reshape(key_heads * pair, length, size), 0, 1)


def turn_mixed(mixed):
    count, key_heads, pair, length, size = mixed.shape
    heads = key_heads * pair
    return pl.pallas_call(
        turn_kernel,
        grid=(count,),
        in_specs=[pl.BlockSpec((1, key_heads, pair, length, size), lambda i: (i, 0, 0, 0, 0))],
        out_specs=pl.BlockSpec((1, length, heads, size), lambda i: (i, 0, 0, 0)),
        out_shape=jax.ShapeDtypeStruct((count, length, heads, size), mixed.dtype),
        compiler_params=pltpu.CompilerParams(vmem_limit_bytes=VMEM_LIMIT),
        cost_estimate=pl.CostEstimate(flops=1000, bytes_accessed=1000, transcendentals=0),
    )(mixed)


def shards(
    queries,
    keys,
    values,
    log_decay,
    write_rate,
    norm_gain,
    parent_cache,
    order,
    parent_owner,
    parent_slot,
    token_count,
):
    seq_count = lax.axis_size("seq")
    me = lax.axis_index("seq")
    per_device, length, key_heads, key_dim = queries.shape
    per_peer = per_device // seq_count
    cache_rows = parent_cache.shape[0]
    heads = 2 * key_heads

    parents = parent_cache.reshape((cache_rows, heads, key_dim, key_dim))
    own = list(pack_parents(parents))

    def swap(tensor, off):
        return lax.ppermute(tensor, "seq", [(i, i ^ off) for i in range(seq_count)])

    def spread(held, off):
        while off:
            held = {**held, **{at ^ off: swap(held[at], off) for at in held}}
            off //= 2
        return held

    half_way = seq_count // 2
    far = swap(own[0], half_way)
    q = jnp.transpose(queries, (0, 2, 1, 3))
    k = jnp.transpose(keys, (0, 2, 1, 3))
    v = jnp.transpose(values, (0, 2, 3, 1, 4))

    def rows_of(tensor):
        return jnp.transpose(tensor, (0, 2, 3, 1)).reshape(per_device, heads, length).astype(F32)

    rates = jnp.concatenate([rows_of(log_decay), rows_of(write_rate)], axis=1)
    gain = norm_gain.reshape(1, -1)
    plan = Plan(order.shape[0], per_device, per_peer)
    flat = Plan.build(order, parent_owner, parent_slot, token_count, me)

    own[0], q = lax.optimization_barrier((own[0], q))
    q, k, v, rates, gain, flat = lax.optimization_barrier((q, k, v, rates, gain, flat))

    pairs = [pair_parts(0, 0, plan, flat, q, k, rates), None]
    pairs[0], far, own[1] = lax.optimization_barrier((pairs[0], far, own[1]))
    held_0 = spread({0: own[0], half_way: far}, half_way // 2)
    far_1 = swap(own[1], half_way)
    pairs[0] = pair_parts(0, 1, plan, flat, q, k, rates, pairs[0])
    rates, pairs[0] = lax.optimization_barrier((rates, pairs[0]))
    pairs[1] = pair_parts(1, 0, plan, flat, q, k, rates)
    pairs, held_0, far_1, own = lax.optimization_barrier((pairs, held_0, far_1, own))
    held_1 = spread({0: own[1], half_way: far_1}, half_way // 2)
    gathered = [[held[at] for at in range(seq_count)] for held in (held_0, held_1)]

    final_shape = (per_device, heads, key_dim, key_dim)
    crossing = list(reversed(range(half_way, seq_count)))
    near = list(reversed(range(1, half_way)))
    mixed, final = None, None
    arrived = {}

    def work(part, aways, mixed, final):
        mixed, *states = recurrence(
            part, aways, plan, flat, q, k, v, rates, pairs[part], gathered[part], gain, mixed, final_shape, final
        )
        for away, state in zip(aways, states):
            if away:
                arrived[part, away] = swap(state, away)
            else:
                final = state
        return mixed, final

    def gone(mixed, aways):
        for away in aways:
            mixed, arrived[0, away] = lax.optimization_barrier((mixed, arrived[0, away]))
        return mixed

    mixed, final = work(0, crossing[:1], mixed, final)
    held_back = []
    for away in crossing[1:] + near:
        if away == near[0]:
            rates, mixed, pairs[1] = lax.optimization_barrier((rates, mixed, pairs[1]))
            pairs[1] = pair_parts(1, 1, plan, flat, q, k, rates, pairs[1])
        mixed, state = recurrence(
            0, [away], plan, flat, q, k, v, rates, pairs[0], gathered[0], gain, mixed, final_shape, final
        )
        held_back.append(state)
    mixed, pairs[1], gathered[1], held_back = lax.optimization_barrier((mixed, pairs[1], gathered[1], held_back))
    for away, state in zip(crossing[1:] + near, held_back):
        arrived[0, away] = swap(state, away)
    mixed = gone(mixed, crossing[:1])
    for away in near + crossing:
        mixed, final = work(1, [away], mixed, final)
    mixed = gone(mixed, crossing[1:])
    for part in range(PARTS):
        mixed, final = work(part, [0], mixed, final)
    away_first = crossing + near
    final = unpack_states(0, away_first, plan, flat, [arrived[0, away] for away in away_first], final)
    for away in near + crossing:
        final = unpack_states(1, [away], plan, flat, [arrived[1, away]], final)
    mixed_out = turn_mixed(mixed).reshape(values.shape)
    final_out = final.reshape((per_device, key_heads, 2, key_dim, key_dim))
    return (mixed_out, final_out)


def solution(mesh):
    placed = (
        P(("groups", "seq"), None, ("head", "sub"), None),
        P(("groups", "seq"), None, ("head", "sub"), None),
        P(("groups", "seq"), None, ("head", "sub"), None, None),
        P(("groups", "seq"), None, ("head", "sub"), None),
        P(("groups", "seq"), None, ("head", "sub"), None),
        P(),
        P(("groups", "seq"), ("head", "sub"), None, None, None),
        P("groups"),
        P("groups"),
        P("groups"),
        P("groups"),
    )
    return jax.shard_map(
        shards,
        mesh=mesh,
        in_specs=placed,
        out_specs=(
            P(("groups", "seq"), None, ("head", "sub"), None, None),
            P(("groups", "seq"), ("head", "sub"), None, None, None),
        ),
        check_vma=False,
    )
```

```python
import functools
from typing import NamedTuple

import jax
import jax.numpy as jnp
from jax import lax
from jax.experimental import pallas as pl
from jax.experimental.pallas import tpu as pltpu
from jax.sharding import PartitionSpec as P

F32 = jnp.float32
BF16 = jnp.bfloat16
HALF = 64
LEN = 128
EPS = 1e-06
TOP = 32512.0
BIAS = 32768.0
CODE = 64.0
VMEM_LIMIT = 8 * 1024 * 1024
PARTS = 2
CODE_ROWS = 8
TOGETHER = 2


def dot(a, b):
    return jnp.dot(a, b, preferred_element_type=F32)


def dot_nt(a, b):
    return lax.dot_general(a, b, (((1,), (1,)), ((), ())), preferred_element_type=F32)


def split(x):
    high = x.astype(BF16)
    return high, (x - high.astype(F32)).astype(BF16)


def iota(shape, dim):
    return lax.broadcasted_iota(jnp.int32, shape, dim)


def step_of(code):
    return jnp.exp2(code * (1.0 / CODE)) * (1.0 / TOP)


def encode(x):
    peak = jnp.maximum(jnp.max(jnp.abs(x), axis=0, keepdims=True), 1e-30)
    code = jnp.ceil(jnp.log2(peak) * CODE) + 1.0
    inverse_step = 1.0 / step_of(code)
    whole = (x * inverse_step + (BIAS + 0.5)).astype(jnp.int32)
    words = jnp.bitwise_or(lax.shift_left(whole[:HALF], 16), whole[HALF:])
    return words, code


def decode(words):
    top = lax.shift_right_logical(words, 16)
    bottom = jnp.bitwise_and(words, 0xFFFF)
    return jnp.concatenate([top, bottom], axis=0).astype(F32) - BIAS


def code_tile(codes):
    row = iota((CODE_ROWS, LEN), 0)
    tile = jnp.zeros((CODE_ROWS, LEN), F32)
    for at, code in enumerate(codes):
        tile = jnp.where(row == at, code, tile)
    return tile.astype(jnp.int32)


def store_packed(ref, states):
    codes = []
    for h, state in enumerate(states):
        words, code = encode(state)
        ref[0, h * HALF:(h + 1) * HALF, :] = words
        codes.append(code)
    at = len(states) * HALF
    ref[0, at:at + CODE_ROWS, :] = code_tile(codes)


def load_steps(ref, heads):
    codes = ref[0, heads * HALF:heads * HALF + CODE_ROWS, :].astype(F32)
    return step_of(codes)


class Plan(NamedTuple):
    group: int
    per_device: int
    per_peer: int

    @staticmethod
    def build(order, owner, slot, tokens, me):
        return jnp.concatenate([order, owner, slot, tokens, me.reshape(1)]).astype(jnp.int32)

    def me(self, flat):
        return flat[4 * self.group]

    def peer(self, flat, away):
        return jnp.bitwise_xor(self.me(flat), away)

    def number(self, flat, away, i):
        return flat[self.peer(flat, away) * self.per_device + self.me(flat) * self.per_peer + i]

    def local(self, flat, away, i):
        return self.number(flat, away, i) - self.me(flat) * self.per_device

    def shard(self, flat, away, i):
        return jnp.bitwise_xor(flat[self.group + self.number(flat, away, i)], self.me(flat))

    def row(self, flat, away, i):
        return flat[2 * self.group + self.number(flat, away, i)]

    def tokens(self, flat, away, i):
        return flat[3 * self.group + self.number(flat, away, i)]

    def tokens_here(self, flat, e):
        return flat[3 * self.group + self.me(flat) * self.per_device + e]


def pack_kernel(state_ref, *out_refs):
    heads = state_ref.shape[1] // len(out_refs)
    for part, out_ref in enumerate(out_refs):
        store_packed(out_ref, [state_ref[0, part * heads + h] for h in range(heads)])


def pack_parents(parents):
    count, heads = parents.shape[:2]
    rows = heads // PARTS * HALF + CODE_ROWS
    return pl.pallas_call(
        pack_kernel,
        grid=(count,),
        in_specs=[pl.BlockSpec((1, heads, LEN, LEN), lambda i: (i, 0, 0, 0))],
        out_specs=[pl.BlockSpec((1, rows, LEN), lambda i: (i, 0, 0))] * PARTS,
        out_shape=[jax.ShapeDtypeStruct((count, rows, LEN), jnp.int32)] * PARTS,
        compiler_params=pltpu.CompilerParams(vmem_limit_bytes=VMEM_LIMIT),
    )(parents)


def block_diag(x, mask):
    return jnp.where(mask, jnp.concatenate([x, x], axis=0), jnp.zeros((), x.dtype))


def live_rates(rates, tokens):
    return jnp.where(iota(rates.shape, 1) < tokens, rates, 0.0).astype(BF16)


def pair_kernel(part, first, plan, flat, q_ref, k_ref, rate_ref, *refs):
    inv_ref, am_ref = refs[-2:]
    expansions, key_heads = q_ref.shape[:2]
    heads = 2 * key_heads
    all_heads = rate_ref.shape[1] // 2
    row = iota((LEN, LEN), 0)
    col = iota((LEN, LEN), 1)
    incl = row >= col
    strict = row > col
    diag_mask = row == col
    prow = iota((HALF, LEN), 0)
    plane = iota((HALF, LEN), 1)
    pcol = jnp.bitwise_and(plane, HALF - 1)
    left = plane < HALF
    bd_mask = (row < HALF) == (col < HALF)
    eye = (prow == pcol).astype(F32)

    def same(size):
        return (prow // size) == (pcol // size)

    base_mask = same(8)
    off_masks = [jnp.logical_and(same(2 * s), jnp.logical_not(same(s))) for s in (8, 16, 32)]
    lower_ones = incl.astype(F32).astype(BF16)
    unit = diag_mask.astype(F32).astype(BF16)

    a_full, where_at = [], []
    for e in range(expansions):
        number = (first + pl.program_id(0)) * expansions + e
        rates = live_rates(rate_ref[e], plan.tokens_here(flat, number))
        cols = dot_nt(jnp.concatenate([lower_ones, unit], axis=0), rates)
        g_cols = cols[:LEN]
        b_cols = cols[LEN:]
        g_rows = dot_nt(rates, lower_ones)
        for m in range(key_heads):
            k = k_ref[e, m]
            gram = dot_nt(jnp.concatenate([q_ref[e, m], k], axis=0), k)
            qk, kk = gram[:LEN], gram[LEN:]
            diagonal = jnp.where(diag_mask, kk, 0.0)
            norm_row = lax.rsqrt(jnp.sum(diagonal, axis=0, keepdims=True) + EPS)
            norm_col = lax.rsqrt(jnp.sum(diagonal, axis=1, keepdims=True) + EPS)
            qk = qk * norm_row
            kk = kk * norm_row
            for r in range(2):
                h = 2 * m + r
                at = part * heads + h
                g_c = g_cols[:, at:at + 1]
                g_r = g_rows[at:at + 1, :]
                pair = jnp.exp(jnp.where(incl, g_c - g_r, -1e4))
                mix = qk * pair
                b_c = b_cols[:, all_heads + at:all_heads + at + 1]
                lower = jnp.where(strict, kk * pair, 0.0) * (b_c * norm_col)
                lower_h, lower_l = split(lower)
                mix_h, mix_l = split(mix)
                am_ref[e, h, :LEN, :LEN] = lower_h
                am_ref[e, h, :LEN, LEN:] = lower_l
                am_ref[e, h, LEN:, :LEN] = mix_h
                am_ref[e, h, LEN:, LEN:] = mix_l
                a_full.append(lower)
                where_at.append((e, h))

    chains = range(len(a_full))
    packed = [jnp.where(left, a_full[c][:HALF], a_full[c][HALF:]) for c in chains]
    base = [jnp.where(base_mask, packed[c], 0.0) for c in chains]
    base_h = [base[c].astype(BF16) for c in chains]
    power = [dot(base_h[c], block_diag(base_h[c], bd_mask)).astype(BF16) for c in chains]
    x = [eye - base[c] for c in chains]
    both = [
        dot(jnp.concatenate([x[c].astype(BF16), power[c]], axis=0), block_diag(power[c], bd_mask))
        for c in chains
    ]
    x = [x[c] + both[c][:HALF] for c in chains]
    power = [both[c][HALF:].astype(BF16) for c in chains]
    x = [x[c] + dot(x[c].astype(BF16), block_diag(power[c], bd_mask)) for c in chains]
    for off in off_masks:
        x_h = [x[c].astype(BF16) for c in chains]
        t = [
            dot(jnp.where(off, packed[c], 0.0).astype(BF16), block_diag(x_h[c], bd_mask)).astype(BF16)
            for c in chains
        ]
        x = [x[c] - dot(x_h[c], block_diag(t[c], bd_mask)) for c in chains]
    x_h = [x[c].astype(BF16) for c in chains]
    t = [
        dot(jnp.where(left, a_full[c][HALF:], 0.0).astype(BF16), block_diag(x_h[c], bd_mask)).astype(BF16)
        for c in chains
    ]
    zero_h = jnp.zeros((HALF, LEN), BF16)
    corner = [dot(jnp.where(left, zero_h, x_h[c]), jnp.concatenate([t[c], t[c]], axis=0)) for c in chains]
    for c in chains:
        e, h = where_at[c]
        inv_ref[e, h, :HALF, :] = jnp.where(left, x[c], 0.0).astype(BF16)
        inv_ref[e, h, HALF:, :] = jnp.where(left, -corner[c], x[c]).astype(BF16)


def pair_parts(part, half, plan, flat, q, k, rates, earlier=None):
    count, all_key_heads = q.shape[:2]
    key_heads = all_key_heads // PARTS
    heads = 2 * key_heads
    block = TOGETHER
    turns = count // block // 2
    first = half * turns
    head_block = pl.BlockSpec((block, key_heads, LEN, LEN), lambda i, t: (first + i, part, 0, 0))
    in_specs = [
        head_block,
        head_block,
        pl.BlockSpec((block,) + rates.shape[1:], lambda i, t: (first + i, 0, 0)),
    ]
    operands = [q, k, rates]
    aliases = {}
    if earlier is not None:
        in_specs += [pl.BlockSpec(memory_space=pl.ANY)] * 2
        aliases = {4: 0, 5: 1}
        operands += list(earlier)
    return pl.pallas_call(
        functools.partial(pair_kernel, part, first, plan),
        grid_spec=pltpu.PrefetchScalarGridSpec(
            num_scalar_prefetch=1,
            grid=(turns,),
            in_specs=in_specs,
            out_specs=[
                pl.BlockSpec((block, heads, LEN, LEN), lambda i, t: (first + i, 0, 0, 0)),
                pl.BlockSpec((block, heads, 2 * LEN, 2 * LEN), lambda i, t: (first + i, 0, 0, 0)),
            ],
        ),
        out_shape=[
            jax.ShapeDtypeStruct((count, heads, LEN, LEN), BF16),
            jax.ShapeDtypeStruct((count, heads, 2 * LEN, 2 * LEN), BF16),
        ],
        input_output_aliases=aliases,
        compiler_params=pltpu.CompilerParams(vmem_limit_bytes=VMEM_LIMIT),
        cost_estimate=pl.CostEstimate(flops=1000, bytes_accessed=1000, transcendentals=0),
    )(flat, *operands)


def turn_of(aways, each, turn):
    if len(aways) == 1:
        return aways[0], turn
    number = turn // each
    away = aways[-1]
    for at in reversed(range(len(aways) - 1)):
        away = jnp.where(number == at, aways[at], away)
    return away, turn - number * each


def state_kernel(part, aways, plan, shards_held, together, flat, gain_ref, *refs):
    per = 6
    inputs = [refs[per * e:per * (e + 1)] for e in range(together)]
    parents = refs[per * together:per * together + shards_held]
    states_in, mixed_out, arrivals, leaving = refs[-4:]
    mixed_hbm, *state_refs = refs[-5 - len(aways):-4]
    turn, turns = pl.program_id(0), pl.num_programs(0)
    each = plan.per_peer // together
    key_heads = inputs[0][0].shape[1]
    heads = 2 * key_heads
    all_heads = inputs[0][3].shape[1] // 2

    def fetch(i, slot):
        for e in range(together):
            away, at = turn_of(aways, each, i)
            shard = plan.shard(flat, away, at * together + e)
            for off in range(shards_held):
                @pl.when(shard == off)
                def _():
                    pltpu.make_async_copy(
                        parents[off].at[plan.row(flat, away, at * together + e)],
                        states_in.at[slot, e],
                        arrivals.at[slot, e],
                    ).start()

    def leave(i, slot, e):
        away, at = turn_of(aways, each, i)
        return pltpu.make_async_copy(
            mixed_out.at[slot, e],
            mixed_hbm.at[plan.local(flat, away, at * together + e), pl.ds(part * key_heads, key_heads)],
            leaving.at[slot, e],
        )

    slot = lax.rem(turn, 2)
    my_away, my_turn = turn_of(aways, each, turn)

    @pl.when(turn == 0)
    def _():
        fetch(0, 0)

    @pl.when(turn + 1 < turns)
    def _():
        fetch(turn + 1, lax.rem(turn + 1, 2))

    for e in range(together):
        pltpu.make_async_copy(parents[0].at[0], states_in.at[slot, e], arrivals.at[slot, e]).wait()

    @pl.when(turn >= 2)
    def _():
        for e in range(together):
            leave(turn - 2, slot, e).wait()

    row = iota((LEN, LEN), 0)
    col = iota((LEN, LEN), 1)
    lower_ones = (row >= col).astype(F32).astype(BF16)
    unit = (row == col).astype(F32).astype(BF16)
    gain = gain_ref[...].astype(F32)

    state, products, n_cols, g_cols, b_cols, eg_cols, steps = [], [], [], [], [], [], []
    for e in range(together):
        q_ref, k_ref, v_ref, rate_ref, inv_ref, am_ref = inputs[e]
        rates = live_rates(rate_ref[0], plan.tokens(flat, my_away, my_turn * together + e))
        cols = dot_nt(jnp.concatenate([lower_ones, unit], axis=0), rates)
        g_cols.append(cols[:LEN])
        b_cols.append(cols[LEN:])
        eg_cols.append(jnp.exp(cols[:LEN]))
        steps.append(load_steps(states_in.at[slot, pl.ds(e, 1)], heads))
        for m in range(key_heads):
            highs, lows = [], []
            for r in range(2):
                h = 2 * m + r
                whole = decode(states_in[slot, e, h * HALF:(h + 1) * HALF, :])
                high, low = split(whole)
                highs.append(high)
                lows.append(low)
                state.append(whole)
            rhs = jnp.concatenate(
                [jnp.concatenate(highs, axis=1), jnp.concatenate(lows, axis=1)], axis=0
            )
            lhs = jnp.concatenate([q_ref[0, m], k_ref[0, m]], axis=0)
            products.append(dot(jnp.concatenate([lhs, lhs], axis=1), rhs))
            keys = k_ref[0, m].astype(F32)
            n_cols.append(lax.rsqrt(jnp.sum(keys * keys, axis=1, keepdims=True) + EPS))

    every = [(e, h) for e in range(together) for h in range(heads)]

    def at_of(h):
        return part * heads + h

    def decay_at(e, h):
        return eg_cols[e][:, at_of(h):at_of(h) + 1]

    def product_at(e, h):
        lane = (h % 2) * LEN
        return products[e * key_heads + h // 2][:, lane:lane + LEN]

    right, first = [], []
    for e, h in every:
        v_ref, inv_ref = inputs[e][2], inputs[e][4]
        ks = product_at(e, h)[LEN:] * steps[e][h:h + 1, :]
        rate = b_cols[e][:, all_heads + at_of(h):all_heads + at_of(h) + 1]
        scale = decay_at(e, h) * n_cols[e * key_heads + h // 2]
        want = rate * (v_ref[0, h // 2, h % 2].astype(F32) - scale * ks)
        right.append(want)
        first.append(dot(inv_ref[0, h], want.astype(BF16)).astype(BF16))
    am_v = [
        dot(inputs[e][5][0, h], jnp.concatenate([first[c], first[c]], axis=0))
        for c, (e, h) in enumerate(every)
    ]
    delta = [
        dot(inputs[e][4][0, h], (right[c] - first[c].astype(F32) - am_v[c][:LEN]).astype(BF16))
        for c, (e, h) in enumerate(every)
    ]
    scaled = []
    for c, (e, h) in enumerate(every):
        g_c = g_cols[e][:, at_of(h):at_of(h) + 1]
        tail = jnp.exp(g_c[LEN - 1:LEN, :] - g_c) * n_cols[e * key_heads + h // 2]
        scaled.append(split(tail * (first[c].astype(F32) + delta[c])))
    finals = []
    for e in range(together):
        for m in range(key_heads):
            turned = jnp.transpose(inputs[e][1][0, m])
            c = e * heads + 2 * m
            rhs = jnp.concatenate(
                [jnp.concatenate([scaled[c][p], scaled[c + 1][p]], axis=1) for p in range(2)], axis=0
            )
            added = dot(jnp.concatenate([turned, turned], axis=1), rhs)
            for r in range(2):
                h = 2 * m + r
                keep = decay_at(e, h)[LEN - 1:LEN, :] * steps[e][h:h + 1, :]
                finals.append(keep * state[c + r] + added[:, r * LEN:(r + 1) * LEN])
    for c, (e, h) in enumerate(every):
        qs = product_at(e, h)[:LEN] * steps[e][h:h + 1, :]
        out = decay_at(e, h) * qs + am_v[c][LEN:]
        out = out + dot(inputs[e][5][0, h, LEN:, :LEN], delta[c].astype(BF16))
        mean_square = jnp.mean(out * out, axis=1, keepdims=True)
        live = iota((LEN, 1), 0) < plan.tokens(flat, my_away, my_turn * together + e)
        scale = jnp.where(live, lax.rsqrt(mean_square + EPS), 0.0)
        mixed_out[slot, e, h // 2, h % 2] = (out * scale * gain).astype(BF16)
    for e in range(together):
        leave(turn, slot, e).start()

    def store(ref, away):
        for e in range(together):
            mine = finals[e * heads:(e + 1) * heads]
            if away:
                store_packed(ref.at[pl.ds(e, 1)], mine)
            else:
                for h in range(heads):
                    ref[e, h] = mine[h]

    for number, away in enumerate(aways):
        if len(aways) == 1:
            store(state_refs[0], away)
        else:
            pl.when(turn // each == number)(functools.partial(store, state_refs[number], away))

    @pl.when(turn == turns - 1)
    def _():
        for e in range(together):
            leave(turn, slot, e).wait()

    @pl.when(jnp.logical_and(turn == turns - 1, turn >= 1))
    def _():
        for e in range(together):
            leave(turn - 1, 1 - slot, e).wait()


def recurrence(part, aways, plan, flat, q, k, v, rates, pairs, parents, gain, mixed, final_shape, final):
    count = plan.per_peer
    together = min(TOGETHER, count)
    turns = count // together
    key_heads = q.shape[1] // PARTS
    heads = 2 * key_heads
    rows = heads * HALF + CODE_ROWS
    in_specs = [pl.BlockSpec((1, LEN), lambda i, t: (0, 0))]
    operands = [gain]

    def one(shape, e, at):
        def index(i, t):
            away, turn = turn_of(aways, turns, i)
            return (plan.local(t, away, turn * together + e), at) + (0,) * (len(shape) - 2)

        return pl.BlockSpec(shape, index)

    for e in range(together):
        in_specs += [
            one((1, key_heads, LEN, LEN), e, part),
            one((1, key_heads, LEN, LEN), e, part),
            one((1, key_heads, 2, LEN, LEN), e, part),
            one((1,) + rates.shape[1:], e, 0),
            one((1, heads, LEN, LEN), e, 0),
            one((1, heads, 2 * LEN, 2 * LEN), e, 0),
        ]
        operands += [q, k, v, rates, *pairs]
    in_specs += [pl.BlockSpec(memory_space=pl.ANY)] * len(parents)
    operands += parents
    aliases = {}
    if mixed is not None:
        in_specs.append(pl.BlockSpec(memory_space=pl.ANY))
        aliases[1 + len(operands)] = 0
        operands.append(mixed)
    mixed_spec = pl.BlockSpec(memory_space=pl.ANY)
    mixed_shape = jax.ShapeDtypeStruct(v.shape, BF16)
    state_specs, state_shapes = [], []

    def turn_in(number, i):
        return i if len(aways) == 1 else jnp.clip(i - number * turns, 0, turns - 1)

    for number, away in enumerate(aways):
        if away:
            state_specs.append(
                pl.BlockSpec((together, rows, LEN), lambda i, t, n=number: (turn_in(n, i), 0, 0))
            )
            state_shapes.append(jax.ShapeDtypeStruct((count, rows, LEN), jnp.int32))
        else:
            if final is not None:
                in_specs.append(pl.BlockSpec(memory_space=pl.ANY))
                aliases[1 + len(operands)] = 1 + number
                operands.append(final)
            state_specs.append(
                pl.BlockSpec(
                    (together, heads, LEN, LEN),
                    lambda i, t, n=number: (plan.me(t) * turns + turn_in(n, i), part, 0, 0),
                )
            )
            state_shapes.append(jax.ShapeDtypeStruct(final_shape, F32))
    return pl.pallas_call(
        functools.partial(state_kernel, part, aways, plan, len(parents), together),
        grid_spec=pltpu.PrefetchScalarGridSpec(
            num_scalar_prefetch=1,
            grid=(turns * len(aways),),
            in_specs=in_specs,
            out_specs=[mixed_spec, *state_specs],
            scratch_shapes=[
                pltpu.VMEM((2, together, rows, LEN), jnp.int32),
                pltpu.VMEM((2, together, key_heads, 2, LEN, LEN), BF16),
                pltpu.SemaphoreType.DMA((2, together)),
                pltpu.SemaphoreType.DMA((2, together)),
            ],
        ),
        out_shape=[mixed_shape, *state_shapes],
        input_output_aliases=aliases,
        compiler_params=pltpu.CompilerParams(vmem_limit_bytes=VMEM_LIMIT),
        cost_estimate=pl.CostEstimate(flops=1000, bytes_accessed=1000, transcendentals=0),
    )(flat, *operands)


def unpack_kernel(turns, flat, *refs):
    *packed_refs, old_ref, out_ref = refs
    count, heads = out_ref.shape[:2]

    def unpack(ref):
        for e in range(count):
            steps = load_steps(ref.at[pl.ds(e, 1)], heads)
            for h in range(heads):
                out_ref[e, h] = decode(ref[e, h * HALF:(h + 1) * HALF, :]) * steps[h:h + 1, :]

    for number, ref in enumerate(packed_refs):
        if len(packed_refs) == 1:
            unpack(ref)
        else:
            pl.when(pl.program_id(0) // turns == number)(functools.partial(unpack, ref))


def unpack_states(part, aways, plan, flat, packed, final):
    count, rows = packed[0].shape[:2]
    heads = final.shape[1] // PARTS
    block = max(1, count // 2)
    turns = count // block

    def place(i, t):
        away, turn = turn_of(aways, turns, i)
        return (plan.peer(t, away) * turns + turn, part, 0, 0)

    def turn_in(number, i):
        return i if len(aways) == 1 else jnp.clip(i - number * turns, 0, turns - 1)

    return pl.pallas_call(
        functools.partial(unpack_kernel, turns),
        grid_spec=pltpu.PrefetchScalarGridSpec(
            num_scalar_prefetch=1,
            grid=(turns * len(aways),),
            in_specs=[
                pl.BlockSpec((block, rows, LEN), lambda i, t, n=number: (turn_in(n, i), 0, 0))
                for number in range(len(aways))
            ]
            + [pl.BlockSpec(memory_space=pl.ANY)],
            out_specs=pl.BlockSpec((block, heads, LEN, LEN), place),
        ),
        out_shape=jax.ShapeDtypeStruct(final.shape, F32),
        input_output_aliases={1 + len(aways): 0},
        compiler_params=pltpu.CompilerParams(vmem_limit_bytes=VMEM_LIMIT),
        cost_estimate=pl.CostEstimate(flops=1000, bytes_accessed=1000, transcendentals=0),
    )(flat, *packed, final)


def turn_kernel(mixed_ref, out_ref):
    key_heads, pair, length, size = mixed_ref.shape[1:]
    out_ref[0] = jnp.swapaxes(mixed_ref[0].reshape(key_heads * pair, length, size), 0, 1)


def turn_mixed(mixed):
    count, key_heads, pair, length, size = mixed.shape
    heads = key_heads * pair
    return pl.pallas_call(
        turn_kernel,
        grid=(count,),
        in_specs=[pl.BlockSpec((1, key_heads, pair, length, size), lambda i: (i, 0, 0, 0, 0))],
        out_specs=pl.BlockSpec((1, length, heads, size), lambda i: (i, 0, 0, 0)),
        out_shape=jax.ShapeDtypeStruct((count, length, heads, size), mixed.dtype),
        compiler_params=pltpu.CompilerParams(vmem_limit_bytes=VMEM_LIMIT),
        cost_estimate=pl.CostEstimate(flops=1000, bytes_accessed=1000, transcendentals=0),
    )(mixed)


def shards(
    queries,
    keys,
    values,
    log_decay,
    write_rate,
    norm_gain,
    parent_cache,
    order,
    parent_owner,
    parent_slot,
    token_count,
):
    seq_count = lax.axis_size("seq")
    me = lax.axis_index("seq")
    per_device, length, key_heads, key_dim = queries.shape
    per_peer = per_device // seq_count
    cache_rows = parent_cache.shape[0]
    heads = 2 * key_heads

    parents = parent_cache.reshape((cache_rows, heads, key_dim, key_dim))
    own = list(pack_parents(parents))

    def swap(tensor, off):
        return lax.ppermute(tensor, "seq", [(i, i ^ off) for i in range(seq_count)])

    def spread(held, off):
        while off:
            held = {**held, **{at ^ off: swap(held[at], off) for at in held}}
            off //= 2
        return held

    half_way = seq_count // 2
    far = swap(own[0], half_way)
    q = jnp.transpose(queries, (0, 2, 1, 3))
    k = jnp.transpose(keys, (0, 2, 1, 3))
    v = jnp.transpose(values, (0, 2, 3, 1, 4))

    def rows_of(tensor):
        return jnp.transpose(tensor, (0, 2, 3, 1)).reshape(per_device, heads, length).astype(F32)

    rates = jnp.concatenate([rows_of(log_decay), rows_of(write_rate)], axis=1)
    gain = norm_gain.reshape(1, -1)
    plan = Plan(order.shape[0], per_device, per_peer)
    flat = Plan.build(order, parent_owner, parent_slot, token_count, me)

    own[0], q = lax.optimization_barrier((own[0], q))
    q, k, v, rates, gain, flat = lax.optimization_barrier((q, k, v, rates, gain, flat))

    pairs = [pair_parts(0, 0, plan, flat, q, k, rates), None]
    pairs[0], far, own[1] = lax.optimization_barrier((pairs[0], far, own[1]))
    held_0 = spread({0: own[0], half_way: far}, half_way // 2)
    far_1 = swap(own[1], half_way)
    pairs[0] = pair_parts(0, 1, plan, flat, q, k, rates, pairs[0])
    rates, pairs[0] = lax.optimization_barrier((rates, pairs[0]))
    pairs[1] = pair_parts(1, 0, plan, flat, q, k, rates)
    pairs, held_0, far_1, own = lax.optimization_barrier((pairs, held_0, far_1, own))
    held_1 = spread({0: own[1], half_way: far_1}, half_way // 2)
    gathered = [[held[at] for at in range(seq_count)] for held in (held_0, held_1)]

    final_shape = (per_device, heads, key_dim, key_dim)
    crossing = list(reversed(range(half_way, seq_count)))
    near = list(reversed(range(1, half_way)))
    mixed, final = None, None
    arrived = {}

    def work(part, aways, mixed, final):
        mixed, *states = recurrence(
            part, aways, plan, flat, q, k, v, rates, pairs[part], gathered[part], gain, mixed, final_shape, final
        )
        for away, state in zip(aways, states):
            if away:
                arrived[part, away] = swap(state, away)
            else:
                final = state
        return mixed, final

    def gone(mixed, aways):
        for away in aways:
            mixed, arrived[0, away] = lax.optimization_barrier((mixed, arrived[0, away]))
        return mixed

    for away in crossing:
        mixed, final = work(0, [away], mixed, final)
    rates, mixed, pairs[1] = lax.optimization_barrier((rates, mixed, pairs[1]))
    pairs[1] = pair_parts(1, 1, plan, flat, q, k, rates, pairs[1])
    held_back = []
    for away in near:
        mixed, state = recurrence(
            0, [away], plan, flat, q, k, v, rates, pairs[0], gathered[0], gain, mixed, final_shape, final
        )
        held_back.append(state)
    mixed, pairs[1], gathered[1], held_back = lax.optimization_barrier((mixed, pairs[1], gathered[1], held_back))
    for away, state in zip(near, held_back):
        arrived[0, away] = swap(state, away)
    mixed = gone(mixed, crossing[:1])
    for away in crossing + near:
        mixed, final = work(1, [away], mixed, final)
    mixed = gone(mixed, crossing[1:])
    for part in range(PARTS):
        mixed, final = work(part, [0], mixed, final)
    away_first = crossing + near
    final = unpack_states(0, away_first, plan, flat, [arrived[0, away] for away in away_first], final)
    for away in crossing + near:
        final = unpack_states(1, [away], plan, flat, [arrived[1, away]], final)
    mixed_out = turn_mixed(mixed).reshape(values.shape)
    final_out = final.reshape((per_device, key_heads, 2, key_dim, key_dim))
    return (mixed_out, final_out)


def solution(mesh):
    placed = (
        P(("groups", "seq"), None, ("head", "sub"), None),
        P(("groups", "seq"), None, ("head", "sub"), None),
        P(("groups", "seq"), None, ("head", "sub"), None, None),
        P(("groups", "seq"), None, ("head", "sub"), None),
        P(("groups", "seq"), None, ("head", "sub"), None),
        P(),
        P(("groups", "seq"), ("head", "sub"), None, None, None),
        P("groups"),
        P("groups"),
        P("groups"),
        P("groups"),
    )
    return jax.shard_map(
        shards,
        mesh=mesh,
        in_specs=placed,
        out_specs=(
            P(("groups", "seq"), None, ("head", "sub"), None, None),
            P(("groups", "seq"), ("head", "sub"), None, None, None),
        ),
        check_vma=False,
    )
```
